32 devices in a mesh: temporal: 16 (over z, y, core), ulysses: 2 (over x).
Axes of the slice: x: 2, y: 2, z: 4, core: 2. Of those that a mesh axis runs over, the one named last changes fastest.
Arguments:
- queries: bfloat16 [16384, 1536], P(('temporal', 'ulysses')), may hold values from -12 to 12
- keys: bfloat16 [16384, 1536], P(('temporal', 'ulysses')), may hold values from -12 to 12
- values: bfloat16 [16384, 1536], P(('temporal', 'ulysses')), may hold values from -6 to 6
- tile_list: int32 [128, 5], P('temporal'), may hold values from 0 to 127, as said below
- counts: int32 [128], P('temporal'), may hold values from 1 to 5, as said below
- out_weight: bfloat16 [1536, 1536], replicated, may hold values from -0.15625 to 0.15625
Outputs:
- projected: bfloat16 [16384, 1536], P(('temporal', 'ulysses'))
The draws below stay inside these ranges and needn't reach their ends.
Inputs may be any that keep to these rules, and one draw needn't show every extreme that they name: `tile_list`: every id in row g lies within 3 of g and in the same video as g; the first entry is g itself; the first counts[g] entries are distinct; entries past counts[g] equal g. `counts`: some tile has 5 live entries.
All inputs are finite; a program needn't handle non-finite values.
Results may differ from the reference program's by a relative error of at most 0.0056.
Values may be sent and summed in bfloat16 or wider, within the bound.
No kernel may reach another device: no remote copies, remote signals or barrier semaphores. Data moves between devices by JAX's collectives and lax.ppermute only.
A program may use at most 64 MiB of HBM per device.

```python
import math
import jax
import jax.numpy as jnp
from jax import lax

D = 1536
HEADS = 12
HD = 128
TILE = 128
REACH = 3
MAXT = 5
TILES_T = 8
VID_GROUPS = 16
TOKENS = 16384
NT = 128


def query_key_pair(key):
    base_key = jax.random.fold_in(key, 7)
    first_key, second_key = jax.random.split(base_key, 2)
    query_out = jax.random.truncated_normal(first_key, -6.0, 6.0, (TOKENS, D), jnp.float32)
    key_out = jax.random.truncated_normal(second_key, -6.0, 6.0, (TOKENS, D), jnp.float32)
    return (query_out, key_out)


def draw_queries(key, part):
    return query_key_pair(key)[0].astype(jnp.bfloat16)


def draw_keys(key, part):
    return query_key_pair(key)[1].astype(jnp.bfloat16)


def tile_lists(key):
    base_key = jax.random.fold_in(key, 11)
    cap_key, count_key, order_key = jax.random.split(base_key, 3)
    tiles = jnp.arange(NT, dtype=jnp.int32)
    video_tiles = VID_GROUPS * TILES_T
    shard_of = tiles // TILES_T
    shard_cap = jax.random.randint(cap_key, (NT // TILES_T,), 2, MAXT + 1)
    wanted = jnp.minimum(jax.random.randint(count_key, (NT,), 1, MAXT + 1), shard_cap[shard_of])
    wanted = jnp.where(tiles == TILES_T, MAXT, wanted)
    offsets = jnp.arange(-REACH, REACH + 1, dtype=jnp.int32)
    window = 2 * REACH + 1
    target = tiles[:, None] + offsets[None, :]
    inside = (target >= 0) & (target < NT) & (target // video_tiles == (tiles // video_tiles)[:, None])
    inside_count = jnp.sum(inside.astype(jnp.int32), axis=1)
    wanted = jnp.minimum(wanted, inside_count)
    ranking = jax.random.randint(order_key, (NT, window), 0, 1 << 20) * window + jnp.arange(window, dtype=jnp.int32)[None, :]
    ranking = jnp.where(offsets[None, :] == 0, -1, ranking)
    ranking = jnp.where(inside, ranking, ranking + (1 << 28))
    order = jnp.argsort(ranking, axis=1, stable=True)[:, :MAXT]
    chosen = jnp.take_along_axis(target, order, axis=1)
    slots = jnp.arange(MAXT, dtype=jnp.int32)[None, :]
    listed = jnp.where(slots < wanted[:, None], chosen, tiles[:, None])
    return (listed.astype(jnp.int32), wanted.astype(jnp.int32))


def draw_tile_list(key, part):
    return tile_lists(key)[0]


def draw_counts(key, part):
    return tile_lists(key)[1]


def shard_levels(stream_key, extent, cuts, least, high):
    factor_of, own = 1.0, jax.random.fold_in(stream_key, 6)
    for position, blocks in cuts:
        steps = jnp.exp(jax.random.uniform(jax.random.fold_in(own, position), (blocks,), jnp.float32, least / len(cuts), high / len(cuts)))
        factor_of = factor_of * jnp.repeat(steps, extent[position] // blocks).reshape([-1 if axis == position else 1 for axis in range(len(extent))])
    return factor_of


def centred(key, extent, spread, most, cuts=(), kind=jnp.bfloat16):
    entries = spread * jax.random.normal(key, extent, jnp.float32)
    if cuts:
        entries = entries * shard_levels(key, extent, cuts, -0.22, 0.18)
    return jnp.clip(entries, -most, most).astype(kind)


def setup_inputs(seed: int = 0) -> dict:
    key_list = jax.random.split(jax.random.key(seed), 7)
    queries = draw_queries(jax.random.fold_in(key_list[6], 71), 0)
    keys = draw_keys(jax.random.fold_in(key_list[6], 71), 0)
    values = centred(key_list[2], (TOKENS, D), 1.0, 6.0, ((0, 32),))
    tile_list = draw_tile_list(jax.random.fold_in(key_list[6], 71), 0)
    counts = draw_counts(jax.random.fold_in(key_list[6], 71), 0)
    out_weight = centred(key_list[5], (D, D), D ** -0.5, 0.15625)
    return {"queries": queries, "keys": keys, "values": values, "tile_list": tile_list, "counts": counts, "out_weight": out_weight}


def reference(queries, keys, values, tile_list, counts, out_weight):
    query_all = queries.reshape(NT, TILE, HEADS, HD)
    key_all = keys.reshape(NT, TILE, HEADS, HD)
    value_all = values.reshape(NT, TILE, HEADS, HD)
    score_scale = 1.0 / math.sqrt(HD)
    slot_of = jnp.arange(MAXT * TILE, dtype=jnp.int32) // TILE

    def one_tile(tile_index):
        chosen = tile_list[tile_index]
        live = slot_of < counts[tile_index]
        query_tile = query_all[tile_index].astype(jnp.float32)
        key_rows = key_all[chosen].reshape(MAXT * TILE, HEADS, HD).astype(jnp.float32)
        value_rows = value_all[chosen].reshape(MAXT * TILE, HEADS, HD).astype(jnp.float32)
        scores = jnp.einsum('qhd,khd->hqk', query_tile, key_rows) * score_scale
        scores = jnp.where(live[None, None, :], scores, -jnp.inf)
        top = lax.optimization_barrier(jnp.max(scores, axis=-1, keepdims=True))
        weights = jnp.exp(scores - top)
        totals = lax.optimization_barrier(jnp.sum(weights, axis=-1, keepdims=True))
        rounded = lax.optimization_barrier(weights.astype(jnp.bfloat16)).astype(jnp.float32)
        mixed = jnp.einsum('hqk,khd->hqd', rounded, value_rows) / totals
        mixed = mixed.astype(jnp.bfloat16)
        return jnp.transpose(mixed, (1, 0, 2)).reshape(TILE, D)
    result = lax.map(one_tile, jnp.arange(NT, dtype=jnp.int32))
    attended = result.reshape(TOKENS, D)
    return jnp.dot(attended, out_weight, preferred_element_type=jnp.float32).astype(jnp.bfloat16)
```

```python
import functools
import math

import jax
import jax.numpy as jnp
from jax import lax
from jax.experimental import pallas as pl
from jax.experimental.pallas import tpu as pltpu
from jax.sharding import PartitionSpec as P

HD = 128
TILE = 128
REACH = 3


def split_heads(heads):
    if heads < 4:
        return [1] * heads
    third = heads // 3
    return [third, third, heads - 2 * third - 1, 1]


def pack_kernel(low, width, k_ref, v_ref, out_ref, sems):
    copies = [
        pltpu.make_async_copy(ref.at[:, pl.ds(low, width)], out_ref.at[i], sems.at[i])
        for i, ref in enumerate((k_ref, v_ref))
    ]
    for copy in copies:
        copy.start()
    for copy in copies:
        copy.wait()


def pack(keys, values, low, width):
    rows = keys.shape[0]
    return pl.pallas_call(
        functools.partial(pack_kernel, low, width),
        out_shape=jax.ShapeDtypeStruct((2, rows, width), keys.dtype),
        in_specs=[pl.BlockSpec(memory_space=pl.ANY)] * 2,
        out_specs=pl.BlockSpec(memory_space=pl.ANY),
        scratch_shapes=[pltpu.SemaphoreType.DMA((2,))],
        cost_estimate=pl.CostEstimate(flops=0, bytes_accessed=8 * rows * width, transcendentals=0),
    )(keys, values)


def attend_kernel(cfg, *refs):
    (low, width, pieces, has_acc) = cfg
    refs = list(refs)
    meta, tiles_ref, counts_ref, q_hbm, k_hbm, v_hbm = refs[:6]
    piece_refs = refs[6 : 6 + pieces]
    w_hbm = refs[6 + pieces]
    at = 7 + pieces
    acc_hbm = None
    if has_acc:
        acc_hbm = refs[at]
        at += 1
    out_hbm, q_buf, k_buf, v_buf, w_buf, att_buf, acc_buf, out_buf, sems, out_sems = refs[at:]
    rows = q_hbm.shape[0]
    tiles = rows // TILE
    slots = tiles_ref.shape[1]
    heads = width // HD
    cols = pl.ds(low, width)
    count = 0
    loads = []

    def load(src, dst):
        nonlocal count
        copy = pltpu.make_async_copy(src, dst, sems.at[count])
        count += 1
        copy.start()
        return copy

    own = pl.ds(pieces // 2 * rows, rows)
    loads.append(load(q_hbm.at[:, cols], q_buf))
    loads.append(load(k_hbm.at[:, cols], k_buf.at[own]))
    loads.append(load(v_hbm.at[:, cols], v_buf.at[own]))
    for i, ref in enumerate(piece_refs):
        place = pl.ds(pl.multiple_of(meta[2 + i] * rows, rows), rows)
        loads.append(load(ref.at[0], k_buf.at[place]))
        loads.append(load(ref.at[1], v_buf.at[place]))
    late = [load(w_hbm.at[pl.ds(low, width)], w_buf)]
    if has_acc:
        late.append(load(acc_hbm, acc_buf))
    for copy in loads:
        copy.wait()

    first, row0 = meta[0], meta[1]
    scale = math.log2(math.e) / math.sqrt(HD)

    def one_tile(tile):
        row = row0 + tile
        live = counts_ref[row]
        places = [
            pl.multiple_of((tiles_ref[row, j] - first) * TILE, TILE) for j in range(slots)
        ]
        here = pl.ds(pl.multiple_of(tile * TILE, TILE), TILE)
        for h in range(heads):
            part = slice(h * HD, (h + 1) * HD)
            q = q_buf[here, part]
            k = jnp.concatenate([k_buf[pl.ds(p, TILE), part] for p in places], axis=0)
            v = jnp.concatenate([v_buf[pl.ds(p, TILE), part] for p in places], axis=0)
            s = lax.dot_general(q, k, (((1,), (1,)), ((), ())), preferred_element_type=jnp.float32)
            slot = lax.broadcasted_iota(jnp.int32, s.shape, 1) // TILE
            s = jnp.where(slot < live, s, -jnp.inf)
            top = jnp.max(s, axis=1, keepdims=True)
            p = jnp.exp2((s - top) * scale)
            total = jnp.sum(p, axis=1, keepdims=True)
            mixed = jnp.dot(p.astype(jnp.bfloat16), v, preferred_element_type=jnp.float32)
            att_buf[here, part] = (mixed / total).astype(jnp.bfloat16)

    if heads == 1:
        for tile in range(tiles):
            one_tile(tile)
    else:
        pl.loop(0, tiles)(one_tile)

    for copy in late:
        copy.wait()
    stores = []
    for tile in range(tiles):
        here = pl.ds(tile * TILE, TILE)
        part = jnp.dot(att_buf[here], w_buf[...], preferred_element_type=jnp.float32)
        if has_acc:
            part = part + acc_buf[here]
        out_buf[here] = part.astype(out_buf.dtype)
        copy = pltpu.make_async_copy(out_buf.at[here], out_hbm.at[here], out_sems.at[tile])
        copy.start()
        stores.append(copy)
    for copy in stores:
        copy.wait()


def attend(meta, tile_list, counts, queries, keys, values, pieces, out_weight, acc, low, width, last):
    rows, model = queries.shape
    tiles = rows // TILE
    count = len(pieces)
    spans = (count + 1) * rows
    out_type = jnp.bfloat16 if last else jnp.float32
    smem = pl.BlockSpec(memory_space=pltpu.SMEM)
    anywhere = pl.BlockSpec(memory_space=pl.ANY)
    operands = [meta, tile_list, counts, queries, keys, values, *pieces, out_weight]
    if acc is not None:
        operands.append(acc)
    heads = width // HD
    pairs = heads * tiles * tile_list.shape[1]
    return pl.pallas_call(
        functools.partial(attend_kernel, (low, width, count, acc is not None)),
        out_shape=jax.ShapeDtypeStruct((rows, out_weight.shape[1]), out_type),
        in_specs=[smem] * 3 + [anywhere] * (len(operands) - 3),
        out_specs=anywhere,
        scratch_shapes=[
            pltpu.VMEM((rows, width), jnp.bfloat16),
            pltpu.VMEM((spans, width), jnp.bfloat16),
            pltpu.VMEM((spans, width), jnp.bfloat16),
            pltpu.VMEM((width, out_weight.shape[1]), jnp.bfloat16),
            pltpu.VMEM((rows, width), jnp.bfloat16),
            pltpu.VMEM((rows, out_weight.shape[1]), jnp.float32),
            pltpu.VMEM((rows, out_weight.shape[1]), out_type),
            pltpu.SemaphoreType.DMA((5 + 2 * count,)),
            pltpu.SemaphoreType.DMA((tiles,)),
        ],
        compiler_params=pltpu.CompilerParams(vmem_limit_bytes=40 * 1024 * 1024),
        cost_estimate=pl.CostEstimate(
            flops=8 * pairs * TILE * TILE * HD + 2 * rows * width * model,
            bytes_accessed=8 * rows * model + 2 * width * model + 4 * spans * width,
            transcendentals=pairs * TILE * TILE,
        ),
    )(*operands)


def on_device(queries, keys, values, tile_list, counts, out_weight):
    rows, model = queries.shape
    tiles = rows // TILE
    groups, members = lax.axis_size("temporal"), lax.axis_size("ulysses")
    group, member = lax.axis_index("temporal"), lax.axis_index("ulysses")
    total = groups * members
    both = ("temporal", "ulysses")
    hops = -(-REACH // tiles)
    relay = members == 2 and hops == 1
    if relay:
        place = [2 - 2 * member, 2 * member]
    else:
        place = [i for i in range(2 * hops + 1) if i != hops]
    first = ((group * members + member) - hops) * tiles
    meta = jnp.stack([jnp.asarray(x, jnp.int32) for x in (first, member * tiles, *place)])

    sizes = split_heads(model // HD)
    lows, received = [], []
    low = 0
    for size in sizes:
        width = size * HD
        block = pack(keys, values, low, width)
        if relay:
            partner = lax.ppermute(block, "ulysses", [(0, 1), (1, 0)])
            onward = [(2 * g, 2 * g + 2) for g in range(groups - 1)]
            onward += [(2 * g + 3, 2 * g + 1) for g in range(groups - 1)]
            beyond = lax.ppermute(partner, both, onward)
            received.append([partner, beyond])
        else:
            received.append(
                [
                    lax.ppermute(block, both, [(i, i - o) for i in range(total) if 0 <= i - o < total])
                    for o in range(-hops, hops + 1)
                    if o
                ]
            )
        lows.append((low, width))
        low += width
    acc = None
    for i, ((low, width), pieces) in enumerate(zip(lows, received)):
        acc = attend(
            meta, tile_list, counts, queries, keys, values, pieces, out_weight, acc, low, width, i == len(lows) - 1
        )
    return acc


def solution(mesh):
    return jax.shard_map(
        on_device,
        mesh=mesh,
        in_specs=(
            P(("temporal", "ulysses"), None),
            P(("temporal", "ulysses"), None),
            P(("temporal", "ulysses"), None),
            P("temporal", None),
            P("temporal"),
            P(),
        ),
        out_specs=P(("temporal", "ulysses"), None),
        check_vma=False,
    )
```

```python
import functools
import math

import jax
import jax.numpy as jnp
from jax import lax
from jax.experimental import pallas as pl
from jax.experimental.pallas import tpu as pltpu
from jax.sharding import PartitionSpec as P

HD = 128
TILE = 128
REACH = 3


def split_heads(heads):
    sizes = []
    left = heads
    while left > 4:
        sizes.append(min(3, left - 4) if sizes else 2)
        left -= sizes[-1]
    while left:
        sizes.append(max(1, left // 2))
        left -= sizes[-1]
    return sizes


def pack_kernel(groups, k_ref, v_ref, *refs):
    outs = refs[: len(groups)]
    k_buf, v_buf, t_buf, sems, out_sems = refs[len(groups) :]
    rows = k_ref.shape[0]
    base = groups[0][0]
    loads, stores = [], []
    for i, (low, width) in enumerate(groups):
        cols, here = pl.ds(low, width), pl.ds(low - base, width)
        loads.append(
            [
                pltpu.make_async_copy(k_ref.at[:, cols], k_buf.at[:, here], sems.at[i, 0]),
                pltpu.make_async_copy(v_ref.at[:, cols], v_buf.at[:, here], sems.at[i, 1]),
            ]
        )
        for copy in loads[-1]:
            copy.start()
    for i, (low, width) in enumerate(groups):
        here = pl.ds(low - base, width)
        loads[i][0].wait()
        for tile in range(rows // TILE):
            span = slice(tile * TILE, (tile + 1) * TILE)
            for at in range(low - base, low - base + width, HD):
                part = slice(at, at + HD)
                t_buf[span, part] = k_buf[span, part].T
        stores.append(pltpu.make_async_copy(t_buf.at[:, here], outs[i].at[0], out_sems.at[i, 0]))
        stores[-1].start()
        loads[i][1].wait()
        stores.append(pltpu.make_async_copy(v_buf.at[:, here], outs[i].at[1], out_sems.at[i, 1]))
        stores[-1].start()
    for copy in stores:
        copy.wait()


def pack(keys, values, groups):
    rows = keys.shape[0]
    span = sum(width for _, width in groups)
    anywhere = pl.BlockSpec(memory_space=pl.ANY)
    return pl.pallas_call(
        functools.partial(pack_kernel, groups),
        out_shape=[jax.ShapeDtypeStruct((2, rows, width), keys.dtype) for _, width in groups],
        in_specs=[anywhere] * 2,
        out_specs=[anywhere] * len(groups),
        scratch_shapes=[pltpu.VMEM((rows, span), keys.dtype)] * 3
        + [pltpu.SemaphoreType.DMA((len(groups), 2))] * 2,
        compiler_params=pltpu.CompilerParams(vmem_limit_bytes=24 * 1024 * 1024),
        cost_estimate=pl.CostEstimate(flops=0, bytes_accessed=8 * rows * span, transcendentals=0),
    )(keys, values)


def attend_kernel(cfg, *refs):
    (low, width, pieces, has_acc) = cfg
    meta, tiles_ref, counts_ref, q_hbm, own_hbm = refs[:5]
    piece_refs = refs[5 : 5 + pieces]
    w_hbm = refs[5 + pieces]
    at = 6 + pieces
    acc_hbm = None
    if has_acc:
        acc_hbm = refs[at]
        at += 1
    out_hbm, q_buf, k_buf, v_buf, w_buf, att_buf, acc_buf, out_buf, sems, out_sems = refs[at:]
    rows = q_hbm.shape[0]
    tiles = rows // TILE
    slots = tiles_ref.shape[1]
    heads = width // HD
    count = 0

    def load(src, dst):
        nonlocal count
        copy = pltpu.make_async_copy(src, dst, sems.at[count])
        count += 1
        copy.start()
        return copy

    loads = [load(q_hbm.at[:, pl.ds(low, width)], q_buf)]
    own = pl.ds(pieces // 2 * rows, rows)
    loads.append(load(own_hbm.at[0], k_buf.at[own]))
    loads.append(load(own_hbm.at[1], v_buf.at[own]))
    for i, ref in enumerate(piece_refs):
        place = pl.ds(pl.multiple_of(meta[2 + i] * rows, rows), rows)
        loads.append(load(ref.at[0], k_buf.at[place]))
        loads.append(load(ref.at[1], v_buf.at[place]))
    late = [load(w_hbm.at[pl.ds(low, width)], w_buf)]
    if has_acc:
        late.append(load(acc_hbm, acc_buf))
    for copy in loads:
        copy.wait()

    first, row0 = meta[0], meta[1]
    scale = math.log2(math.e) / math.sqrt(HD)
    ones = jnp.ones((slots * TILE, HD), jnp.bfloat16)

    def one_tile(tile):
        row = row0 + tile
        live = counts_ref[row]
        places = [
            pl.multiple_of((tiles_ref[row, j] - first) * TILE, TILE) for j in range(slots)
        ]
        here = pl.ds(pl.multiple_of(tile * TILE, TILE), TILE)
        for h in range(heads):
            part = slice(h * HD, (h + 1) * HD)
            k = jnp.concatenate([k_buf[pl.ds(p, TILE), part] for p in places], axis=1)
            v = jnp.concatenate([v_buf[pl.ds(p, TILE), part] for p in places], axis=0)
            s = jnp.dot(q_buf[here, part], k, preferred_element_type=jnp.float32)
            s = jnp.concatenate(
                [
                    s[:, j * TILE : (j + 1) * TILE] + jnp.where(j < live, 0.0, -jnp.inf)
                    for j in range(slots)
                ],
                axis=1,
            )
            top = jnp.max(s, axis=1, keepdims=True)
            p = jnp.exp2((s - top) * scale).astype(jnp.bfloat16)
            both = jnp.dot(p, jnp.concatenate([v, ones], axis=1), preferred_element_type=jnp.float32)
            att_buf[here, part] = (both[:, :HD] / both[:, HD:]).astype(jnp.bfloat16)

    if heads == 1:
        for tile in range(tiles):
            one_tile(tile)
    else:
        pl.loop(0, tiles)(one_tile)

    for copy in late:
        copy.wait()
    stores = []
    for tile in range(tiles):
        here = pl.ds(tile * TILE, TILE)
        part = jnp.dot(att_buf[here], w_buf[...], preferred_element_type=jnp.float32)
        if has_acc:
            part = part + acc_buf[here]
        out_buf[here] = part.astype(out_buf.dtype)
        copy = pltpu.make_async_copy(out_buf.at[here], out_hbm.at[here], out_sems.at[tile])
        copy.start()
        stores.append(copy)
    for copy in stores:
        copy.wait()


def attend(meta, tile_list, counts, queries, own, pieces, out_weight, acc, low, width, last):
    rows, model = queries.shape
    tiles = rows // TILE
    count = len(pieces)
    spans = (count + 1) * rows
    out_type = jnp.bfloat16 if last else jnp.float32
    smem = pl.BlockSpec(memory_space=pltpu.SMEM)
    anywhere = pl.BlockSpec(memory_space=pl.ANY)
    operands = [meta, tile_list, counts, queries, own, *pieces, out_weight]
    if acc is not None:
        operands.append(acc)
    pairs = width // HD * tiles * tile_list.shape[1]
    return pl.pallas_call(
        functools.partial(attend_kernel, (low, width, count, acc is not None)),
        out_shape=jax.ShapeDtypeStruct((rows, out_weight.shape[1]), out_type),
        in_specs=[smem] * 3 + [anywhere] * (len(operands) - 3),
        out_specs=anywhere,
        scratch_shapes=[
            pltpu.VMEM((rows, width), jnp.bfloat16),
            pltpu.VMEM((spans, width), jnp.bfloat16),
            pltpu.VMEM((spans, width), jnp.bfloat16),
            pltpu.VMEM((width, out_weight.shape[1]), jnp.bfloat16),
            pltpu.VMEM((rows, width), jnp.bfloat16),
            pltpu.VMEM((rows, out_weight.shape[1]), jnp.float32),
            pltpu.VMEM((rows, out_weight.shape[1]), out_type),
            pltpu.SemaphoreType.DMA((5 + 2 * count,)),
            pltpu.SemaphoreType.DMA((tiles,)),
        ],
        compiler_params=pltpu.CompilerParams(vmem_limit_bytes=24 * 1024 * 1024),
        cost_estimate=pl.CostEstimate(
            flops=8 * pairs * TILE * TILE * HD + 2 * rows * width * model,
            bytes_accessed=8 * rows * model + 2 * width * model + 4 * spans * width,
            transcendentals=pairs * TILE * TILE,
        ),
    )(*operands)


def after(array, *others):
    return lax.optimization_barrier((array, *others))[0]


def on_device(queries, keys, values, tile_list, counts, out_weight):
    rows, model = queries.shape
    tiles = rows // TILE
    groups, members = lax.axis_size("temporal"), lax.axis_size("ulysses")
    group, member = lax.axis_index("temporal"), lax.axis_index("ulysses")
    total = groups * members
    both = ("temporal", "ulysses")
    hops = -(-REACH // tiles)
    relay = members == 2 and hops == 1
    if relay:
        place = [2 - 2 * member, 2 * member]
    else:
        place = [i for i in range(2 * hops + 1) if i != hops]
    first = ((group * members + member) - hops) * tiles
    meta = jnp.stack([jnp.asarray(x, jnp.int32) for x in (first, member * tiles, *place)])

    spans, low = [], 0
    for size in split_heads(model // HD):
        spans.append((low, size * HD))
        low += size * HD
    blocks = pack(keys, values, spans[:1])
    if len(spans) > 1:
        blocks = [*blocks, *pack(after(keys, *blocks), values, spans[1:])]

    onward = [(2 * g, 2 * g + 2) for g in range(groups - 1)]
    onward += [(2 * g + 3, 2 * g + 1) for g in range(groups - 1)]
    count = len(spans)
    near, far = [None] * count, [None] * count
    acc = None

    def exchange(i):
        block = blocks[i]
        if relay:
            if i >= 2:
                block = after(block, near[i - 2][0])
            near[i] = [lax.ppermute(block, "ulysses", [(0, 1), (1, 0)])]
        else:
            if i >= 2:
                block = after(block, *near[i - 2])
            near[i] = [
                lax.ppermute(block, both, [(j, j - o) for j in range(total) if 0 <= j - o < total])
                for o in range(-hops, hops + 1)
                if o
            ]

    def pass_on(i, gate):
        far[i] = []
        if relay:
            block = near[i][0] if gate is None else after(near[i][0], gate)
            far[i] = [lax.ppermute(block, both, onward)]

    def work(i, acc):
        low, width = spans[i]
        return attend(
            meta, tile_list, counts, queries, blocks[i], [*near[i], *far[i]], out_weight, acc, low, width, i == count - 1
        )

    gate = None
    for i in range(count):
        exchange(i)
    for i in range(count):
        pass_on(i, acc)
        if i >= 1:
            acc = work(i - 1, acc)
    return work(count - 1, acc)


def solution(mesh):
    return jax.shard_map(
        on_device,
        mesh=mesh,
        in_specs=(
            P(("temporal", "ulysses"), None),
            P(("temporal", "ulysses"), None),
            P(("temporal", "ulysses"), None),
            P("temporal", None),
            P("temporal"),
            P(),
        ),
        out_specs=P(("temporal", "ulysses"), None),
        check_vma=False,
    )
```

```python
import functools
import math

import jax
import jax.numpy as jnp
from jax import lax
from jax.experimental import pallas as pl
from jax.experimental.pallas import tpu as pltpu
from jax.sharding import PartitionSpec as P

HD = 128
TILE = 128
REACH = 3
HBM = pl.BlockSpec(memory_space=pltpu.HBM)
SMEM = pl.BlockSpec(memory_space=pltpu.SMEM)
VMEM_LIMIT = 32 * 1024 * 1024
VMEM_ALL = 63 * 1024 * 1024


def split_heads(heads):
    sizes = []
    left = heads
    while left:
        sizes.append(max(1, (left + 1) // 3))
        left -= sizes[-1]
    return sizes


def pack_kernel(groups, k_ref, v_ref, *refs):
    outs = refs[: len(groups)]
    k_buf, out_buf, sems = refs[len(groups) :]
    rows = k_ref.shape[0]
    jobs = []
    for out, (low, size) in zip(outs, groups):
        for h in range(size):
            at = len(jobs)
            cols = pl.ds((low + h) * HD, HD)
            jobs.append(
                (
                    pltpu.make_async_copy(k_ref.at[:, cols], k_buf.at[at], sems.at[at, 0]),
                    pltpu.make_async_copy(v_ref.at[:, cols], out_buf.at[at, 1], sems.at[at, 1]),
                    pltpu.make_async_copy(out_buf.at[at], out.at[h], sems.at[at, 2]),
                )
            )
    for load_k, load_v, _ in jobs:
        load_k.start()
        load_v.start()
    for at, (load_k, load_v, store) in enumerate(jobs):
        load_k.wait()
        for tile in range(rows // TILE):
            span = slice(tile * TILE, (tile + 1) * TILE)
            out_buf[at, 0, span] = k_buf[at, span].T
        load_v.wait()
        store.start()
    for _, _, store in jobs:
        store.wait()


def pack(keys, values, groups):
    rows = keys.shape[0]
    heads = sum(size for _, size in groups)
    return pl.pallas_call(
        functools.partial(pack_kernel, groups),
        out_shape=[jax.ShapeDtypeStruct((size, 2, rows, HD), keys.dtype) for _, size in groups],
        in_specs=[HBM] * 2,
        out_specs=[HBM] * len(groups),
        scratch_shapes=[
            pltpu.VMEM((heads, rows, HD), keys.dtype),
            pltpu.VMEM((heads, 2, rows, HD), keys.dtype),
            pltpu.SemaphoreType.DMA((heads, 3)),
        ],
        compiler_params=pltpu.CompilerParams(vmem_limit_bytes=VMEM_ALL),
        cost_estimate=pl.CostEstimate(flops=0, bytes_accessed=8 * rows * heads * HD, transcendentals=0),
    )(keys, values)


def attend_kernel(cfg, meta, tiles_ref, counts_ref, q_hbm, *refs):
    low, size, pieces, project, has_acc = cfg
    refs = list(refs)
    piece_refs = [refs.pop(0) for _ in range(pieces)]
    early_refs = [refs.pop(0) for _ in project]
    w_hbm = refs.pop(0) if project else None
    acc_hbm = refs.pop(0) if has_acc else None
    out_hbm = refs.pop(0)
    q_buf, kv_buf, att_buf, load_sems, out_sems = refs[:5]
    refs = refs[5:]
    rows = q_hbm.shape[0]
    tiles = rows // TILE
    slots = tiles_ref.shape[1]
    spans = pieces * rows
    loads = []
    for h in range(size):
        copies = [pltpu.make_async_copy(q_hbm.at[:, pl.ds((low + h) * HD, HD)], q_buf.at[h], load_sems.at[h, pieces])]
        for i, ref in enumerate(piece_refs):
            place = pl.ds(pl.multiple_of(meta[2 + i] * rows, rows), rows)
            copies.append(pltpu.make_async_copy(ref.at[h], kv_buf.at[h, :, place], load_sems.at[h, i]))
        for copy in copies:
            copy.start()
        loads.append(copies)
    late = []
    if project:
        w_buf, out_buf = refs[0], refs[1]
        late_sems = refs[2]
        first_head = project[0][0]
        late.append(
            pltpu.make_async_copy(
                w_hbm.at[pl.ds(first_head * HD, (low + size - first_head) * HD)], w_buf, late_sems.at[0]
            )
        )
        for i, ((early_low, early_size), ref) in enumerate(zip(project, early_refs)):
            if ref is not None:
                where = pl.ds((early_low - first_head) * HD, early_size * HD)
                late.append(pltpu.make_async_copy(ref, att_buf.at[:, where], late_sems.at[1 + i]))
        if has_acc:
            acc_buf = refs[3]
            late.append(pltpu.make_async_copy(acc_hbm, acc_buf, late_sems.at[1 + len(project)]))
        for copy in late:
            copy.start()
        lead = low - first_head
    else:
        lead = 0

    first, row0 = meta[0], meta[1]
    scale = math.log2(math.e) / math.sqrt(HD)
    zeros = jnp.zeros((TILE, HD), jnp.bfloat16)
    places, v_places, ones = [], [], []
    for tile in range(tiles):
        row = row0 + tile
        live = counts_ref[row]
        at = [pl.multiple_of((tiles_ref[row, j] - first) * TILE, TILE) for j in range(slots)]
        places.append(at)
        v_places.append([pl.multiple_of(jnp.where(j < live, at[j], spans), TILE) for j in range(slots)])
        ones.append([zeros + jnp.where(j < live, 1.0, 0.0).astype(jnp.bfloat16) for j in range(slots)])

    def scores(h, tile):
        k = jnp.concatenate([kv_buf[h, 0, pl.ds(p, TILE)] for p in places[tile]], axis=1)
        q = q_buf[h, tile * TILE : (tile + 1) * TILE]
        return jnp.dot(q, k, preferred_element_type=jnp.float32)

    def finish(h, tile, s):
        top = jnp.max(s, axis=1, keepdims=True)
        p = jnp.exp2((s - top) * scale).astype(jnp.bfloat16)
        v = jnp.concatenate(
            [
                jnp.concatenate([kv_buf[h, 1, pl.ds(at, TILE)], one], axis=1)
                for at, one in zip(v_places[tile], ones[tile])
            ],
            axis=0,
        )
        mixed = jnp.dot(p, v, preferred_element_type=jnp.float32)
        here = slice(tile * TILE, (tile + 1) * TILE)
        col = lead + h
        att_buf[here, col * HD : (col + 1) * HD] = (mixed[:, :HD] / mixed[:, HD:]).astype(jnp.bfloat16)

    def ready(h):
        for copy in loads[h]:
            copy.wait()
        kv_buf[h, 1, spans : spans + TILE] = zeros

    jobs = [(h, tile) for h in range(size) for tile in range(tiles)]
    ready(0)
    ahead = scores(*jobs[0])
    for i, (h, tile) in enumerate(jobs):
        now = ahead
        if i + 1 < len(jobs):
            if jobs[i + 1][0] != h:
                ready(h + 1)
            ahead = scores(*jobs[i + 1])
        finish(h, tile, now)

    if not project:
        store = pltpu.make_async_copy(att_buf, out_hbm, out_sems.at[0])
        store.start()
        store.wait()
        return
    for copy in late:
        copy.wait()
    stores = []
    for tile in range(tiles):
        here = pl.ds(tile * TILE, TILE)
        part = jnp.dot(att_buf[here], w_buf[...], preferred_element_type=jnp.float32)
        if has_acc:
            part = part + acc_buf[here]
        out_buf[here] = part.astype(out_buf.dtype)
        stores.append(pltpu.make_async_copy(out_buf.at[here], out_hbm.at[here], out_sems.at[tile]))
        stores[-1].start()
    for copy in stores:
        copy.wait()


def attend(meta, tile_list, counts, queries, pieces, span, early, out_weight, acc, out_type):
    rows, model = queries.shape
    low, size = span
    tiles = rows // TILE
    count = len(pieces)
    operands = [meta, tile_list, counts, queries, *pieces]
    bf16 = jnp.bfloat16
    project = ()
    if early is None:
        out_shape = jax.ShapeDtypeStruct((rows, size * HD), bf16)
        att_heads = size
    else:
        project = tuple(where for where, _ in early)
        operands += [result for _, result in early]
        att_heads = size + sum(extent for _, extent in project)
        operands.append(out_weight)
        if acc is not None:
            operands.append(acc)
        project = project or ((low, 0),)
        out_shape = jax.ShapeDtypeStruct((rows, out_weight.shape[1]), out_type)
    scratch = [
        pltpu.VMEM((size, rows, HD), bf16),
        pltpu.VMEM((size, 2, count * rows + TILE, HD), bf16),
        pltpu.VMEM((rows, att_heads * HD), bf16),
        pltpu.SemaphoreType.DMA((size, count + 1)),
        pltpu.SemaphoreType.DMA((tiles,)),
    ]
    if early is not None:
        scratch += [
            pltpu.VMEM((att_heads * HD, out_weight.shape[1]), bf16),
            pltpu.VMEM(out_shape.shape, out_type),
            pltpu.SemaphoreType.DMA((2 + len(project),)),
        ]
        if acc is not None:
            scratch.append(pltpu.VMEM(acc.shape, acc.dtype))
    pairs = size * tiles * tile_list.shape[1]
    return pl.pallas_call(
        functools.partial(attend_entry, (low, size, count, project, bool(early), acc is not None)),
        out_shape=out_shape,
        in_specs=[SMEM] * 3 + [HBM] * (len(operands) - 3),
        out_specs=HBM,
        scratch_shapes=scratch,
        compiler_params=pltpu.CompilerParams(vmem_limit_bytes=VMEM_LIMIT),
        cost_estimate=pl.CostEstimate(
            flops=8 * pairs * TILE * TILE * HD + (0 if early is None else 2 * rows * att_heads * HD * model),
            bytes_accessed=4 * rows * model + 4 * size * (count + 1) * rows * HD,
            transcendentals=pairs * TILE * TILE,
        ),
    )(*operands)


def attend_entry(cfg, *refs):
    low, size, count, project, has_early, has_acc = cfg
    refs = list(refs)
    if project and not has_early:
        refs.insert(4 + count, None)
    attend_kernel((low, size, count, project, has_acc), *refs)


def after(array, *others):
    return lax.optimization_barrier((array, *others))[0]


def on_device(queries, keys, values, tile_list, counts, out_weight):
    rows, model = queries.shape
    tiles = rows // TILE
    groups, members = lax.axis_size("temporal"), lax.axis_size("ulysses")
    group, member = lax.axis_index("temporal"), lax.axis_index("ulysses")
    total = groups * members
    both = ("temporal", "ulysses")
    hops = -(-REACH // tiles)
    relay = members == 2 and hops == 1
    if relay:
        place = [1, 2 - 2 * member, 2 * member]
    else:
        place = [hops] + [i for i in range(2 * hops + 1) if i != hops]
    first = ((group * members + member) - hops) * tiles
    meta = jnp.stack([jnp.asarray(x, jnp.int32) for x in (first, member * tiles, *place)])

    spans, low = [], 0
    for size in split_heads(model // HD):
        spans.append((low, size))
        low += size
    count = len(spans)
    blocks = pack(keys, values, spans[:1])
    if count > 1:
        blocks = [*blocks, *pack(after(keys, *blocks), values, spans[1:])]

    onward = [(2 * g, 2 * g + 2) for g in range(groups - 1)]
    onward += [(2 * g + 3, 2 * g + 1) for g in range(groups - 1)]
    near = []
    for block in blocks:
        if relay:
            near.append([lax.ppermute(block, "ulysses", [(0, 1), (1, 0)])])
        else:
            near.append(
                [
                    lax.ppermute(block, both, [(j, j - o) for j in range(total) if 0 <= j - o < total])
                    for o in range(-hops, hops + 1)
                    if o
                ]
            )

    whole = max(0, count - 3)
    results, acc, last = [], None, None
    for i in range(count + 1):
        if i < count:
            pieces = [blocks[i], *near[i]]
            if relay:
                gate = near[i][0] if last is None else after(near[i][0], last)
                pieces.append(lax.ppermute(gate, both, onward))
        if i >= 1:
            j = i - 1
            early = None
            if j == whole:
                early = list(zip(spans[:j], results))
            elif j > whole:
                early = []
            out_type = jnp.bfloat16 if j == count - 1 else jnp.float32
            last = attend(meta, tile_list, counts, queries, held, spans[j], early, out_weight, acc, out_type)
            if early is None:
                results.append(last)
            else:
                acc = last
        held = pieces
    return acc


def solution(mesh):
    return jax.shard_map(
        on_device,
        mesh=mesh,
        in_specs=(
            P(("temporal", "ulysses"), None),
            P(("temporal", "ulysses"), None),
            P(("temporal", "ulysses"), None),
            P("temporal", None),
            P("temporal"),
            P(),
        ),
        out_specs=P(("temporal", "ulysses"), None),
        check_vma=False,
    )
```

```python
import functools
import math

import jax
import jax.numpy as jnp
from jax import lax
from jax.experimental import pallas as pl
from jax.experimental.pallas import tpu as pltpu
from jax.sharding import PartitionSpec as P

HD = 128
TILE = 128
REACH = 3
HBM = pl.BlockSpec(memory_space=pltpu.HBM)
SMEM = pl.BlockSpec(memory_space=pltpu.SMEM)
VMEM_LIMIT = 63 * 1024 * 1024


def split_heads(heads):
    sizes = []
    for share in (4 / 12, 3 / 12, 2 / 12, 2 / 12):
        size = min(max(1, round(share * heads)), heads - sum(sizes) - 1)
        if size > 0:
            sizes.append(size)
    return sizes + [heads - sum(sizes)]


def pack_kernel(groups, k_ref, v_ref, *refs):
    outs = refs[: len(groups)]
    k_buf, out_buf, sems = refs[len(groups) :]
    rows = k_ref.shape[0]
    jobs = []
    for out, (low, size) in zip(outs, groups):
        for h in range(size):
            at = len(jobs)
            cols = pl.ds((low + h) * HD, HD)
            jobs.append(
                (
                    pltpu.make_async_copy(k_ref.at[:, cols], k_buf.at[at], sems.at[at, 0]),
                    pltpu.make_async_copy(v_ref.at[:, cols], out_buf.at[at, 1], sems.at[at, 1]),
                    pltpu.make_async_copy(out_buf.at[at], out.at[h], sems.at[at, 2]),
                )
            )
    for load_k, load_v, _ in jobs:
        load_k.start()
        load_v.start()
    for at, (load_k, load_v, store) in enumerate(jobs):
        load_k.wait()
        for tile in range(rows // TILE):
            span = slice(tile * TILE, (tile + 1) * TILE)
            out_buf[at, 0, span] = k_buf[at, span].T
        load_v.wait()
        store.start()
    for _, _, store in jobs:
        store.wait()


def pack(keys, values, groups):
    rows = keys.shape[0]
    heads = sum(size for _, size in groups)
    return pl.pallas_call(
        functools.partial(pack_kernel, groups),
        out_shape=[jax.ShapeDtypeStruct((size, 2, rows, HD), keys.dtype) for _, size in groups],
        in_specs=[HBM] * 2,
        out_specs=[HBM] * len(groups),
        scratch_shapes=[
            pltpu.VMEM((heads, rows, HD), keys.dtype),
            pltpu.VMEM((heads, 2, rows, HD), keys.dtype),
            pltpu.SemaphoreType.DMA((heads, 3)),
        ],
        compiler_params=pltpu.CompilerParams(vmem_limit_bytes=VMEM_LIMIT),
        cost_estimate=pl.CostEstimate(flops=0, bytes_accessed=8 * rows * heads * HD, transcendentals=0),
    )(keys, values)


def attend_kernel(cfg, meta, tiles_ref, counts_ref, q_hbm, *refs):
    low, size, pieces, project, has_acc = cfg
    refs = list(refs)
    piece_refs = [refs.pop(0) for _ in range(pieces)]
    early_refs = [refs.pop(0) for _ in project]
    w_hbm = refs.pop(0) if project else None
    acc_hbm = refs.pop(0) if has_acc else None
    out_hbm = refs.pop(0)
    q_buf, kv_buf, att_buf, load_sems, out_sems = refs[:5]
    refs = refs[5:]
    rows = q_hbm.shape[0]
    tiles = rows // TILE
    slots = tiles_ref.shape[1]
    spans = pieces * rows
    loads = []
    for h in range(size):
        copies = [pltpu.make_async_copy(q_hbm.at[:, pl.ds((low + h) * HD, HD)], q_buf.at[h], load_sems.at[h, pieces])]
        for i, ref in enumerate(piece_refs):
            place = pl.ds(pl.multiple_of(meta[2 + i] * rows, rows), rows)
            copies.append(pltpu.make_async_copy(ref.at[h], kv_buf.at[h, :, place], load_sems.at[h, i]))
        for copy in copies:
            copy.start()
        loads.append(copies)
    late = []
    if project:
        w_buf, out_buf = refs[0], refs[1]
        late_sems = refs[2]
        first_head = project[0][0]
        late.append(
            pltpu.make_async_copy(
                w_hbm.at[pl.ds(first_head * HD, (low + size - first_head) * HD)], w_buf, late_sems.at[0]
            )
        )
        for i, ((early_low, early_size), ref) in enumerate(zip(project, early_refs)):
            if ref is not None:
                where = pl.ds((early_low - first_head) * HD, early_size * HD)
                late.append(pltpu.make_async_copy(ref, att_buf.at[:, where], late_sems.at[1 + i]))
        if has_acc:
            acc_buf = refs[3]
            late.append(pltpu.make_async_copy(acc_hbm, acc_buf, late_sems.at[1 + len(project)]))
        for copy in late:
            copy.start()
        lead = low - first_head
    else:
        lead = 0

    first, row0 = meta[0], meta[1]
    scale = math.log2(math.e) / math.sqrt(HD)
    zeros = jnp.zeros((TILE, HD), jnp.bfloat16)
    places, v_places, ones = [], [], []
    for tile in range(tiles):
        row = row0 + tile
        live = counts_ref[row]
        at = [pl.multiple_of((tiles_ref[row, j] - first) * TILE, TILE) for j in range(slots)]
        places.append(at)
        v_places.append([pl.multiple_of(jnp.where(j < live, at[j], spans), TILE) for j in range(slots)])
        ones.append([zeros + jnp.where(j < live, 1.0, 0.0).astype(jnp.bfloat16) for j in range(slots)])

    def scores(h, tile):
        k = jnp.concatenate([kv_buf[h, 0, pl.ds(p, TILE)] for p in places[tile]], axis=1)
        q = q_buf[h, tile * TILE : (tile + 1) * TILE]
        return jnp.dot(q, k, preferred_element_type=jnp.float32)

    def finish(h, tile, s):
        top = jnp.max(s, axis=1, keepdims=True)
        p = jnp.exp2((s - top) * scale).astype(jnp.bfloat16)
        v = jnp.concatenate(
            [
                jnp.concatenate([kv_buf[h, 1, pl.ds(at, TILE)], one], axis=1)
                for at, one in zip(v_places[tile], ones[tile])
            ],
            axis=0,
        )
        mixed = jnp.dot(p, v, preferred_element_type=jnp.float32)
        here = slice(tile * TILE, (tile + 1) * TILE)
        col = lead + h
        att_buf[here, col * HD : (col + 1) * HD] = (mixed[:, :HD] / mixed[:, HD:]).astype(jnp.bfloat16)

    def ready(h):
        for copy in loads[h]:
            copy.wait()
        kv_buf[h, 1, spans : spans + TILE] = zeros

    stores = []

    def project_tile(tile):
        here = slice(tile * TILE, (tile + 1) * TILE)
        part = jnp.dot(att_buf[here], w_buf[...], preferred_element_type=jnp.float32)
        if has_acc:
            part = part + acc_buf[here]
        out_buf[here] = part.astype(out_buf.dtype)
        rows_here = pl.ds(tile * TILE, TILE)
        stores.append(pltpu.make_async_copy(out_buf.at[rows_here], out_hbm.at[rows_here], out_sems.at[tile]))
        stores[-1].start()

    jobs = [(h, tile) for h in range(size) for tile in range(tiles)]
    ready(0)
    ahead = scores(*jobs[0])
    for i, (h, tile) in enumerate(jobs):
        now = ahead
        if i + 1 < len(jobs):
            if jobs[i + 1][0] != h:
                ready(h + 1)
            ahead = scores(*jobs[i + 1])
        finish(h, tile, now)
        if project and h == size - 1:
            if tile == 0:
                for copy in late:
                    copy.wait()
            project_tile(tile)

    if not project:
        stores.append(pltpu.make_async_copy(att_buf, out_hbm, out_sems.at[0]))
        stores[-1].start()
    for copy in stores:
        copy.wait()


def attend(meta, tile_list, counts, queries, pieces, span, early, out_weight, acc, out_type):
    rows, model = queries.shape
    low, size = span
    tiles = rows // TILE
    count = len(pieces)
    operands = [meta, tile_list, counts, queries, *pieces]
    bf16 = jnp.bfloat16
    project = ()
    if early is None:
        out_shape = jax.ShapeDtypeStruct((rows, size * HD), bf16)
        att_heads = size
    else:
        project = tuple(where for where, _ in early)
        operands += [result for _, result in early]
        att_heads = size + sum(extent for _, extent in project)
        operands.append(out_weight)
        if acc is not None:
            operands.append(acc)
        project = project or ((low, 0),)
        out_shape = jax.ShapeDtypeStruct((rows, out_weight.shape[1]), out_type)
    scratch = [
        pltpu.VMEM((size, rows, HD), bf16),
        pltpu.VMEM((size, 2, count * rows + TILE, HD), bf16),
        pltpu.VMEM((rows, att_heads * HD), bf16),
        pltpu.SemaphoreType.DMA((size, count + 1)),
        pltpu.SemaphoreType.DMA((tiles,)),
    ]
    if early is not None:
        scratch += [
            pltpu.VMEM((att_heads * HD, out_weight.shape[1]), bf16),
            pltpu.VMEM(out_shape.shape, out_type),
            pltpu.SemaphoreType.DMA((2 + len(project),)),
        ]
        if acc is not None:
            scratch.append(pltpu.VMEM(acc.shape, acc.dtype))
    return pl.pallas_call(
        functools.partial(attend_entry, (low, size, count, project, bool(early), acc is not None)),
        out_shape=out_shape,
        in_specs=[SMEM] * 3 + [HBM] * (len(operands) - 3),
        out_specs=HBM,
        scratch_shapes=scratch,
        compiler_params=pltpu.CompilerParams(vmem_limit_bytes=VMEM_LIMIT),
        cost_estimate=pl.CostEstimate(flops=0, bytes_accessed=0, transcendentals=0),
    )(*operands)


def attend_entry(cfg, *refs):
    low, size, count, project, has_early, has_acc = cfg
    refs = list(refs)
    if project and not has_early:
        refs.insert(4 + count, None)
    attend_kernel((low, size, count, project, has_acc), *refs)


def after(array, *others):
    return lax.optimization_barrier((array, *others))[0]


def on_device(queries, keys, values, tile_list, counts, out_weight):
    rows, model = queries.shape
    tiles = rows // TILE
    groups, members = lax.axis_size("temporal"), lax.axis_size("ulysses")
    group, member = lax.axis_index("temporal"), lax.axis_index("ulysses")
    total = groups * members
    both = ("temporal", "ulysses")
    hops = -(-REACH // tiles)
    relay = members == 2 and hops == 1
    if relay:
        place = [1, 2 - 2 * member, 2 * member]
    else:
        place = [hops] + [i for i in range(2 * hops + 1) if i != hops]
    first = ((group * members + member) - hops) * tiles
    meta = jnp.stack([jnp.asarray(x, jnp.int32) for x in (first, member * tiles, *place)])

    spans, low = [], 0
    for size in split_heads(model // HD):
        spans.append((low, size))
        low += size
    count = len(spans)
    blocks = pack(keys, values, spans[:1])
    if count > 1:
        blocks = [*blocks, *pack(after(keys, *blocks), values, spans[1:])]

    onward = [(2 * g, 2 * g + 2) for g in range(groups - 1)]
    onward += [(2 * g + 3, 2 * g + 1) for g in range(groups - 1)]
    near = []
    for block in blocks:
        if relay:
            with jax.named_scope(f"partner_{len(near)}"):
                near.append([lax.ppermute(block, "ulysses", [(0, 1), (1, 0)])])
        else:
            near.append(
                [
                    lax.ppermute(block, both, [(j, j - o) for j in range(total) if 0 <= j - o < total])
                    for o in range(-hops, hops + 1)
                    if o
                ]
            )

    whole = max(0, count - 3)
    results, acc, last = [], None, None
    for i in range(count + 1):
        if i < count:
            pieces = [blocks[i], *near[i]]
            if relay:
                gate = near[i][0] if last is None else after(near[i][0], last)
                with jax.named_scope(f"onward_{i}"):
                    pieces.append(lax.ppermute(gate, both, onward))
        if i >= 1:
            j = i - 1
            early = None
            if j == whole:
                early = list(zip(spans[:j], results))
            elif j > whole:
                early = []
            out_type = jnp.bfloat16 if j == count - 1 else jnp.float32
            with jax.named_scope(f"attend_{j}"):
                last = attend(meta, tile_list, counts, queries, held, spans[j], early, out_weight, acc, out_type)
            if early is None:
                results.append(last)
            else:
                acc = last
        held = pieces
    return acc


def solution(mesh):
    return jax.shard_map(
        on_device,
        mesh=mesh,
        in_specs=(
            P(("temporal", "ulysses"), None),
            P(("temporal", "ulysses"), None),
            P(("temporal", "ulysses"), None),
            P("temporal", None),
            P("temporal"),
            P(),
        ),
        out_specs=P(("temporal", "ulysses"), None),
        check_vma=False,
    )
```

```python
import functools
import math

import jax
import jax.numpy as jnp
from jax import lax
from jax.experimental import pallas as pl
from jax.experimental.pallas import tpu as pltpu
from jax.sharding import PartitionSpec as P

HD = 128
TILE = 128
REACH = 3
STRIP = 256
HBM = pl.BlockSpec(memory_space=pltpu.HBM)
SMEM = pl.BlockSpec(memory_space=pltpu.SMEM)
VMEM_LIMIT = 63 * 1024 * 1024


def split_heads(heads):
    sizes = []
    for share in (4 / 12, 3 / 12, 2 / 12, 2 / 12):
        size = min(max(1, round(share * heads)), heads - sum(sizes) - 1)
        if size > 0:
            sizes.append(size)
    return sizes + [heads - sum(sizes)]


def pack_kernel(groups, k_ref, v_ref, *refs):
    outs = refs[: len(groups)]
    k_buf, out_buf, sems = refs[len(groups) :]
    rows = k_ref.shape[0]
    jobs = []
    for out, (low, size) in zip(outs, groups):
        for h in range(size):
            at = len(jobs)
            cols = pl.ds((low + h) * HD, HD)
            jobs.append(
                (
                    pltpu.make_async_copy(k_ref.at[:, cols], k_buf.at[at], sems.at[at, 0]),
                    pltpu.make_async_copy(v_ref.at[:, cols], out_buf.at[at, 1], sems.at[at, 1]),
                    pltpu.make_async_copy(out_buf.at[at], out.at[h], sems.at[at, 2]),
                )
            )
    for load_k, load_v, _ in jobs:
        load_k.start()
        load_v.start()
    for at, (load_k, load_v, store) in enumerate(jobs):
        load_k.wait()
        for tile in range(rows // TILE):
            span = slice(tile * TILE, (tile + 1) * TILE)
            out_buf[at, 0, span] = k_buf[at, span].T
        load_v.wait()
        store.start()
    for _, _, store in jobs:
        store.wait()


def pack(keys, values, groups):
    rows = keys.shape[0]
    heads = sum(size for _, size in groups)
    return pl.pallas_call(
        functools.partial(pack_kernel, groups),
        out_shape=[jax.ShapeDtypeStruct((size, 2, rows, HD), keys.dtype) for _, size in groups],
        in_specs=[HBM] * 2,
        out_specs=[HBM] * len(groups),
        scratch_shapes=[
            pltpu.VMEM((heads, rows, HD), keys.dtype),
            pltpu.VMEM((heads, 2, rows, HD), keys.dtype),
            pltpu.SemaphoreType.DMA((heads, 3)),
        ],
        compiler_params=pltpu.CompilerParams(vmem_limit_bytes=VMEM_LIMIT),
        cost_estimate=pl.CostEstimate(flops=0, bytes_accessed=8 * rows * heads * HD, transcendentals=0),
    )(keys, values)


def attend_kernel(cfg, meta, tiles_ref, counts_ref, q_hbm, *refs):
    low, size, pieces, project = cfg
    refs = list(refs)
    piece_refs = [refs.pop(0) for _ in range(pieces)]
    early_refs = [refs.pop(0) for _ in project or ()]
    w_hbm = None if project is None else refs.pop(0)
    out_hbm, q_buf, kv_buf, att_buf, load_sems, out_sems = refs[:6]
    rows = q_hbm.shape[0]
    tiles = rows // TILE
    slots = tiles_ref.shape[1]
    spans = pieces * rows
    loads = []
    for h in range(size):
        copies = [pltpu.make_async_copy(q_hbm.at[:, pl.ds((low + h) * HD, HD)], q_buf.at[h], load_sems.at[h, pieces])]
        for i, ref in enumerate(piece_refs):
            place = pl.ds(pl.multiple_of(meta[2 + i] * rows, rows), rows)
            copies.append(pltpu.make_async_copy(ref.at[h], kv_buf.at[h, :, place], load_sems.at[h, i]))
        for copy in copies:
            copy.start()
        loads.append(copies)
    late, lead = [], 0
    if project is not None:
        w_buf, out_buf, late_sems = refs[6:]
        lead = low
        late.append(pltpu.make_async_copy(w_hbm, w_buf, late_sems.at[0]))
        for i, ((early_low, early_size), ref) in enumerate(zip(project, early_refs)):
            where = pl.ds(early_low * HD, early_size * HD)
            late.append(pltpu.make_async_copy(ref, att_buf.at[:, where], late_sems.at[1 + i]))
        for copy in late:
            copy.start()

    first, row0 = meta[0], meta[1]
    scale = math.log2(math.e) / math.sqrt(HD)
    zeros = jnp.zeros((TILE, HD), jnp.bfloat16)
    places, v_places, ones = [], [], []
    for tile in range(tiles):
        row = row0 + tile
        live = counts_ref[row]
        at = [pl.multiple_of((tiles_ref[row, j] - first) * TILE, TILE) for j in range(slots)]
        places.append(at)
        v_places.append([pl.multiple_of(jnp.where(j < live, at[j], spans), TILE) for j in range(slots)])
        ones.append([zeros + jnp.where(j < live, 1.0, 0.0).astype(jnp.bfloat16) for j in range(slots)])

    def scores(h, tile):
        k = jnp.concatenate([kv_buf[h, 0, pl.ds(p, TILE)] for p in places[tile]], axis=1)
        q = q_buf[h, tile * TILE : (tile + 1) * TILE]
        return jnp.dot(q, k, preferred_element_type=jnp.float32)

    def finish(h, tile, s):
        top = jnp.max(s, axis=1, keepdims=True)
        p = jnp.exp2((s - top) * scale).astype(jnp.bfloat16)
        v = jnp.concatenate(
            [
                jnp.concatenate([kv_buf[h, 1, pl.ds(at, TILE)], one], axis=1)
                for at, one in zip(v_places[tile], ones[tile])
            ],
            axis=0,
        )
        mixed = jnp.dot(p, v, preferred_element_type=jnp.float32)
        here = slice(tile * TILE, (tile + 1) * TILE)
        col = lead + h
        att_buf[here, col * HD : (col + 1) * HD] = (mixed[:, :HD] / mixed[:, HD:]).astype(jnp.bfloat16)

    def ready(h):
        for copy in loads[h]:
            copy.wait()
        kv_buf[h, 1, spans : spans + TILE] = zeros

    jobs = [(h, tile) for h in range(size) for tile in range(tiles)]
    ready(0)
    ahead = scores(*jobs[0])
    for i, (h, tile) in enumerate(jobs):
        now = ahead
        if i + 1 < len(jobs):
            if jobs[i + 1][0] != h:
                ready(h + 1)
            ahead = scores(*jobs[i + 1])
        finish(h, tile, now)

    stores = []
    if project is None:
        stores.append(pltpu.make_async_copy(att_buf, out_hbm, out_sems.at[0]))
        stores[-1].start()
    else:
        for copy in late:
            copy.wait()
        for i, at in enumerate(range(0, out_buf.shape[1], STRIP)):
            here = slice(at, min(at + STRIP, out_buf.shape[1]))
            out_buf[:, here] = jnp.dot(att_buf[...], w_buf[:, here], preferred_element_type=jnp.float32).astype(
                out_buf.dtype
            )
            cols = pl.ds(at, here.stop - at)
            stores.append(pltpu.make_async_copy(out_buf.at[:, cols], out_hbm.at[:, cols], out_sems.at[i]))
            stores[-1].start()
    for copy in stores:
        copy.wait()


def attend(meta, tile_list, counts, queries, pieces, span, early, out_weight):
    rows, model = queries.shape
    low, size = span
    tiles = rows // TILE
    count = len(pieces)
    width = out_weight.shape[1]
    operands = [meta, tile_list, counts, queries, *pieces]
    bf16 = jnp.bfloat16
    project = None if early is None else tuple(where for where, _ in early)
    if early is None:
        out_shape = jax.ShapeDtypeStruct((rows, size * HD), bf16)
        heads = size
    else:
        operands += [result for _, result in early]
        operands.append(out_weight)
        out_shape = jax.ShapeDtypeStruct((rows, width), bf16)
        heads = model // HD
    scratch = [
        pltpu.VMEM((size, rows, HD), bf16),
        pltpu.VMEM((size, 2, count * rows + TILE, HD), bf16),
        pltpu.VMEM((rows, heads * HD), bf16),
        pltpu.SemaphoreType.DMA((size, count + 1)),
        pltpu.SemaphoreType.DMA((-(-width // STRIP),)),
    ]
    if early is not None:
        scratch += [
            pltpu.VMEM((model, width), bf16),
            pltpu.VMEM((rows, width), bf16),
            pltpu.SemaphoreType.DMA((1 + len(project),)),
        ]
    return pl.pallas_call(
        functools.partial(attend_kernel, (low, size, count, project)),
        out_shape=out_shape,
        in_specs=[SMEM] * 3 + [HBM] * (len(operands) - 3),
        out_specs=HBM,
        scratch_shapes=scratch,
        compiler_params=pltpu.CompilerParams(vmem_limit_bytes=VMEM_LIMIT),
        cost_estimate=pl.CostEstimate(flops=0, bytes_accessed=0, transcendentals=0),
    )(*operands)


def after(array, *others):
    return lax.optimization_barrier((array, *others))[0]


def on_device(queries, keys, values, tile_list, counts, out_weight):
    rows, model = queries.shape
    tiles = rows // TILE
    groups, members = lax.axis_size("temporal"), lax.axis_size("ulysses")
    group, member = lax.axis_index("temporal"), lax.axis_index("ulysses")
    total = groups * members
    both = ("temporal", "ulysses")
    hops = -(-REACH // tiles)
    relay = members == 2 and hops == 1
    if relay:
        place = [1, 2 - 2 * member, 2 * member]
    else:
        place = [hops] + [i for i in range(2 * hops + 1) if i != hops]
    first = ((group * members + member) - hops) * tiles
    meta = jnp.stack([jnp.asarray(x, jnp.int32) for x in (first, member * tiles, *place)])

    spans, low = [], 0
    for size in split_heads(model // HD):
        spans.append((low, size))
        low += size
    count = len(spans)
    blocks = pack(keys, values, spans[:1])
    if count > 1:
        blocks = [*blocks, *pack(after(keys, *blocks), values, spans[1:])]

    onward = [(2 * g, 2 * g + 2) for g in range(groups - 1)]
    onward += [(2 * g + 3, 2 * g + 1) for g in range(groups - 1)]
    near = []
    for block in blocks:
        if relay:
            with jax.named_scope(f"partner_{len(near)}"):
                near.append([lax.ppermute(block, "ulysses", [(0, 1), (1, 0)])])
        else:
            near.append(
                [
                    lax.ppermute(block, both, [(j, j - o) for j in range(total) if 0 <= j - o < total])
                    for o in range(-hops, hops + 1)
                    if o
                ]
            )

    results = []
    for i in range(count + 1):
        if i < count:
            pieces = [blocks[i], *near[i]]
            if relay:
                gate = near[i][0] if i < 2 else after(near[i][0], results[i - 2])
                with jax.named_scope(f"onward_{i}"):
                    pieces.append(lax.ppermute(gate, both, onward))
        if i >= 1:
            j = i - 1
            early = list(zip(spans[:j], results)) if i == count else None
            with jax.named_scope(f"attend_{j}"):
                results.append(attend(meta, tile_list, counts, queries, held, spans[j], early, out_weight))
        held = pieces
    return results[-1]


def solution(mesh):
    return jax.shard_map(
        on_device,
        mesh=mesh,
        in_specs=(
            P(("temporal", "ulysses"), None),
            P(("temporal", "ulysses"), None),
            P(("temporal", "ulysses"), None),
            P("temporal", None),
            P("temporal"),
            P(),
        ),
        out_specs=P(("temporal", "ulysses"), None),
        check_vma=False,
    )
```

```python
import functools
import math

import jax
import jax.numpy as jnp
from jax import lax
from jax.experimental import pallas as pl
from jax.experimental.pallas import tpu as pltpu
from jax.sharding import PartitionSpec as P

HD = 128
TILE = 128
REACH = 3
STRIP = 256
HBM = pl.BlockSpec(memory_space=pltpu.HBM)
SMEM = pl.BlockSpec(memory_space=pltpu.SMEM)
VMEM_LIMIT = 24 * 1024 * 1024
VMEM_WHOLE = 63 * 1024 * 1024


def split_heads(heads):
    sizes = []
    for share in (4 / 12, 3 / 12, 2 / 12, 2 / 12):
        size = min(max(1, round(share * heads)), heads - sum(sizes) - 1)
        if size > 0:
            sizes.append(size)
    return sizes + [heads - sum(sizes)]


def pack_kernel(groups, q_groups, q_ref, k_ref, v_ref, *refs):
    outs, q_outs = refs[: len(groups)], refs[len(groups) : len(groups) + len(q_groups)]
    k_buf, out_buf, q_buf, sems, q_sems = refs[len(groups) + len(q_groups) :]
    rows = k_ref.shape[0]
    jobs, q_jobs = [], []
    for out, (low, size) in zip(outs, groups):
        for h in range(size):
            at = len(jobs)
            cols = pl.ds((low + h) * HD, HD)
            jobs.append(
                (
                    pltpu.make_async_copy(k_ref.at[:, cols], k_buf.at[at], sems.at[at, 0]),
                    pltpu.make_async_copy(v_ref.at[:, cols], out_buf.at[at, 1], sems.at[at, 1]),
                    pltpu.make_async_copy(out_buf.at[at], out.at[h], sems.at[at, 2]),
                )
            )
    for out, (low, size) in zip(q_outs, q_groups):
        for h in range(size):
            at = len(q_jobs)
            cols = pl.ds((low + h) * HD, HD)
            q_jobs.append(
                (
                    pltpu.make_async_copy(q_ref.at[:, cols], q_buf.at[at], q_sems.at[at, 0]),
                    pltpu.make_async_copy(q_buf.at[at], out.at[h], q_sems.at[at, 1]),
                )
            )
    for load_k, load_v, _ in jobs:
        load_k.start()
        load_v.start()
    for load, _ in q_jobs:
        load.start()
    for at, (load_k, load_v, store) in enumerate(jobs):
        load_k.wait()
        for tile in range(rows // TILE):
            span = slice(tile * TILE, (tile + 1) * TILE)
            out_buf[at, 0, span] = k_buf[at, span].T
        load_v.wait()
        store.start()
    for load, store in q_jobs:
        load.wait()
        store.start()
    for _, _, store in jobs:
        store.wait()
    for _, store in q_jobs:
        store.wait()


def pack(queries, keys, values, groups, q_groups, limit):
    rows = keys.shape[0]
    heads = sum(size for _, size in groups)
    q_heads = sum(size for _, size in q_groups)
    shapes = [(size, 2, rows, HD) for _, size in groups] + [(size, rows, HD) for _, size in q_groups]
    return pl.pallas_call(
        functools.partial(pack_kernel, groups, q_groups),
        out_shape=[jax.ShapeDtypeStruct(shape, keys.dtype) for shape in shapes],
        in_specs=[HBM] * 3,
        out_specs=[HBM] * len(shapes),
        scratch_shapes=[
            pltpu.VMEM((heads, rows, HD), keys.dtype),
            pltpu.VMEM((heads, 2, rows, HD), keys.dtype),
            pltpu.VMEM((max(q_heads, 1), rows, HD), keys.dtype),
            pltpu.SemaphoreType.DMA((heads, 3)),
            pltpu.SemaphoreType.DMA((max(q_heads, 1), 2)),
        ],
        compiler_params=pltpu.CompilerParams(vmem_limit_bytes=limit),
        cost_estimate=pl.CostEstimate(flops=0, bytes_accessed=8 * rows * heads * HD, transcendentals=0),
    )(queries, keys, values)


def attend_kernel(cfg, meta, tiles_ref, counts_ref, q_hbm, *refs):
    low, size, pieces, project = cfg
    refs = list(refs)
    piece_refs = [refs.pop(0) for _ in range(pieces)]
    early_refs = [refs.pop(0) for _ in project or ()]
    w_hbm = None if project is None else refs.pop(0)
    out_hbm, q_buf, kv_buf, att_buf, load_sems, out_sems = refs[:6]
    rows = q_hbm.shape[1]
    tiles = rows // TILE
    slots = tiles_ref.shape[1]
    spans = pieces * rows
    loads = []
    for h in range(size):
        copies = [pltpu.make_async_copy(q_hbm.at[h], q_buf.at[h], load_sems.at[h, pieces])]
        for i, ref in enumerate(piece_refs):
            place = pl.ds(pl.multiple_of(meta[2 + i] * rows, rows), rows)
            copies.append(pltpu.make_async_copy(ref.at[h], kv_buf.at[h, :, place], load_sems.at[h, i]))
        for copy in copies:
            copy.start()
        loads.append(copies)
    late, lead = [], 0
    if project is not None:
        w_buf, out_buf, late_sems = refs[6:]
        lead = low
        late.append(pltpu.make_async_copy(w_hbm, w_buf, late_sems.at[0]))
        for i, ((early_low, early_size), ref) in enumerate(zip(project, early_refs)):
            where = pl.ds(early_low * HD, early_size * HD)
            late.append(pltpu.make_async_copy(ref, att_buf.at[:, where], late_sems.at[1 + i]))
        for copy in late:
            copy.start()

    first, row0 = meta[0], meta[1]
    scale = math.log2(math.e) / math.sqrt(HD)
    zeros = jnp.zeros((TILE, HD), jnp.bfloat16)
    places, v_places, ones = [], [], []
    for tile in range(tiles):
        row = row0 + tile
        live = counts_ref[row]
        at = [pl.multiple_of((tiles_ref[row, j] - first) * TILE, TILE) for j in range(slots)]
        places.append(at)
        v_places.append([pl.multiple_of(jnp.where(j < live, at[j], spans), TILE) for j in range(slots)])
        ones.append([zeros + jnp.where(j < live, 1.0, 0.0).astype(jnp.bfloat16) for j in range(slots)])

    def scores(h, tile):
        k = jnp.concatenate([kv_buf[h, 0, pl.ds(p, TILE)] for p in places[tile]], axis=1)
        q = q_buf[h, tile * TILE : (tile + 1) * TILE]
        return jnp.dot(q, k, preferred_element_type=jnp.float32)

    def finish(h, tile, s):
        top = jnp.max(s, axis=1, keepdims=True)
        p = jnp.exp2((s - top) * scale).astype(jnp.bfloat16)
        v = jnp.concatenate(
            [
                jnp.concatenate([kv_buf[h, 1, pl.ds(at, TILE)], one], axis=1)
                for at, one in zip(v_places[tile], ones[tile])
            ],
            axis=0,
        )
        mixed = jnp.dot(p, v, preferred_element_type=jnp.float32)
        here = slice(tile * TILE, (tile + 1) * TILE)
        col = lead + h
        att_buf[here, col * HD : (col + 1) * HD] = (mixed[:, :HD] / mixed[:, HD:]).astype(jnp.bfloat16)

    def ready(h):
        for copy in loads[h]:
            copy.wait()
        kv_buf[h, 1, spans : spans + TILE] = zeros

    jobs = [(h, tile) for h in range(size) for tile in range(tiles)]
    ready(0)
    ahead = scores(*jobs[0])
    for i, (h, tile) in enumerate(jobs):
        now = ahead
        if i + 1 < len(jobs):
            if jobs[i + 1][0] != h:
                ready(h + 1)
            ahead = scores(*jobs[i + 1])
        finish(h, tile, now)

    stores = []
    if project is None:
        stores.append(pltpu.make_async_copy(att_buf, out_hbm, out_sems.at[0]))
        stores[-1].start()
    else:
        for copy in late:
            copy.wait()
        for i, at in enumerate(range(0, out_buf.shape[1], STRIP)):
            here = slice(at, min(at + STRIP, out_buf.shape[1]))
            out_buf[:, here] = jnp.dot(att_buf[...], w_buf[:, here], preferred_element_type=jnp.float32).astype(
                out_buf.dtype
            )
            cols = pl.ds(at, here.stop - at)
            stores.append(pltpu.make_async_copy(out_buf.at[:, cols], out_hbm.at[:, cols], out_sems.at[i]))
            stores[-1].start()
    for copy in stores:
        copy.wait()


def attend(meta, tile_list, counts, queries, pieces, span, early, out_weight):
    rows, model = queries.shape[1], out_weight.shape[0]
    low, size = span
    tiles = rows // TILE
    count = len(pieces)
    width = out_weight.shape[1]
    operands = [meta, tile_list, counts, queries, *pieces]
    bf16 = jnp.bfloat16
    project = None if early is None else tuple(where for where, _ in early)
    if early is None:
        out_shape = jax.ShapeDtypeStruct((rows, size * HD), bf16)
        heads = size
    else:
        operands += [result for _, result in early]
        operands.append(out_weight)
        out_shape = jax.ShapeDtypeStruct((rows, width), bf16)
        heads = model // HD
    scratch = [
        pltpu.VMEM((size, rows, HD), bf16),
        pltpu.VMEM((size, 2, count * rows + TILE, HD), bf16),
        pltpu.VMEM((rows, heads * HD), bf16),
        pltpu.SemaphoreType.DMA((size, count + 1)),
        pltpu.SemaphoreType.DMA((-(-width // STRIP),)),
    ]
    if early is not None:
        scratch += [
            pltpu.VMEM((model, width), bf16),
            pltpu.VMEM((rows, width), bf16),
            pltpu.SemaphoreType.DMA((1 + len(project),)),
        ]
    return pl.pallas_call(
        functools.partial(attend_kernel, (low, size, count, project)),
        out_shape=out_shape,
        in_specs=[SMEM] * 3 + [HBM] * (len(operands) - 3),
        out_specs=HBM,
        scratch_shapes=scratch,
        compiler_params=pltpu.CompilerParams(vmem_limit_bytes=VMEM_LIMIT),
        cost_estimate=pl.CostEstimate(flops=0, bytes_accessed=0, transcendentals=0),
    )(*operands)


def after(array, *others):
    return lax.optimization_barrier((array, *others))[0]


def on_device(queries, keys, values, tile_list, counts, out_weight):
    rows, model = queries.shape
    tiles = rows // TILE
    groups, members = lax.axis_size("temporal"), lax.axis_size("ulysses")
    group, member = lax.axis_index("temporal"), lax.axis_index("ulysses")
    total = groups * members
    both = ("temporal", "ulysses")
    hops = -(-REACH // tiles)
    relay = members == 2 and hops == 1
    if relay:
        place = [1, 2 - 2 * member, 2 * member]
    else:
        place = [hops] + [i for i in range(2 * hops + 1) if i != hops]
    first = ((group * members + member) - hops) * tiles
    meta = jnp.stack([jnp.asarray(x, jnp.int32) for x in (first, member * tiles, *place)])

    spans, low = [], 0
    for size in split_heads(model // HD):
        spans.append((low, size))
        low += size
    count = len(spans)
    sent = pack(queries, keys, values, spans[:1], [], VMEM_WHOLE)
    laid = pack(queries, after(keys, *sent), values, spans, spans, VMEM_LIMIT)
    blocks, heads_of = laid[:count], laid[count:]
    sent = [*sent, *blocks[1:]]

    onward = [(2 * g, 2 * g + 2) for g in range(groups - 1)]
    onward += [(2 * g + 3, 2 * g + 1) for g in range(groups - 1)]
    near = []
    for block in sent:
        if relay:
            with jax.named_scope(f"partner_{len(near)}"):
                near.append([lax.ppermute(block, "ulysses", [(0, 1), (1, 0)])])
        else:
            near.append(
                [
                    lax.ppermute(block, both, [(j, j - o) for j in range(total) if 0 <= j - o < total])
                    for o in range(-hops, hops + 1)
                    if o
                ]
            )

    results = []
    for i in range(count + 1):
        if i < count:
            pieces = [blocks[i], *near[i]]
            if relay:
                gate = near[i][0] if i < 2 else after(near[i][0], results[i - 2])
                with jax.named_scope(f"onward_{i}"):
                    pieces.append(lax.ppermute(gate, both, onward))
        if i >= 1:
            j = i - 1
            early = list(zip(spans[:j], results)) if i == count else None
            with jax.named_scope(f"attend_{j}"):
                results.append(attend(meta, tile_list, counts, heads_of[j], held, spans[j], early, out_weight))
        held = pieces
    return results[-1]


def solution(mesh):
    return jax.shard_map(
        on_device,
        mesh=mesh,
        in_specs=(
            P(("temporal", "ulysses"), None),
            P(("temporal", "ulysses"), None),
            P(("temporal", "ulysses"), None),
            P("temporal", None),
            P("temporal"),
            P(),
        ),
        out_specs=P(("temporal", "ulysses"), None),
        check_vma=False,
    )
```

```python
import functools
import math

import jax
import jax.numpy as jnp
from jax import lax
from jax.experimental import pallas as pl
from jax.experimental.pallas import tpu as pltpu
from jax.sharding import PartitionSpec as P

HD = 128
TILE = 128
REACH = 3
STRIP = 256
SHARES = (3 / 12, 3 / 12, 3 / 12, 2 / 12)
HBM = pl.BlockSpec(memory_space=pltpu.HBM)
SMEM = pl.BlockSpec(memory_space=pltpu.SMEM)
VMEM_LIMIT = 16 * 1024 * 1024
VMEM_WHOLE = 63 * 1024 * 1024


def split_heads(heads):
    sizes = []
    for share in SHARES:
        size = min(max(1, round(share * heads)), heads - sum(sizes) - 1)
        if size > 0:
            sizes.append(size)
    return sizes + [heads - sum(sizes)]


def pack_kernel(groups, q_groups, q_ref, k_ref, v_ref, *refs):
    outs, q_outs = refs[: len(groups)], refs[len(groups) : len(groups) + len(q_groups)]
    k_buf, out_buf, q_buf, sems, q_sems = refs[len(groups) + len(q_groups) :]
    rows = k_ref.shape[0]
    jobs, q_jobs = [], []
    for out, (low, size) in zip(outs, groups):
        for h in range(size):
            at = len(jobs)
            cols = pl.ds((low + h) * HD, HD)
            jobs.append(
                (
                    pltpu.make_async_copy(k_ref.at[:, cols], k_buf.at[at], sems.at[at, 0]),
                    pltpu.make_async_copy(v_ref.at[:, cols], out_buf.at[at, 1], sems.at[at, 1]),
                    pltpu.make_async_copy(out_buf.at[at], out.at[h], sems.at[at, 2]),
                )
            )
    for out, (low, size) in zip(q_outs, q_groups):
        for h in range(size):
            at = len(q_jobs)
            cols = pl.ds((low + h) * HD, HD)
            q_jobs.append(
                (
                    pltpu.make_async_copy(q_ref.at[:, cols], q_buf.at[at], q_sems.at[at, 0]),
                    pltpu.make_async_copy(q_buf.at[at], out.at[h], q_sems.at[at, 1]),
                )
            )
    for load_k, load_v, _ in jobs:
        load_k.start()
        load_v.start()
    for load, _ in q_jobs:
        load.start()
    for at, (load_k, load_v, store) in enumerate(jobs):
        load_k.wait()
        for tile in range(rows // TILE):
            span = slice(tile * TILE, (tile + 1) * TILE)
            out_buf[at, 0, span] = k_buf[at, span].T
        load_v.wait()
        store.start()
    for load, store in q_jobs:
        load.wait()
        store.start()
    for _, _, store in jobs:
        store.wait()
    for _, store in q_jobs:
        store.wait()


def pack(queries, keys, values, groups, q_groups, limit):
    rows = keys.shape[0]
    heads = sum(size for _, size in groups)
    q_heads = sum(size for _, size in q_groups)
    shapes = [(size, 2, rows, HD) for _, size in groups] + [(size, rows, HD) for _, size in q_groups]
    return pl.pallas_call(
        functools.partial(pack_kernel, groups, q_groups),
        out_shape=[jax.ShapeDtypeStruct(shape, keys.dtype) for shape in shapes],
        in_specs=[HBM] * 3,
        out_specs=[HBM] * len(shapes),
        scratch_shapes=[
            pltpu.VMEM((heads, rows, HD), keys.dtype),
            pltpu.VMEM((heads, 2, rows, HD), keys.dtype),
            pltpu.VMEM((max(q_heads, 1), rows, HD), keys.dtype),
            pltpu.SemaphoreType.DMA((heads, 3)),
            pltpu.SemaphoreType.DMA((max(q_heads, 1), 2)),
        ],
        compiler_params=pltpu.CompilerParams(vmem_limit_bytes=limit),
        cost_estimate=pl.CostEstimate(flops=0, bytes_accessed=8 * rows * heads * HD, transcendentals=0),
    )(queries, keys, values)


def attend_kernel(cfg, meta, tiles_ref, counts_ref, q_hbm, *refs):
    low, size, pieces, project, has_acc = cfg
    refs = list(refs)
    piece_refs = [refs.pop(0) for _ in range(pieces)]
    early_refs = [refs.pop(0) for _ in project or ()]
    w_hbm = None if project is None else refs.pop(0)
    acc_hbm = refs.pop(0) if has_acc else None
    out_hbm, q_buf, kv_buf, att_buf, load_sems, out_sems = refs[:6]
    rows = q_hbm.shape[1]
    tiles = rows // TILE
    slots = tiles_ref.shape[1]
    spans = pieces * rows
    loads = []
    for h in range(size):
        copies = [pltpu.make_async_copy(q_hbm.at[h], q_buf.at[h], load_sems.at[h, pieces])]
        for i, ref in enumerate(piece_refs):
            place = pl.ds(pl.multiple_of(meta[2 + i] * rows, rows), rows)
            copies.append(pltpu.make_async_copy(ref.at[h], kv_buf.at[h, :, place], load_sems.at[h, i]))
        for copy in copies:
            copy.start()
        loads.append(copies)
    late, lead = [], 0
    if project is not None:
        w_buf, out_buf, late_sems = refs[6:9]
        base = project[0][0] if project else low
        lead = low - base
        late.append(pltpu.make_async_copy(w_hbm.at[pl.ds(base * HD, (lead + size) * HD)], w_buf, late_sems.at[0]))
        for i, ((early_low, early_size), ref) in enumerate(zip(project, early_refs)):
            where = pl.ds((early_low - base) * HD, early_size * HD)
            late.append(pltpu.make_async_copy(ref, att_buf.at[:, where], late_sems.at[1 + i]))
        if has_acc:
            acc_buf = refs[9]
            late.append(pltpu.make_async_copy(acc_hbm, acc_buf, late_sems.at[1 + len(project)]))
        for copy in late:
            copy.start()

    first, row0 = meta[0], meta[1]
    scale = math.log2(math.e) / math.sqrt(HD)
    zeros = jnp.zeros((TILE, HD), jnp.bfloat16)
    places, v_places, ones = [], [], []
    for tile in range(tiles):
        row = row0 + tile
        live = counts_ref[row]
        at = [pl.multiple_of((tiles_ref[row, j] - first) * TILE, TILE) for j in range(slots)]
        places.append(at)
        v_places.append([pl.multiple_of(jnp.where(j < live, at[j], spans), TILE) for j in range(slots)])
        ones.append([zeros + jnp.where(j < live, 1.0, 0.0).astype(jnp.bfloat16) for j in range(slots)])

    def scores(h, tile):
        k = jnp.concatenate([kv_buf[h, 0, pl.ds(p, TILE)] for p in places[tile]], axis=1)
        q = q_buf[h, tile * TILE : (tile + 1) * TILE]
        return jnp.dot(q, k, preferred_element_type=jnp.float32)

    def finish(h, tile, s):
        top = jnp.max(s, axis=1, keepdims=True)
        p = jnp.exp2((s - top) * scale).astype(jnp.bfloat16)
        v = jnp.concatenate(
            [
                jnp.concatenate([kv_buf[h, 1, pl.ds(at, TILE)], one], axis=1)
                for at, one in zip(v_places[tile], ones[tile])
            ],
            axis=0,
        )
        mixed = jnp.dot(p, v, preferred_element_type=jnp.float32)
        here = slice(tile * TILE, (tile + 1) * TILE)
        col = lead + h
        att_buf[here, col * HD : (col + 1) * HD] = (mixed[:, :HD] / mixed[:, HD:]).astype(jnp.bfloat16)

    def ready(h):
        for copy in loads[h]:
            copy.wait()
        kv_buf[h, 1, spans : spans + TILE] = zeros

    jobs = [(h, tile) for h in range(size) for tile in range(tiles)]
    ready(0)
    ahead = scores(*jobs[0])
    for i, (h, tile) in enumerate(jobs):
        now = ahead
        if i + 1 < len(jobs):
            if jobs[i + 1][0] != h:
                ready(h + 1)
            ahead = scores(*jobs[i + 1])
        finish(h, tile, now)

    stores = []
    if project is None:
        stores.append(pltpu.make_async_copy(att_buf, out_hbm, out_sems.at[0]))
        stores[-1].start()
    else:
        for copy in late:
            copy.wait()
        for i, at in enumerate(range(0, out_buf.shape[1], STRIP)):
            here = slice(at, min(at + STRIP, out_buf.shape[1]))
            part = jnp.dot(att_buf[...], w_buf[:, here], preferred_element_type=jnp.float32)
            if has_acc:
                part = part + acc_buf[:, here]
            out_buf[:, here] = part.astype(out_buf.dtype)
            cols = pl.ds(at, here.stop - at)
            stores.append(pltpu.make_async_copy(out_buf.at[:, cols], out_hbm.at[:, cols], out_sems.at[i]))
            stores[-1].start()
    for copy in stores:
        copy.wait()


def attend(meta, tile_list, counts, queries, pieces, span, early, out_weight, acc):
    rows, model = queries.shape[1], out_weight.shape[0]
    low, size = span
    tiles = rows // TILE
    count = len(pieces)
    width = out_weight.shape[1]
    operands = [meta, tile_list, counts, queries, *pieces]
    bf16 = jnp.bfloat16
    project = None if early is None else tuple(where for where, _ in early)
    if early is None:
        out_shape = jax.ShapeDtypeStruct((rows, size * HD), bf16)
        heads = size
    else:
        operands += [result for _, result in early]
        operands.append(out_weight)
        if acc is not None:
            operands.append(acc)
        out_shape = jax.ShapeDtypeStruct((rows, width), bf16)
        heads = size + sum(extent for _, extent in project)
    scratch = [
        pltpu.VMEM((size, rows, HD), bf16),
        pltpu.VMEM((size, 2, count * rows + TILE, HD), bf16),
        pltpu.VMEM((rows, heads * HD), bf16),
        pltpu.SemaphoreType.DMA((size, count + 1)),
        pltpu.SemaphoreType.DMA((-(-width // STRIP),)),
    ]
    if early is not None:
        scratch += [
            pltpu.VMEM((heads * HD, width), bf16),
            pltpu.VMEM((rows, width), bf16),
            pltpu.SemaphoreType.DMA((2 + len(project),)),
        ]
        if acc is not None:
            scratch.append(pltpu.VMEM(acc.shape, acc.dtype))
    return pl.pallas_call(
        functools.partial(attend_kernel, (low, size, count, project, acc is not None)),
        out_shape=out_shape,
        in_specs=[SMEM] * 3 + [HBM] * (len(operands) - 3),
        out_specs=HBM,
        scratch_shapes=scratch,
        compiler_params=pltpu.CompilerParams(vmem_limit_bytes=VMEM_LIMIT),
        cost_estimate=pl.CostEstimate(flops=0, bytes_accessed=0, transcendentals=0),
    )(*operands)


def project_kernel(spans, *refs):
    parts = refs[: len(spans)]
    w_hbm, out_hbm, att_buf, w_buf, out_buf, sems, out_sems = refs[len(spans) :]
    loads = [pltpu.make_async_copy(w_hbm.at[pl.ds(0, w_buf.shape[0])], w_buf, sems.at[len(spans)])]
    for i, ((low, size), ref) in enumerate(zip(spans, parts)):
        loads.append(pltpu.make_async_copy(ref, att_buf.at[:, pl.ds(low * HD, size * HD)], sems.at[i]))
    for copy in loads:
        copy.start()
    for copy in loads:
        copy.wait()
    stores = []
    for i, at in enumerate(range(0, out_buf.shape[1], STRIP)):
        here = slice(at, min(at + STRIP, out_buf.shape[1]))
        out_buf[:, here] = jnp.dot(att_buf[...], w_buf[:, here], preferred_element_type=jnp.float32)
        cols = pl.ds(at, here.stop - at)
        stores.append(pltpu.make_async_copy(out_buf.at[:, cols], out_hbm.at[:, cols], out_sems.at[i]))
        stores[-1].start()
    for copy in stores:
        copy.wait()


def project(spans, results, out_weight):
    rows, width = results[0].shape[0], out_weight.shape[1]
    depth = sum(size for _, size in spans) * HD
    return pl.pallas_call(
        functools.partial(project_kernel, spans),
        out_shape=jax.ShapeDtypeStruct((rows, width), jnp.float32),
        in_specs=[HBM] * (len(spans) + 1),
        out_specs=HBM,
        scratch_shapes=[
            pltpu.VMEM((rows, depth), jnp.bfloat16),
            pltpu.VMEM((depth, width), jnp.bfloat16),
            pltpu.VMEM((rows, width), jnp.float32),
            pltpu.SemaphoreType.DMA((len(spans) + 1,)),
            pltpu.SemaphoreType.DMA((-(-width // STRIP),)),
        ],
        compiler_params=pltpu.CompilerParams(vmem_limit_bytes=VMEM_LIMIT),
        cost_estimate=pl.CostEstimate(flops=0, bytes_accessed=0, transcendentals=0),
    )(*results, out_weight)


def after(array, *others):
    return lax.optimization_barrier((array, *others))[0]


def on_device(queries, keys, values, tile_list, counts, out_weight):
    rows, model = queries.shape
    tiles = rows // TILE
    groups, members = lax.axis_size("temporal"), lax.axis_size("ulysses")
    group, member = lax.axis_index("temporal"), lax.axis_index("ulysses")
    total = groups * members
    both = ("temporal", "ulysses")
    hops = -(-REACH // tiles)
    relay = members == 2 and hops == 1
    if relay:
        place = [1, 2 - 2 * member, 2 * member]
    else:
        place = [hops] + [i for i in range(2 * hops + 1) if i != hops]
    first = ((group * members + member) - hops) * tiles
    meta = jnp.stack([jnp.asarray(x, jnp.int32) for x in (first, member * tiles, *place)])

    spans, low = [], 0
    for size in split_heads(model // HD):
        spans.append((low, size))
        low += size
    count = len(spans)
    sent = pack(queries, keys, values, spans[:1], [], VMEM_WHOLE)
    laid = pack(queries, after(keys, *sent), values, spans, spans, VMEM_LIMIT)
    blocks, heads_of = laid[:count], laid[count:]
    sent = [*sent, *blocks[1:]]

    onward = [(2 * g, 2 * g + 2) for g in range(groups - 1)]
    onward += [(2 * g + 3, 2 * g + 1) for g in range(groups - 1)]
    near = []
    for block in sent:
        if relay:
            with jax.named_scope(f"partner_{len(near)}"):
                near.append([lax.ppermute(block, "ulysses", [(0, 1), (1, 0)])])
        else:
            near.append(
                [
                    lax.ppermute(block, both, [(j, j - o) for j in range(total) if 0 <= j - o < total])
                    for o in range(-hops, hops + 1)
                    if o
                ]
            )

    results, acc = [], None
    ahead = max(0, count - 2)
    for i in range(count + 1):
        if i < count:
            pieces = [blocks[i], *near[i]]
            if relay:
                gate = near[i][0] if i < 2 else after(near[i][0], results[i - 2])
                with jax.named_scope(f"onward_{i}"):
                    pieces.append(lax.ppermute(gate, both, onward))
        if i >= 1:
            j = i - 1
            if j == ahead and ahead:
                with jax.named_scope("projection"):
                    acc = project(spans[:ahead], results, out_weight)
            early = list(zip(spans[ahead:j], results[ahead:])) if i == count else None
            own = heads_of[j] if acc is None or i == count else after(heads_of[j], acc)
            with jax.named_scope(f"attend_{j}"):
                results.append(
                    attend(meta, tile_list, counts, own, held, spans[j], early, out_weight, acc if i == count else None)
                )
        held = pieces
    return results[-1]


def solution(mesh):
    return jax.shard_map(
        on_device,
        mesh=mesh,
        in_specs=(
            P(("temporal", "ulysses"), None),
            P(("temporal", "ulysses"), None),
            P(("temporal", "ulysses"), None),
            P("temporal", None),
            P("temporal"),
            P(),
        ),
        out_specs=P(("temporal", "ulysses"), None),
        check_vma=False,
    )
```

```python
import functools
import math

import jax
import jax.numpy as jnp
from jax import lax
from jax.experimental import pallas as pl
from jax.experimental.pallas import tpu as pltpu
from jax.sharding import PartitionSpec as P

HD = 128
TILE = 128
REACH = 3
STRIP = 256
SUM_ROWS = 16
HBM = pl.BlockSpec(memory_space=pltpu.HBM)
SMEM = pl.BlockSpec(memory_space=pltpu.SMEM)
VMEM_LIMIT = 16 * 1024 * 1024
VMEM_WHOLE = 63 * 1024 * 1024


def split_heads(heads):
    sizes = []
    for share in (4 / 12, 3 / 12, 2 / 12, 2 / 12):
        size = min(max(1, round(share * heads)), heads - sum(sizes) - 1)
        if size > 0:
            sizes.append(size)
    return sizes + [heads - sum(sizes)]


def pack_kernel(groups, q_groups, q_ref, k_ref, v_ref, *refs):
    outs, q_outs = refs[: len(groups)], refs[len(groups) : len(groups) + len(q_groups)]
    v_buf, out_buf, q_buf, q_out, sems, q_sems = refs[len(groups) + len(q_groups) :]
    rows = k_ref.shape[0]

    def turn(source, target, at):
        for tile in range(rows // TILE):
            span = slice(tile * TILE, (tile + 1) * TILE)
            target[span] = source[at, span].T

    jobs, q_jobs = [], []
    for out, (low, size) in zip(outs, groups):
        for h in range(size):
            at = len(jobs)
            cols = pl.ds((low + h) * HD, HD)
            jobs.append(
                (
                    pltpu.make_async_copy(k_ref.at[:, cols], out_buf.at[at, 0], sems.at[at, 0]),
                    pltpu.make_async_copy(v_ref.at[:, cols], v_buf.at[at], sems.at[at, 1]),
                    pltpu.make_async_copy(out_buf.at[at], out.at[h], sems.at[at, 2]),
                )
            )
    for out, (low, size) in zip(q_outs, q_groups):
        for h in range(size):
            at = len(q_jobs)
            cols = pl.ds((low + h) * HD, HD)
            q_jobs.append(
                (
                    pltpu.make_async_copy(q_ref.at[:, cols], q_buf.at[at], q_sems.at[at, 0]),
                    pltpu.make_async_copy(q_out.at[at], out.at[h], q_sems.at[at, 1]),
                )
            )
    for load_k, load_v, _ in jobs:
        load_k.start()
        load_v.start()
    for load, _ in q_jobs:
        load.start()
    for at, (load_k, load_v, store) in enumerate(jobs):
        load_v.wait()
        turn(v_buf, out_buf.at[at, 1], at)
        load_k.wait()
        store.start()
    for at, (load, store) in enumerate(q_jobs):
        load.wait()
        turn(q_buf, q_out.at[at], at)
        store.start()
    for _, _, store in jobs:
        store.wait()
    for _, store in q_jobs:
        store.wait()


def pack(queries, keys, values, groups, q_groups, limit):
    rows = keys.shape[0]
    heads = sum(size for _, size in groups)
    q_heads = sum(size for _, size in q_groups)
    shapes = [(size, 2, rows, HD) for _, size in groups] + [(size, rows, HD) for _, size in q_groups]
    return pl.pallas_call(
        functools.partial(pack_kernel, groups, q_groups),
        out_shape=[jax.ShapeDtypeStruct(shape, keys.dtype) for shape in shapes],
        in_specs=[HBM] * 3,
        out_specs=[HBM] * len(shapes),
        scratch_shapes=[
            pltpu.VMEM((heads, rows, HD), keys.dtype),
            pltpu.VMEM((heads, 2, rows, HD), keys.dtype),
            pltpu.VMEM((max(q_heads, 1), rows, HD), keys.dtype),
            pltpu.VMEM((max(q_heads, 1), rows, HD), keys.dtype),
            pltpu.SemaphoreType.DMA((heads, 3)),
            pltpu.SemaphoreType.DMA((max(q_heads, 1), 2)),
        ],
        compiler_params=pltpu.CompilerParams(vmem_limit_bytes=limit),
        cost_estimate=pl.CostEstimate(flops=0, bytes_accessed=8 * rows * heads * HD, transcendentals=0),
    )(queries, keys, values)


def attend_kernel(cfg, meta, tiles_ref, counts_ref, q_hbm, *refs):
    low, size, pieces, project = cfg
    refs = list(refs)
    piece_refs = [refs.pop(0) for _ in range(pieces)]
    early_refs = [refs.pop(0) for _ in project or ()]
    w_hbm = None if project is None else refs.pop(0)
    out_hbm, q_buf, kv_buf, att_buf, load_sems, out_sems = refs[:6]
    rows = q_hbm.shape[1]
    tiles = rows // TILE
    slots = tiles_ref.shape[1]
    spans = pieces * rows
    loads = []
    for h in range(size):
        copies = [pltpu.make_async_copy(q_hbm.at[h], q_buf.at[h], load_sems.at[h, pieces])]
        for i, ref in enumerate(piece_refs):
            place = pl.ds(pl.multiple_of(meta[2 + i] * rows, rows), rows)
            copies.append(pltpu.make_async_copy(ref.at[h], kv_buf.at[h, :, place], load_sems.at[h, i]))
        for copy in copies:
            copy.start()
        loads.append(copies)
    late, lead = [], 0
    if project is not None:
        w_buf, out_buf, late_sems = refs[6:]
        lead = low
        late.append(pltpu.make_async_copy(w_hbm, w_buf, late_sems.at[0]))
        for i, ((early_low, early_size), ref) in enumerate(zip(project, early_refs)):
            where = pl.ds(early_low * HD, early_size * HD)
            late.append(pltpu.make_async_copy(ref, att_buf.at[:, where], late_sems.at[1 + i]))
        for copy in late:
            copy.start()

    first, row0 = meta[0], meta[1]
    scale = math.log2(math.e) / math.sqrt(HD)
    zeros = jnp.zeros((HD, TILE), jnp.bfloat16)
    places, v_places, ones = [], [], []
    for tile in range(tiles):
        row = row0 + tile
        live = counts_ref[row]
        at = [pl.multiple_of((tiles_ref[row, j] - first) * TILE, TILE) for j in range(slots)]
        places.append(at)
        v_places.append([pl.multiple_of(jnp.where(j < live, at[j], spans), TILE) for j in range(slots)])
        ones.append(
            [zeros[:SUM_ROWS] + jnp.where(j < live, 1.0, 0.0).astype(jnp.bfloat16) for j in range(slots)]
        )

    def scores(h, tile):
        k = jnp.concatenate([kv_buf[h, 0, pl.ds(p, TILE)] for p in places[tile]], axis=0)
        q = q_buf[h, tile * TILE : (tile + 1) * TILE]
        return jnp.dot(k, q, preferred_element_type=jnp.float32)

    def finish(h, tile, s):
        top = jnp.max(s, axis=0, keepdims=True)
        p = jnp.exp2((s - top) * scale).astype(jnp.bfloat16)
        v = jnp.concatenate([kv_buf[h, 1, pl.ds(at, HD)] for at in v_places[tile]], axis=1)
        sums = jnp.concatenate(ones[tile], axis=1)
        mixed = jnp.dot(jnp.concatenate([v, sums], axis=0), p, preferred_element_type=jnp.float32)
        here = slice(tile * TILE, (tile + 1) * TILE)
        col = lead + h
        att = (mixed[:HD] / mixed[HD : HD + 1]).astype(jnp.bfloat16)
        att_buf[here, col * HD : (col + 1) * HD] = att.T

    def ready(h):
        for copy in loads[h]:
            copy.wait()
        kv_buf[h, 1, spans : spans + TILE] = zeros

    jobs = [(h, tile) for h in range(size) for tile in range(tiles)]
    ready(0)
    ahead = scores(*jobs[0])
    for i, (h, tile) in enumerate(jobs):
        now = ahead
        if i + 1 < len(jobs):
            if jobs[i + 1][0] != h:
                ready(h + 1)
            ahead = scores(*jobs[i + 1])
        finish(h, tile, now)

    stores = []
    if project is None:
        stores.append(pltpu.make_async_copy(att_buf, out_hbm, out_sems.at[0]))
        stores[-1].start()
    else:
        for copy in late:
            copy.wait()
        for i, at in enumerate(range(0, out_buf.shape[1], STRIP)):
            here = slice(at, min(at + STRIP, out_buf.shape[1]))
            out_buf[:, here] = jnp.dot(att_buf[...], w_buf[:, here], preferred_element_type=jnp.float32).astype(
                out_buf.dtype
            )
            cols = pl.ds(at, here.stop - at)
            stores.append(pltpu.make_async_copy(out_buf.at[:, cols], out_hbm.at[:, cols], out_sems.at[i]))
            stores[-1].start()
    for copy in stores:
        copy.wait()


def attend(meta, tile_list, counts, queries, pieces, span, early, out_weight):
    rows, model = queries.shape[1], out_weight.shape[0]
    low, size = span
    tiles = rows // TILE
    count = len(pieces)
    width = out_weight.shape[1]
    operands = [meta, tile_list, counts, queries, *pieces]
    bf16 = jnp.bfloat16
    project = None if early is None else tuple(where for where, _ in early)
    if early is None:
        out_shape = jax.ShapeDtypeStruct((rows, size * HD), bf16)
        heads = size
    else:
        operands += [result for _, result in early]
        operands.append(out_weight)
        out_shape = jax.ShapeDtypeStruct((rows, width), bf16)
        heads = model // HD
    scratch = [
        pltpu.VMEM((size, rows, HD), bf16),
        pltpu.VMEM((size, 2, count * rows + TILE, HD), bf16),
        pltpu.VMEM((rows, heads * HD), bf16),
        pltpu.SemaphoreType.DMA((size, count + 1)),
        pltpu.SemaphoreType.DMA((-(-width // STRIP),)),
    ]
    if early is not None:
        scratch += [
            pltpu.VMEM((model, width), bf16),
            pltpu.VMEM((rows, width), bf16),
            pltpu.SemaphoreType.DMA((1 + len(project),)),
        ]
    return pl.pallas_call(
        functools.partial(attend_kernel, (low, size, count, project)),
        out_shape=out_shape,
        in_specs=[SMEM] * 3 + [HBM] * (len(operands) - 3),
        out_specs=HBM,
        scratch_shapes=scratch,
        compiler_params=pltpu.CompilerParams(vmem_limit_bytes=VMEM_LIMIT),
        cost_estimate=pl.CostEstimate(flops=0, bytes_accessed=0, transcendentals=0),
    )(*operands)


def after(array, *others):
    return lax.optimization_barrier((array, *others))[0]


def on_device(queries, keys, values, tile_list, counts, out_weight):
    rows, model = queries.shape
    tiles = rows // TILE
    groups, members = lax.axis_size("temporal"), lax.axis_size("ulysses")
    group, member = lax.axis_index("temporal"), lax.axis_index("ulysses")
    total = groups * members
    both = ("temporal", "ulysses")
    hops = -(-REACH // tiles)
    relay = members == 2 and hops == 1
    if relay:
        place = [1, 2 - 2 * member, 2 * member]
    else:
        place = [hops] + [i for i in range(2 * hops + 1) if i != hops]
    first = ((group * members + member) - hops) * tiles
    meta = jnp.stack([jnp.asarray(x, jnp.int32) for x in (first, member * tiles, *place)])

    spans, low = [], 0
    for size in split_heads(model // HD):
        spans.append((low, size))
        low += size
    count = len(spans)
    sent = pack(queries, keys, values, spans[:1], [], VMEM_WHOLE)
    laid = pack(queries, after(keys, *sent), values, spans, spans, VMEM_LIMIT)
    blocks, heads_of = laid[:count], laid[count:]
    sent = [*sent, *blocks[1:]]

    onward = [(2 * g, 2 * g + 2) for g in range(groups - 1)]
    onward += [(2 * g + 3, 2 * g + 1) for g in range(groups - 1)]
    near = []
    for block in sent:
        if relay:
            with jax.named_scope(f"partner_{len(near)}"):
                near.append([lax.ppermute(block, "ulysses", [(0, 1), (1, 0)])])
        else:
            near.append(
                [
                    lax.ppermute(block, both, [(j, j - o) for j in range(total) if 0 <= j - o < total])
                    for o in range(-hops, hops + 1)
                    if o
                ]
            )

    results = []
    for i in range(count + 1):
        if i < count:
            pieces = [blocks[i], *near[i]]
            if relay:
                gate = near[i][0] if i < 2 else after(near[i][0], results[i - 2])
                with jax.named_scope(f"onward_{i}"):
                    pieces.append(lax.ppermute(gate, both, onward))
        if i >= 1:
            j = i - 1
            early = list(zip(spans[:j], results)) if i == count else None
            with jax.named_scope(f"attend_{j}"):
                results.append(attend(meta, tile_list, counts, heads_of[j], held, spans[j], early, out_weight))
        held = pieces
    return results[-1]


def solution(mesh):
    return jax.shard_map(
        on_device,
        mesh=mesh,
        in_specs=(
            P(("temporal", "ulysses"), None),
            P(("temporal", "ulysses"), None),
            P(("temporal", "ulysses"), None),
            P("temporal", None),
            P("temporal"),
            P(),
        ),
        out_specs=P(("temporal", "ulysses"), None),
        check_vma=False,
    )
```

```python
import functools
import math

import jax
import jax.numpy as jnp
from jax import lax
from jax.experimental import pallas as pl
from jax.experimental.pallas import tpu as pltpu
from jax.sharding import PartitionSpec as P

HD = 128
TILE = 128
REACH = 3
STRIP = 256
HBM = pl.BlockSpec(memory_space=pltpu.HBM)
VMEM = pl.BlockSpec(memory_space=pltpu.VMEM)
SMEM = pl.BlockSpec(memory_space=pltpu.SMEM)
VMEM_LIMIT = 16 * 1024 * 1024
VMEM_WHOLE = 63 * 1024 * 1024


def split_heads(heads):
    sizes = []
    for share in (4 / 12, 3 / 12, 2 / 12, 2 / 12):
        size = min(max(1, round(share * heads)), heads - sum(sizes) - 1)
        if size > 0:
            sizes.append(size)
    return sizes + [heads - sum(sizes)]


def pack_kernel(groups, q_groups, q_ref, k_ref, v_ref, *refs):
    outs, q_outs = refs[: len(groups)], refs[len(groups) : len(groups) + len(q_groups)]
    k_buf, out_buf, q_buf, sems, q_sems = refs[len(groups) + len(q_groups) :]
    rows = k_ref.shape[0]
    jobs, q_jobs = [], []
    for out, (low, size) in zip(outs, groups):
        for h in range(size):
            at = len(jobs)
            cols = pl.ds((low + h) * HD, HD)
            jobs.append(
                (
                    pltpu.make_async_copy(k_ref.at[:, cols], k_buf.at[at], sems.at[at, 0]),
                    pltpu.make_async_copy(v_ref.at[:, cols], out_buf.at[at, 1], sems.at[at, 1]),
                    pltpu.make_async_copy(out_buf.at[at], out.at[h], sems.at[at, 2]),
                )
            )
    for out, (low, size) in zip(q_outs, q_groups):
        for h in range(size):
            at = len(q_jobs)
            cols = pl.ds((low + h) * HD, HD)
            q_jobs.append(
                (
                    pltpu.make_async_copy(q_ref.at[:, cols], q_buf.at[at], q_sems.at[at, 0]),
                    pltpu.make_async_copy(q_buf.at[at], out.at[h], q_sems.at[at, 1]),
                )
            )
    for load_k, load_v, _ in jobs:
        load_k.start()
        load_v.start()
    for load, _ in q_jobs:
        load.start()
    for at, (load_k, load_v, store) in enumerate(jobs):
        load_k.wait()
        for tile in range(rows // TILE):
            span = slice(tile * TILE, (tile + 1) * TILE)
            out_buf[at, 0, span] = k_buf[at, span].T
        load_v.wait()
        store.start()
    for load, store in q_jobs:
        load.wait()
        store.start()
    for _, _, store in jobs:
        store.wait()
    for _, store in q_jobs:
        store.wait()


def pack(queries, keys, values, groups, q_groups, limit):
    rows = keys.shape[0]
    heads = sum(size for _, size in groups)
    q_heads = sum(size for _, size in q_groups)
    shapes = [(size, 2, rows, HD) for _, size in groups] + [(size, rows, HD) for _, size in q_groups]
    return pl.pallas_call(
        functools.partial(pack_kernel, groups, q_groups),
        out_shape=[jax.ShapeDtypeStruct(shape, keys.dtype) for shape in shapes],
        in_specs=[HBM] * 3,
        out_specs=[HBM] * len(shapes),
        scratch_shapes=[
            pltpu.VMEM((heads, rows, HD), keys.dtype),
            pltpu.VMEM((heads, 2, rows, HD), keys.dtype),
            pltpu.VMEM((max(q_heads, 1), rows, HD), keys.dtype),
            pltpu.SemaphoreType.DMA((heads, 3)),
            pltpu.SemaphoreType.DMA((max(q_heads, 1), 2)),
        ],
        compiler_params=pltpu.CompilerParams(vmem_limit_bytes=limit),
        cost_estimate=pl.CostEstimate(flops=0, bytes_accessed=8 * rows * heads * HD, transcendentals=0),
    )(queries, keys, values)


def attend_kernel(cfg, meta, tiles_ref, counts_ref, q_ref, *refs):
    low, size, pieces, project = cfg
    refs = list(refs)
    piece_refs = [refs.pop(0) for _ in range(pieces)]
    early_refs = [refs.pop(0) for _ in project or ()]
    w_ref = None if project is None else refs.pop(0)
    out_ref, kv_buf = refs[:2]
    rows = q_ref.shape[1]
    tiles = rows // TILE
    slots = tiles_ref.shape[1]
    spans = pieces * rows
    lead = 0
    att_buf = out_ref
    if project is not None:
        att_buf, out_buf, out_sems = refs[2:]
        lead = low
        for (early_low, early_size), ref in zip(project, early_refs):
            att_buf[:, early_low * HD : (early_low + early_size) * HD] = ref[...]

    first, row0 = meta[0], meta[1]
    scale = math.log2(math.e) / math.sqrt(HD)
    zeros = jnp.zeros((TILE, HD), jnp.bfloat16)
    places, v_places, ones = [], [], []
    for tile in range(tiles):
        row = row0 + tile
        live = counts_ref[row]
        at = [pl.multiple_of((tiles_ref[row, j] - first) * TILE, TILE) for j in range(slots)]
        places.append(at)
        v_places.append([pl.multiple_of(jnp.where(j < live, at[j], spans), TILE) for j in range(slots)])
        ones.append([zeros + jnp.where(j < live, 1.0, 0.0).astype(jnp.bfloat16) for j in range(slots)])

    def scores(h, tile):
        k = jnp.concatenate([kv_buf[h % 2, 0, pl.ds(p, TILE)] for p in places[tile]], axis=1)
        q = q_ref[h, tile * TILE : (tile + 1) * TILE]
        return jnp.dot(q, k, preferred_element_type=jnp.float32)

    def finish(h, tile, s):
        top = jnp.max(s, axis=1, keepdims=True)
        p = jnp.exp2((s - top) * scale).astype(jnp.bfloat16)
        v = jnp.concatenate(
            [
                jnp.concatenate([kv_buf[h % 2, 1, pl.ds(at, TILE)], one], axis=1)
                for at, one in zip(v_places[tile], ones[tile])
            ],
            axis=0,
        )
        mixed = jnp.dot(p, v, preferred_element_type=jnp.float32)
        here = slice(tile * TILE, (tile + 1) * TILE)
        col = lead + h
        att_buf[here, col * HD : (col + 1) * HD] = (mixed[:, :HD] / mixed[:, HD:]).astype(jnp.bfloat16)

    def ready(h):
        for i, ref in enumerate(piece_refs):
            place = pl.ds(pl.multiple_of(meta[2 + i] * rows, rows), rows)
            for part in range(2):
                kv_buf[h % 2, part, place] = ref[h, part]
        kv_buf[h % 2, 1, spans : spans + TILE] = zeros

    jobs = [(h, tile) for h in range(size) for tile in range(tiles)]
    ready(0)
    ahead = scores(*jobs[0])
    for i, (h, tile) in enumerate(jobs):
        now = ahead
        if i + 1 < len(jobs):
            if jobs[i + 1][0] != h:
                ready(h + 1)
            ahead = scores(*jobs[i + 1])
        finish(h, tile, now)

    if project is None:
        return
    stores = []
    for i, at in enumerate(range(0, out_buf.shape[1], STRIP)):
        here = slice(at, min(at + STRIP, out_buf.shape[1]))
        part = jnp.dot(att_buf[...], w_ref[:, here], preferred_element_type=jnp.float32)
        out_buf[:, here] = part.astype(out_buf.dtype)
        cols = pl.ds(at, here.stop - at)
        stores.append(pltpu.make_async_copy(out_buf.at[:, cols], out_ref.at[:, cols], out_sems.at[i]))
        stores[-1].start()
    for copy in stores:
        copy.wait()


def attend(meta, tile_list, counts, queries, pieces, span, early, out_weight):
    rows, model = queries.shape[1], out_weight.shape[0]
    low, size = span
    tiles = rows // TILE
    count = len(pieces)
    width = out_weight.shape[1]
    operands = [meta, tile_list, counts, queries, *pieces]
    bf16 = jnp.bfloat16
    project = None if early is None else tuple(where for where, _ in early)
    if early is None:
        out_shape = jax.ShapeDtypeStruct((rows, size * HD), bf16)
        heads = size
    else:
        operands += [result for _, result in early]
        operands.append(out_weight)
        out_shape = jax.ShapeDtypeStruct((rows, width), bf16)
        heads = model // HD
    scratch = [pltpu.VMEM((2, 2, count * rows + TILE, HD), bf16)]
    if early is not None:
        scratch += [
            pltpu.VMEM((rows, heads * HD), bf16),
            pltpu.VMEM((rows, width), bf16),
            pltpu.SemaphoreType.DMA((-(-width // STRIP),)),
        ]
    return pl.pallas_call(
        functools.partial(attend_kernel, (low, size, count, project)),
        out_shape=out_shape,
        in_specs=[SMEM] * 3 + [VMEM] * (len(operands) - 3),
        out_specs=VMEM if early is None else HBM,
        scratch_shapes=scratch,
        compiler_params=pltpu.CompilerParams(vmem_limit_bytes=VMEM_LIMIT),
        cost_estimate=pl.CostEstimate(flops=0, bytes_accessed=0, transcendentals=0),
    )(*operands)


def after(array, *others):
    return lax.optimization_barrier((array, *others))[0]


def on_device(queries, keys, values, tile_list, counts, out_weight):
    rows, model = queries.shape
    tiles = rows // TILE
    groups, members = lax.axis_size("temporal"), lax.axis_size("ulysses")
    group, member = lax.axis_index("temporal"), lax.axis_index("ulysses")
    total = groups * members
    both = ("temporal", "ulysses")
    hops = -(-REACH // tiles)
    relay = members == 2 and hops == 1
    if relay:
        place = [1, 2 - 2 * member, 2 * member]
    else:
        place = [hops] + [i for i in range(2 * hops + 1) if i != hops]
    first = ((group * members + member) - hops) * tiles
    meta = jnp.stack([jnp.asarray(x, jnp.int32) for x in (first, member * tiles, *place)])

    spans, low = [], 0
    for size in split_heads(model // HD):
        spans.append((low, size))
        low += size
    count = len(spans)
    sent = pack(queries, keys, values, spans[:1], [], VMEM_WHOLE)
    laid = pack(queries, after(keys, *sent), values, spans, spans, VMEM_LIMIT)
    blocks, heads_of = laid[:count], laid[count:]
    sent = [*sent, *blocks[1:]]

    onward = [(2 * g, 2 * g + 2) for g in range(groups - 1)]
    onward += [(2 * g + 3, 2 * g + 1) for g in range(groups - 1)]
    near = []
    for block in sent:
        if relay:
            with jax.named_scope(f"partner_{len(near)}"):
                near.append([lax.ppermute(block, "ulysses", [(0, 1), (1, 0)])])
        else:
            near.append(
                [
                    lax.ppermute(block, both, [(j, j - o) for j in range(total) if 0 <= j - o < total])
                    for o in range(-hops, hops + 1)
                    if o
                ]
            )

    results = []
    for i in range(count + 1):
        if i < count:
            pieces = [blocks[i], *near[i]]
            if relay:
                gate = near[i][0] if i < 2 else after(near[i][0], results[i - 2])
                with jax.named_scope(f"onward_{i}"):
                    pieces.append(lax.ppermute(gate, both, onward))
        if i >= 1:
            j = i - 1
            early = list(zip(spans[:j], results)) if i == count else None
            with jax.named_scope(f"attend_{j}"):
                results.append(attend(meta, tile_list, counts, heads_of[j], held, spans[j], early, out_weight))
        held = pieces
    return results[-1]


def solution(mesh):
    return jax.shard_map(
        on_device,
        mesh=mesh,
        in_specs=(
            P(("temporal", "ulysses"), None),
            P(("temporal", "ulysses"), None),
            P(("temporal", "ulysses"), None),
            P("temporal", None),
            P("temporal"),
            P(),
        ),
        out_specs=P(("temporal", "ulysses"), None),
        check_vma=False,
    )
```

```python
import functools
import math

import jax
import jax.numpy as jnp
from jax import lax
from jax.experimental import pallas as pl
from jax.experimental.pallas import tpu as pltpu
from jax.sharding import PartitionSpec as P

HD = 128
TILE = 128
REACH = 3
STRIP = 256
HBM = pl.BlockSpec(memory_space=pltpu.HBM)
VMEM = pl.BlockSpec(memory_space=pltpu.VMEM)
SMEM = pl.BlockSpec(memory_space=pltpu.SMEM)
VMEM_LIMIT = 14 * 1024 * 1024
VMEM_WHOLE = 63 * 1024 * 1024


def split_heads(heads):
    sizes = []
    for share in (4 / 12, 3 / 12, 2 / 12, 2 / 12):
        size = min(max(1, round(share * heads)), heads - sum(sizes) - 1)
        if size > 0:
            sizes.append(size)
    return sizes + [heads - sum(sizes)]


def pack_kernel(groups, q_groups, q_ref, k_ref, v_ref, *refs):
    outs, q_outs = refs[: len(groups)], refs[len(groups) : len(groups) + len(q_groups)]
    k_buf, out_buf, q_buf, sems, q_sems = refs[len(groups) + len(q_groups) :]
    rows = k_ref.shape[0]
    jobs, q_jobs = [], []
    for out, (low, size) in zip(outs, groups):
        for h in range(size):
            at = len(jobs)
            cols = pl.ds((low + h) * HD, HD)
            jobs.append(
                (
                    pltpu.make_async_copy(k_ref.at[:, cols], k_buf.at[at], sems.at[at, 0]),
                    pltpu.make_async_copy(v_ref.at[:, cols], out_buf.at[at, 1], sems.at[at, 1]),
                    pltpu.make_async_copy(out_buf.at[at], out.at[h], sems.at[at, 2]),
                )
            )
    for out, (low, size) in zip(q_outs, q_groups):
        for h in range(size):
            at = len(q_jobs)
            cols = pl.ds((low + h) * HD, HD)
            q_jobs.append(
                (
                    pltpu.make_async_copy(q_ref.at[:, cols], q_buf.at[at], q_sems.at[at, 0]),
                    pltpu.make_async_copy(q_buf.at[at], out.at[h], q_sems.at[at, 1]),
                )
            )
    for load_k, load_v, _ in jobs:
        load_k.start()
        load_v.start()
    for load, _ in q_jobs:
        load.start()
    for at, (load_k, load_v, store) in enumerate(jobs):
        load_k.wait()
        for tile in range(rows // TILE):
            span = slice(tile * TILE, (tile + 1) * TILE)
            out_buf[at, 0, span] = k_buf[at, span].T
        load_v.wait()
        store.start()
    for load, store in q_jobs:
        load.wait()
        store.start()
    for _, _, store in jobs:
        store.wait()
    for _, store in q_jobs:
        store.wait()


def pack(queries, keys, values, groups, q_groups, limit):
    rows = keys.shape[0]
    heads = sum(size for _, size in groups)
    q_heads = sum(size for _, size in q_groups)
    shapes = [(size, 2, rows, HD) for _, size in groups] + [(size, rows, HD) for _, size in q_groups]
    return pl.pallas_call(
        functools.partial(pack_kernel, groups, q_groups),
        out_shape=[jax.ShapeDtypeStruct(shape, keys.dtype) for shape in shapes],
        in_specs=[HBM] * 3,
        out_specs=[HBM] * len(shapes),
        scratch_shapes=[
            pltpu.VMEM((heads, rows, HD), keys.dtype),
            pltpu.VMEM((heads, 2, rows, HD), keys.dtype),
            pltpu.VMEM((max(q_heads, 1), rows, HD), keys.dtype),
            pltpu.SemaphoreType.DMA((heads, 3)),
            pltpu.SemaphoreType.DMA((max(q_heads, 1), 2)),
        ],
        compiler_params=pltpu.CompilerParams(vmem_limit_bytes=limit),
        cost_estimate=pl.CostEstimate(flops=0, bytes_accessed=8 * rows * heads * HD, transcendentals=0),
    )(queries, keys, values)


def attend_kernel(cfg, meta, q_ref, *refs):
    low, size, pieces, slots, early = cfg
    last = early is not None
    refs = list(refs)
    piece_refs = [refs.pop(0) for _ in range(pieces)]
    early_refs = [refs.pop(0) for _ in early or ()]
    w_ref, acc_ref = (refs.pop(0), refs.pop(0)) if last else (None, None)
    out_ref, kv_buf = refs[:2]
    rows = q_ref.shape[1]
    tiles = rows // TILE
    spans = pieces * rows
    att_buf, lead = out_ref, 0
    if last:
        att_buf, out_buf, out_sems = refs[2:]
        for extent, ref in zip(early, early_refs):
            att_buf[:, lead * HD : (lead + extent) * HD] = ref[...]
            lead += extent

    scale = math.log2(math.e) / math.sqrt(HD)
    zeros = jnp.zeros((TILE, HD), jnp.bfloat16)
    places, v_places, ones = [], [], []
    for tile in range(tiles):
        row = pieces + tile * (slots + 1)
        live = meta[row]
        at = [pl.multiple_of(meta[row + 1 + j] * TILE, TILE) for j in range(slots)]
        places.append(at)
        v_places.append([pl.multiple_of(jnp.where(j < live, at[j], spans), TILE) for j in range(slots)])
        ones.append([zeros + jnp.where(j < live, 1.0, 0.0).astype(jnp.bfloat16) for j in range(slots)])

    def scores(h, tile):
        k = jnp.concatenate([kv_buf[h % 2, 0, pl.ds(p, TILE)] for p in places[tile]], axis=1)
        q = q_ref[h, tile * TILE : (tile + 1) * TILE]
        return jnp.dot(q, k, preferred_element_type=jnp.float32)

    def finish(h, tile, s):
        top = jnp.max(s, axis=1, keepdims=True)
        p = jnp.exp2((s - top) * scale).astype(jnp.bfloat16)
        v = jnp.concatenate(
            [
                jnp.concatenate([kv_buf[h % 2, 1, pl.ds(at, TILE)], one], axis=1)
                for at, one in zip(v_places[tile], ones[tile])
            ],
            axis=0,
        )
        mixed = jnp.dot(p, v, preferred_element_type=jnp.float32)
        here = slice(tile * TILE, (tile + 1) * TILE)
        att_buf[here, (lead + h) * HD : (lead + h + 1) * HD] = (mixed[:, :HD] / mixed[:, HD:]).astype(jnp.bfloat16)

    def ready(h):
        for i, ref in enumerate(piece_refs):
            place = pl.ds(pl.multiple_of(meta[i] * rows, rows), rows)
            for part in range(2):
                kv_buf[h % 2, part, place] = ref[h, part]
        kv_buf[h % 2, 1, spans : spans + TILE] = zeros

    jobs = [(h, tile) for h in range(size) for tile in range(tiles)]
    ready(0)
    ahead = scores(*jobs[0])
    for i, (h, tile) in enumerate(jobs):
        now = ahead
        if i + 1 < len(jobs):
            if jobs[i + 1][0] != h:
                ready(h + 1)
            ahead = scores(*jobs[i + 1])
        finish(h, tile, now)

    if not last:
        return
    stores = []
    for i, at in enumerate(range(0, out_buf.shape[1], STRIP)):
        here = slice(at, min(at + STRIP, out_buf.shape[1]))
        weights = w_ref[(low - lead) * HD : (low + size) * HD, here]
        part = acc_ref[:, here] + jnp.dot(att_buf[...], weights, preferred_element_type=jnp.float32)
        out_buf[:, here] = part.astype(out_buf.dtype)
        cols = pl.ds(at, here.stop - at)
        stores.append(pltpu.make_async_copy(out_buf.at[:, cols], out_ref.at[:, cols], out_sems.at[i]))
        stores[-1].start()
    for copy in stores:
        copy.wait()


def attend(meta, slots, queries, pieces, span, early, out_weight, acc):
    rows = queries.shape[1]
    low, size = span
    count = len(pieces)
    width = out_weight.shape[1]
    bf16 = jnp.bfloat16
    last = early is not None
    operands = [meta, queries, *pieces]
    scratch = [pltpu.VMEM((2, 2, count * rows + TILE, HD), bf16)]
    if last:
        operands += [*early, out_weight, acc]
        scratch += [
            pltpu.VMEM((rows, size * HD + sum(part.shape[1] for part in early)), bf16),
            pltpu.VMEM((rows, width), bf16),
            pltpu.SemaphoreType.DMA((-(-width // STRIP),)),
        ]
    return pl.pallas_call(
        functools.partial(attend_kernel, (low, size, count, slots, tuple(part.shape[1] // HD for part in early) if last else None)),
        out_shape=jax.ShapeDtypeStruct((rows, width if last else size * HD), bf16),
        in_specs=[SMEM] + [VMEM] * (len(operands) - 1),
        out_specs=HBM if last else VMEM,
        scratch_shapes=scratch,
        compiler_params=pltpu.CompilerParams(vmem_limit_bytes=VMEM_LIMIT),
        cost_estimate=pl.CostEstimate(flops=0, bytes_accessed=0, transcendentals=0),
    )(*operands)


def project_kernel(spans, *refs):
    parts = refs[: len(spans)]
    w_ref, out_ref, att_buf = refs[len(spans) :]
    for (low, size), ref in zip(spans, parts):
        att_buf[:, low * HD : (low + size) * HD] = ref[...]
    depth = att_buf.shape[1]
    for at in range(0, out_ref.shape[1], STRIP):
        here = slice(at, min(at + STRIP, out_ref.shape[1]))
        out_ref[:, here] = jnp.dot(att_buf[...], w_ref[:depth, here], preferred_element_type=jnp.float32)


def project(spans, results, out_weight):
    rows, width = results[0].shape[0], out_weight.shape[1]
    depth = sum(size for _, size in spans) * HD
    return pl.pallas_call(
        functools.partial(project_kernel, spans),
        out_shape=jax.ShapeDtypeStruct((rows, width), jnp.float32),
        in_specs=[VMEM] * (len(spans) + 1),
        out_specs=VMEM,
        scratch_shapes=[pltpu.VMEM((rows, depth), jnp.bfloat16)],
        compiler_params=pltpu.CompilerParams(vmem_limit_bytes=VMEM_LIMIT),
        cost_estimate=pl.CostEstimate(flops=0, bytes_accessed=0, transcendentals=0),
    )(*results, out_weight)


def after(array, *others):
    return lax.optimization_barrier((array, *others))[0]


def on_device(queries, keys, values, tile_list, counts, out_weight):
    rows, model = queries.shape
    tiles = rows // TILE
    groups, members = lax.axis_size("temporal"), lax.axis_size("ulysses")
    group, member = lax.axis_index("temporal"), lax.axis_index("ulysses")
    total = groups * members
    both = ("temporal", "ulysses")
    hops = -(-REACH // tiles)
    relay = members == 2 and hops == 1
    if relay:
        place = [1, 2 - 2 * member, 2 * member]
    else:
        place = [hops] + [i for i in range(2 * hops + 1) if i != hops]
    first = ((group * members + member) - hops) * tiles
    slots = tile_list.shape[1]
    lists = jnp.concatenate([counts[:, None], tile_list - first], axis=1)
    lists = lax.dynamic_slice_in_dim(lists, member * tiles, tiles, axis=0)
    meta = jnp.concatenate([jnp.stack([jnp.asarray(x, jnp.int32) for x in place]), lists.reshape(-1)])

    spans, low = [], 0
    for size in split_heads(model // HD):
        spans.append((low, size))
        low += size
    count = len(spans)
    sent = pack(queries, keys, values, spans[:1], [], VMEM_WHOLE)
    laid = pack(queries, after(keys, *sent), values, spans, spans, VMEM_LIMIT)
    blocks, heads_of = laid[:count], laid[count:]
    sent = [*sent, *blocks[1:]]

    onward = [(2 * g, 2 * g + 2) for g in range(groups - 1)]
    onward += [(2 * g + 3, 2 * g + 1) for g in range(groups - 1)]
    near = []
    for block in sent:
        if relay:
            with jax.named_scope(f"partner_{len(near)}"):
                near.append([lax.ppermute(block, "ulysses", [(0, 1), (1, 0)])])
        else:
            near.append(
                [
                    lax.ppermute(block, both, [(j, j - o) for j in range(total) if 0 <= j - o < total])
                    for o in range(-hops, hops + 1)
                    if o
                ]
            )

    results, acc, ahead = [], None, max(0, count - 2)
    for i in range(count + 1):
        if i < count:
            pieces = [blocks[i], *near[i]]
            if relay:
                gate = near[i][0] if i < 2 else after(near[i][0], results[i - 2])
                with jax.named_scope(f"onward_{i}"):
                    pieces.append(lax.ppermute(gate, both, onward))
        if i >= 1:
            j = i - 1
            own = heads_of[j]
            if j == ahead:
                if ahead:
                    with jax.named_scope("projection"):
                        acc = project(spans[:ahead], results, out_weight)
                    own = after(own, acc)
                else:
                    acc = jnp.zeros((rows, out_weight.shape[1]), jnp.float32)
            early = results[ahead:] if i == count else None
            with jax.named_scope(f"attend_{j}"):
                results.append(attend(meta, slots, own, held, spans[j], early, out_weight, acc))
        held = pieces
    return results[-1]


def solution(mesh):
    return jax.shard_map(
        on_device,
        mesh=mesh,
        in_specs=(
            P(("temporal", "ulysses"), None),
            P(("temporal", "ulysses"), None),
            P(("temporal", "ulysses"), None),
            P("temporal", None),
            P("temporal"),
            P(),
        ),
        out_specs=P(("temporal", "ulysses"), None),
        check_vma=False,
    )
```

```python
import functools
import math

import jax
import jax.numpy as jnp
from jax import lax
from jax.experimental import pallas as pl
from jax.experimental.pallas import tpu as pltpu
from jax.sharding import PartitionSpec as P

HD = 128
TILE = 128
REACH = 3
STRIP = 256
HBM = pl.BlockSpec(memory_space=pltpu.HBM)
VMEM = pl.BlockSpec(memory_space=pltpu.VMEM)
SMEM = pl.BlockSpec(memory_space=pltpu.SMEM)
VMEM_LIMIT = 14 * 1024 * 1024
VMEM_WHOLE = 63 * 1024 * 1024


def split_heads(heads):
    sizes = []
    for share in (3 / 12, 3 / 12, 2 / 12, 2 / 12):
        size = min(max(1, round(share * heads)), heads - sum(sizes) - 1)
        if size > 0:
            sizes.append(size)
    return sizes + [heads - sum(sizes)]


def pack_kernel(groups, q_groups, cuts, cut_ref, q_ref, k_ref, v_ref, *refs):
    refs = list(refs)
    outs = [refs.pop(0) for _ in groups]
    q_outs = [refs.pop(0) for _ in q_groups]
    cut_outs = [refs.pop(0) for _ in cuts]
    k_buf, out_buf, q_buf, sems, q_sems, cut_sems = refs
    rows = k_ref.shape[0]
    jobs, q_jobs = [], []
    for out, (low, size) in zip(outs, groups):
        for h in range(size):
            at = len(jobs)
            cols = pl.ds((low + h) * HD, HD)
            jobs.append(
                (
                    pltpu.make_async_copy(k_ref.at[:, cols], k_buf.at[at], sems.at[at, 0]),
                    pltpu.make_async_copy(v_ref.at[:, cols], out_buf.at[at, 1], sems.at[at, 1]),
                    pltpu.make_async_copy(out_buf.at[at], out.at[h], sems.at[at, 2]),
                )
            )
    for out, (low, size) in zip(q_outs, q_groups):
        for h in range(size):
            at = len(q_jobs)
            cols = pl.ds((low + h) * HD, HD)
            q_jobs.append(
                (
                    pltpu.make_async_copy(q_ref.at[:, cols], q_buf.at[at], q_sems.at[at, 0]),
                    pltpu.make_async_copy(q_buf.at[at], out.at[h], q_sems.at[at, 1]),
                )
            )
    for load_k, load_v, _ in jobs:
        load_k.start()
        load_v.start()
    for load, _ in q_jobs:
        load.start()
    for at, (load_k, load_v, store) in enumerate(jobs):
        load_k.wait()
        for tile in range(rows // TILE):
            span = slice(tile * TILE, (tile + 1) * TILE)
            out_buf[at, 0, span] = k_buf[at, span].T
        load_v.wait()
        store.start()
    cut_jobs = []
    if cuts:
        size = groups[-1][1]
        for h in range(size):
            for i, (extent, out) in enumerate(zip(cuts, cut_outs)):
                part = pl.ds(pl.multiple_of(cut_ref[i] * TILE, TILE), extent * TILE)
                source = out_buf.at[len(jobs) - size + h, :, part]
                cut_jobs.append(pltpu.make_async_copy(source, out.at[h], cut_sems.at[h, i]))
                cut_jobs[-1].start()
    for load, store in q_jobs:
        load.wait()
        store.start()
    for _, _, store in jobs:
        store.wait()
    for _, store in q_jobs:
        store.wait()
    for store in cut_jobs:
        store.wait()


def pack(cut_at, queries, keys, values, groups, q_groups, cuts, limit):
    rows = keys.shape[0]
    heads = sum(size for _, size in groups)
    q_heads = sum(size for _, size in q_groups)
    last = groups[-1][1]
    shapes = [(size, 2, rows, HD) for _, size in groups] + [(size, rows, HD) for _, size in q_groups]
    shapes += [(last, 2, extent * TILE, HD) for extent in cuts]
    return pl.pallas_call(
        functools.partial(pack_kernel, groups, q_groups, cuts),
        out_shape=[jax.ShapeDtypeStruct(shape, keys.dtype) for shape in shapes],
        in_specs=[SMEM] + [HBM] * 3,
        out_specs=[HBM] * len(shapes),
        scratch_shapes=[
            pltpu.VMEM((heads, rows, HD), keys.dtype),
            pltpu.VMEM((heads, 2, rows, HD), keys.dtype),
            pltpu.VMEM((max(q_heads, 1), rows, HD), keys.dtype),
            pltpu.SemaphoreType.DMA((heads, 3)),
            pltpu.SemaphoreType.DMA((max(q_heads, 1), 2)),
            pltpu.SemaphoreType.DMA((last, max(len(cuts), 1))),
        ],
        compiler_params=pltpu.CompilerParams(vmem_limit_bytes=limit),
        cost_estimate=pl.CostEstimate(flops=0, bytes_accessed=8 * rows * heads * HD, transcendentals=0),
    )(cut_at, queries, keys, values)


def attend_kernel(cfg, meta, q_ref, *refs):
    low, size, pieces, place_at, list_at, slots, spans, early = cfg
    last = early is not None
    refs = list(refs)
    piece_refs = [refs.pop(0) for _ in range(pieces)]
    early_refs = [refs.pop(0) for _ in early or ()]
    w_ref, acc_ref = (refs.pop(0), refs.pop(0)) if last else (None, None)
    out_ref, kv_buf = refs[:2]
    rows = q_ref.shape[1]
    tiles = rows // TILE
    att_buf, lead = out_ref, 0
    if last:
        att_buf, out_buf, out_sems = refs[2:]
        for extent, ref in zip(early, early_refs):
            att_buf[:, lead * HD : (lead + extent) * HD] = ref[...]
            lead += extent

    scale = math.log2(math.e) / math.sqrt(HD)
    zeros = jnp.zeros((TILE, HD), jnp.bfloat16)
    places, v_places, ones = [], [], []
    for tile in range(tiles):
        row = list_at + tile * (slots + 1)
        live = meta[row]
        at = [pl.multiple_of(meta[row + 1 + j] * TILE, TILE) for j in range(slots)]
        places.append(at)
        v_places.append([pl.multiple_of(jnp.where(j < live, at[j], spans), TILE) for j in range(slots)])
        ones.append([zeros + jnp.where(j < live, 1.0, 0.0).astype(jnp.bfloat16) for j in range(slots)])

    def scores(h, tile):
        k = jnp.concatenate([kv_buf[h % 2, 0, pl.ds(p, TILE)] for p in places[tile]], axis=1)
        q = q_ref[h, tile * TILE : (tile + 1) * TILE]
        return jnp.dot(q, k, preferred_element_type=jnp.float32)

    def finish(h, tile, s):
        top = jnp.max(s, axis=1, keepdims=True)
        p = jnp.exp2((s - top) * scale).astype(jnp.bfloat16)
        v = jnp.concatenate(
            [
                jnp.concatenate([kv_buf[h % 2, 1, pl.ds(at, TILE)], one], axis=1)
                for at, one in zip(v_places[tile], ones[tile])
            ],
            axis=0,
        )
        mixed = jnp.dot(p, v, preferred_element_type=jnp.float32)
        here = slice(tile * TILE, (tile + 1) * TILE)
        att_buf[here, (lead + h) * HD : (lead + h + 1) * HD] = (mixed[:, :HD] / mixed[:, HD:]).astype(jnp.bfloat16)

    def ready(h):
        for i, ref in enumerate(piece_refs):
            place = pl.ds(pl.multiple_of(meta[place_at + i] * TILE, TILE), ref.shape[2])
            for part in range(2):
                kv_buf[h % 2, part, place] = ref[h, part]
        kv_buf[h % 2, 1, spans : spans + TILE] = zeros

    jobs = [(h, tile) for h in range(size) for tile in range(tiles)]
    ready(0)
    ahead = scores(*jobs[0])
    for i, (h, tile) in enumerate(jobs):
        now = ahead
        if i + 1 < len(jobs):
            if jobs[i + 1][0] != h:
                ready(h + 1)
            ahead = scores(*jobs[i + 1])
        finish(h, tile, now)

    if not last:
        return
    stores = []
    for i, at in enumerate(range(0, out_buf.shape[1], STRIP)):
        here = slice(at, min(at + STRIP, out_buf.shape[1]))
        weights = w_ref[(low - lead) * HD : (low + size) * HD, here]
        part = acc_ref[:, here] + jnp.dot(att_buf[...], weights, preferred_element_type=jnp.float32)
        out_buf[:, here] = part.astype(out_buf.dtype)
        cols = pl.ds(at, here.stop - at)
        stores.append(pltpu.make_async_copy(out_buf.at[:, cols], out_ref.at[:, cols], out_sems.at[i]))
        stores[-1].start()
    for copy in stores:
        copy.wait()


def attend(meta, layout, queries, pieces, span, early, out_weight, acc):
    rows = queries.shape[1]
    low, size = span
    place_at, list_at, slots, reach = layout
    width = out_weight.shape[1]
    bf16 = jnp.bfloat16
    last = early is not None
    parts = tuple(part.shape[1] // HD for part in early) if last else None
    operands = [meta, queries, *pieces]
    scratch = [pltpu.VMEM((2, 2, reach + TILE, HD), bf16)]
    if last:
        operands += [*early, out_weight, acc]
        scratch += [
            pltpu.VMEM((rows, size * HD + sum(part.shape[1] for part in early)), bf16),
            pltpu.VMEM((rows, width), bf16),
            pltpu.SemaphoreType.DMA((-(-width // STRIP),)),
        ]
    return pl.pallas_call(
        functools.partial(attend_kernel, (low, size, len(pieces), place_at, list_at, slots, reach, parts)),
        out_shape=jax.ShapeDtypeStruct((rows, width if last else size * HD), bf16),
        in_specs=[SMEM] + [VMEM] * (len(operands) - 1),
        out_specs=HBM if last else VMEM,
        scratch_shapes=scratch,
        compiler_params=pltpu.CompilerParams(vmem_limit_bytes=VMEM_LIMIT),
        cost_estimate=pl.CostEstimate(flops=0, bytes_accessed=0, transcendentals=0),
    )(*operands)


def project_kernel(spans, *refs):
    parts = refs[: len(spans)]
    w_ref, out_ref, att_buf = refs[len(spans) :]
    for (low, size), ref in zip(spans, parts):
        att_buf[:, low * HD : (low + size) * HD] = ref[...]
    depth = att_buf.shape[1]
    for at in range(0, out_ref.shape[1], STRIP):
        here = slice(at, min(at + STRIP, out_ref.shape[1]))
        out_ref[:, here] = jnp.dot(att_buf[...], w_ref[:depth, here], preferred_element_type=jnp.float32)


def project(spans, results, out_weight):
    rows, width = results[0].shape[0], out_weight.shape[1]
    depth = sum(size for _, size in spans) * HD
    return pl.pallas_call(
        functools.partial(project_kernel, spans),
        out_shape=jax.ShapeDtypeStruct((rows, width), jnp.float32),
        in_specs=[VMEM] * (len(spans) + 1),
        out_specs=VMEM,
        scratch_shapes=[pltpu.VMEM((rows, depth), jnp.bfloat16)],
        compiler_params=pltpu.CompilerParams(vmem_limit_bytes=VMEM_LIMIT),
        cost_estimate=pl.CostEstimate(flops=0, bytes_accessed=0, transcendentals=0),
    )(*results, out_weight)


def after(array, *others):
    return lax.optimization_barrier((array, *others))[0]


def on_device(queries, keys, values, tile_list, counts, out_weight):
    rows, model = queries.shape
    tiles = rows // TILE
    groups, members = lax.axis_size("temporal"), lax.axis_size("ulysses")
    group, member = lax.axis_index("temporal"), lax.axis_index("ulysses")
    total = groups * members
    both = ("temporal", "ulysses")
    hops = -(-REACH // tiles)
    relay = members == 2 and hops == 1
    rim = min(REACH, tiles)
    cuts = [rim, tiles - rim] if relay and tiles > rim else []
    whole_at = [tiles * hops] + [tiles * i for i in range(2 * hops + 1) if i != hops]
    cut_at = [member * (tiles - rim), (1 - member) * rim]
    part_at = []
    if relay:
        whole_at = [tiles, 2 * tiles * (1 - member), 2 * tiles * member]
        part_at = [
            tiles,
            (1 - member) * (3 * tiles - rim),
            (1 - member) * 2 * tiles + member * rim,
            (1 - member) * (tiles - rim) + member * 2 * tiles,
        ]
    first = ((group * members + member) - hops) * tiles
    slots = tile_list.shape[1]
    lists = jnp.concatenate([counts[:, None], tile_list - first], axis=1)
    lists = lax.dynamic_slice_in_dim(lists, member * tiles, tiles, axis=0)
    meta = jnp.concatenate([jnp.stack([jnp.asarray(x, jnp.int32) for x in whole_at + part_at]), lists.reshape(-1)])
    cut_at = jnp.stack([jnp.asarray(x, jnp.int32) for x in cut_at])

    spans, low = [], 0
    for size in split_heads(model // HD):
        spans.append((low, size))
        low += size
    count = len(spans)
    sent = pack(jnp.zeros((2,), jnp.int32), queries, keys, values, spans[:1], [], [], VMEM_WHOLE)
    laid = pack(cut_at, queries, after(keys, *sent), values, spans, spans, cuts, VMEM_LIMIT)
    blocks, heads_of, parts = laid[:count], laid[count : 2 * count], laid[2 * count :]
    sent = [[block] for block in (*sent, *blocks[1:])]
    if parts and count > 1:
        sent[-1] = parts

    onward = [(2 * g, 2 * g + 2) for g in range(groups - 1)]
    onward += [(2 * g + 3, 2 * g + 1) for g in range(groups - 1)]
    near = []
    for i, group_sent in enumerate(sent):
        if relay:
            swap = [(0, 1), (1, 0)]
            near.append([])
            for name, block in zip(("partner", "rest"), group_sent):
                with jax.named_scope(f"{name}_{i}"):
                    near[-1].append(lax.ppermute(block, "ulysses", swap))
        else:
            near.append(
                [
                    lax.ppermute(group_sent[0], both, [(j, j - o) for j in range(total) if 0 <= j - o < total])
                    for o in range(-hops, hops + 1)
                    if o
                ]
            )

    results, acc, ahead = [], None, max(0, count - 1)
    for i in range(count + 1):
        if i < count:
            pieces = [blocks[i], *near[i]]
            if relay:
                gate = near[i][0] if i < 2 else after(near[i][0], results[i - 2])
                with jax.named_scope(f"onward_{i}"):
                    pieces.append(lax.ppermute(gate, both, onward))
        if i >= 1:
            j = i - 1
            own = heads_of[j]
            if j == ahead:
                if ahead:
                    with jax.named_scope("projection"):
                        acc = project(spans[:ahead], results, out_weight)
                    own = after(own, acc)
                else:
                    acc = jnp.zeros((rows, out_weight.shape[1]), jnp.float32)
            early = results[ahead:] if i == count else None
            split = relay and len(sent[j]) > 1
            layout = (len(whole_at) if split else 0, meta.shape[0] - lists.size, slots, len(whole_at) * rows)
            with jax.named_scope(f"attend_{j}"):
                results.append(attend(meta, layout, own, held, spans[j], early, out_weight, acc))
        held = pieces
    return results[-1]


def solution(mesh):
    return jax.shard_map(
        on_device,
        mesh=mesh,
        in_specs=(
            P(("temporal", "ulysses"), None),
            P(("temporal", "ulysses"), None),
            P(("temporal", "ulysses"), None),
            P("temporal", None),
            P("temporal"),
            P(),
        ),
        out_specs=P(("temporal", "ulysses"), None),
        check_vma=False,
    )
```

```python
import functools
import math

import jax
import jax.numpy as jnp
from jax import lax
from jax.experimental import pallas as pl
from jax.experimental.pallas import tpu as pltpu
from jax.sharding import PartitionSpec as P

HD = 128
TILE = 128
REACH = 3
STRIP = 256
HBM = pl.BlockSpec(memory_space=pltpu.HBM)
VMEM = pl.BlockSpec(memory_space=pltpu.VMEM)
SMEM = pl.BlockSpec(memory_space=pltpu.SMEM)
VMEM_LIMIT = 14 * 1024 * 1024
VMEM_WHOLE = 63 * 1024 * 1024


def split_heads(heads):
    sizes = []
    for share in (3 / 12, 3 / 12, 2 / 12, 2 / 12):
        size = min(max(1, round(share * heads)), heads - sum(sizes) - 1)
        if size > 0:
            sizes.append(size)
    return sizes + [heads - sum(sizes)]


def pack_kernel(groups, q_groups, cuts, *refs):
    refs = list(refs)
    cut_ref = refs.pop(0) if cuts else None
    q_ref, k_ref, v_ref = [refs.pop(0) for _ in range(3)]
    outs = [refs.pop(0) for _ in groups]
    q_outs = [refs.pop(0) for _ in q_groups]
    cut_outs = [refs.pop(0) for _ in cuts]
    k_buf, out_buf, q_buf, sems, q_sems, cut_sems = refs
    rows = k_ref.shape[0]
    jobs, q_jobs = [], []
    for out, (low, size) in zip(outs, groups):
        for h in range(size):
            at = len(jobs)
            cols = pl.ds((low + h) * HD, HD)
            jobs.append(
                (
                    pltpu.make_async_copy(k_ref.at[:, cols], k_buf.at[at], sems.at[at, 0]),
                    pltpu.make_async_copy(v_ref.at[:, cols], out_buf.at[at, 1], sems.at[at, 1]),
                    pltpu.make_async_copy(out_buf.at[at], out.at[h], sems.at[at, 2]),
                )
            )
    for out, (low, size) in zip(q_outs, q_groups):
        for h in range(size):
            at = len(q_jobs)
            cols = pl.ds((low + h) * HD, HD)
            q_jobs.append(
                (
                    pltpu.make_async_copy(q_ref.at[:, cols], q_buf.at[at], q_sems.at[at, 0]),
                    pltpu.make_async_copy(q_buf.at[at], out.at[h], q_sems.at[at, 1]),
                )
            )
    for load_k, load_v, _ in jobs:
        load_k.start()
        load_v.start()
    for load, _ in q_jobs:
        load.start()
    for at, (load_k, load_v, store) in enumerate(jobs):
        load_k.wait()
        for tile in range(rows // TILE):
            span = slice(tile * TILE, (tile + 1) * TILE)
            out_buf[at, 0, span] = k_buf[at, span].T
        load_v.wait()
        store.start()
    cut_jobs = []
    if cuts:
        size = groups[-1][1]
        for h in range(size):
            for i, (extent, out) in enumerate(zip(cuts, cut_outs)):
                part = pl.ds(pl.multiple_of(cut_ref[i] * TILE, TILE), extent * TILE)
                source = out_buf.at[len(jobs) - size + h, :, part]
                cut_jobs.append(pltpu.make_async_copy(source, out.at[h], cut_sems.at[h, i]))
                cut_jobs[-1].start()
    for load, store in q_jobs:
        load.wait()
        store.start()
    for _, _, store in jobs:
        store.wait()
    for _, store in q_jobs:
        store.wait()
    for store in cut_jobs:
        store.wait()


def pack(cut_at, queries, keys, values, groups, q_groups, cuts, limit):
    rows = keys.shape[0]
    heads = sum(size for _, size in groups)
    q_heads = sum(size for _, size in q_groups)
    last = groups[-1][1]
    shapes = [(size, 2, rows, HD) for _, size in groups] + [(size, rows, HD) for _, size in q_groups]
    shapes += [(last, 2, extent * TILE, HD) for extent in cuts]
    return pl.pallas_call(
        functools.partial(pack_kernel, groups, q_groups, cuts),
        out_shape=[jax.ShapeDtypeStruct(shape, keys.dtype) for shape in shapes],
        in_specs=[SMEM] * bool(cuts) + [HBM] * 3,
        out_specs=[HBM] * len(shapes),
        scratch_shapes=[
            pltpu.VMEM((heads, rows, HD), keys.dtype),
            pltpu.VMEM((heads, 2, rows, HD), keys.dtype),
            pltpu.VMEM((max(q_heads, 1), rows, HD), keys.dtype),
            pltpu.SemaphoreType.DMA((heads, 3)),
            pltpu.SemaphoreType.DMA((max(q_heads, 1), 2)),
            pltpu.SemaphoreType.DMA((last, max(len(cuts), 1))),
        ],
        compiler_params=pltpu.CompilerParams(vmem_limit_bytes=limit),
        cost_estimate=pl.CostEstimate(flops=0, bytes_accessed=8 * rows * heads * HD, transcendentals=0),
    )(*([cut_at] if cuts else []), queries, keys, values)


def attend_kernel(cfg, meta, q_ref, *refs):
    low, size, pieces, place_at, list_at, slots, spans, early, has_acc, final = cfg
    refs = list(refs)
    piece_refs = [refs.pop(0) for _ in range(pieces)]
    early_refs = [refs.pop(0) for _ in early or ()]
    w_ref = None if early is None else refs.pop(0)
    acc_ref = refs.pop(0) if has_acc else None
    out_ref, kv_buf = refs[:2]
    rows = q_ref.shape[1]
    tiles = rows // TILE
    att_buf, lead = out_ref, 0
    if early is not None:
        att_buf = refs[2]
        for extent, ref in zip(early, early_refs):
            att_buf[:, lead * HD : (lead + extent) * HD] = ref[...]
            lead += extent

    scale = math.log2(math.e) / math.sqrt(HD)
    zeros = jnp.zeros((TILE, HD), jnp.bfloat16)
    places, v_places, ones = [], [], []
    for tile in range(tiles):
        row = list_at + tile * (slots + 1)
        live = meta[row]
        at = [pl.multiple_of(meta[row + 1 + j] * TILE, TILE) for j in range(slots)]
        places.append(at)
        v_places.append([pl.multiple_of(jnp.where(j < live, at[j], spans), TILE) for j in range(slots)])
        ones.append([zeros + jnp.where(j < live, 1.0, 0.0).astype(jnp.bfloat16) for j in range(slots)])

    def scores(h, tile):
        k = jnp.concatenate([kv_buf[h % 2, 0, pl.ds(p, TILE)] for p in places[tile]], axis=1)
        q = q_ref[h, tile * TILE : (tile + 1) * TILE]
        return jnp.dot(q, k, preferred_element_type=jnp.float32)

    def finish(h, tile, s):
        top = jnp.max(s, axis=1, keepdims=True)
        p = jnp.exp2((s - top) * scale).astype(jnp.bfloat16)
        v = jnp.concatenate(
            [
                jnp.concatenate([kv_buf[h % 2, 1, pl.ds(at, TILE)], one], axis=1)
                for at, one in zip(v_places[tile], ones[tile])
            ],
            axis=0,
        )
        mixed = jnp.dot(p, v, preferred_element_type=jnp.float32)
        here = slice(tile * TILE, (tile + 1) * TILE)
        att_buf[here, (lead + h) * HD : (lead + h + 1) * HD] = (mixed[:, :HD] / mixed[:, HD:]).astype(jnp.bfloat16)

    def ready(h):
        for i, ref in enumerate(piece_refs):
            place = pl.ds(pl.multiple_of(meta[place_at + i] * TILE, TILE), ref.shape[2])
            for part in range(2):
                kv_buf[h % 2, part, place] = ref[h, part]
        kv_buf[h % 2, 1, spans : spans + TILE] = zeros

    jobs = [(h, tile) for h in range(size) for tile in range(tiles)]
    ready(0)
    ahead = scores(*jobs[0])
    for i, (h, tile) in enumerate(jobs):
        now = ahead
        if i + 1 < len(jobs):
            if jobs[i + 1][0] != h:
                ready(h + 1)
            ahead = scores(*jobs[i + 1])
        finish(h, tile, now)

    if early is None:
        return
    stores = []
    out_buf, out_sems = refs[3:] if final else (out_ref, None)
    for i, at in enumerate(range(0, out_buf.shape[1], STRIP)):
        here = slice(at, min(at + STRIP, out_buf.shape[1]))
        weights = w_ref[(low - lead) * HD : (low + size) * HD, here]
        part = jnp.dot(att_buf[...], weights, preferred_element_type=jnp.float32)
        if has_acc:
            part = part + acc_ref[:, here]
        out_buf[:, here] = part.astype(out_buf.dtype)
        if final:
            cols = pl.ds(at, here.stop - at)
            stores.append(pltpu.make_async_copy(out_buf.at[:, cols], out_ref.at[:, cols], out_sems.at[i]))
            stores[-1].start()
    for copy in stores:
        copy.wait()


def attend(meta, layout, queries, pieces, span, early, out_weight, acc, final):
    rows = queries.shape[1]
    low, size = span
    place_at, list_at, slots, reach = layout
    width = out_weight.shape[1]
    bf16 = jnp.bfloat16
    operands = [meta, queries, *pieces]
    scratch = [pltpu.VMEM((2, 2, reach + TILE, HD), bf16)]
    parts = None
    out_shape = jax.ShapeDtypeStruct((rows, size * HD), bf16)
    if early is not None:
        parts = tuple(part.shape[1] // HD for part in early)
        operands += [*early, out_weight]
        if acc is not None:
            operands.append(acc)
        scratch.append(pltpu.VMEM((rows, (size + sum(parts)) * HD), bf16))
        out_shape = jax.ShapeDtypeStruct((rows, width), bf16 if final else jnp.float32)
        if final:
            scratch += [pltpu.VMEM((rows, width), bf16), pltpu.SemaphoreType.DMA((-(-width // STRIP),))]
    return pl.pallas_call(
        functools.partial(
            attend_kernel, (low, size, len(pieces), place_at, list_at, slots, reach, parts, acc is not None, final)
        ),
        out_shape=out_shape,
        in_specs=[SMEM] + [VMEM] * (len(operands) - 1),
        out_specs=HBM if final else VMEM,
        scratch_shapes=scratch,
        compiler_params=pltpu.CompilerParams(vmem_limit_bytes=VMEM_LIMIT),
        cost_estimate=pl.CostEstimate(flops=0, bytes_accessed=0, transcendentals=0),
    )(*operands)


def after(array, *others):
    return lax.optimization_barrier((array, *others))[0]


def on_device(queries, keys, values, tile_list, counts, out_weight):
    rows, model = queries.shape
    tiles = rows // TILE
    groups, members = lax.axis_size("temporal"), lax.axis_size("ulysses")
    group, member = lax.axis_index("temporal"), lax.axis_index("ulysses")
    total = groups * members
    both = ("temporal", "ulysses")
    hops = -(-REACH // tiles)
    relay = members == 2 and hops == 1
    rim = min(REACH, tiles)
    cuts = [rim, tiles - rim] if relay and tiles > rim else []
    whole_at = [tiles * hops] + [tiles * i for i in range(2 * hops + 1) if i != hops]
    cut_at = [member * (tiles - rim), (1 - member) * rim]
    part_at = []
    if relay:
        whole_at = [tiles, 2 * tiles * (1 - member), 2 * tiles * member]
        part_at = [
            tiles,
            (1 - member) * (3 * tiles - rim),
            (1 - member) * 2 * tiles + member * rim,
            (1 - member) * (tiles - rim) + member * 2 * tiles,
        ]
    first = ((group * members + member) - hops) * tiles
    slots = tile_list.shape[1]
    lists = jnp.concatenate([counts[:, None], tile_list - first], axis=1)
    lists = lax.dynamic_slice_in_dim(lists, member * tiles, tiles, axis=0)
    meta = jnp.concatenate([jnp.stack([jnp.asarray(x, jnp.int32) for x in whole_at + part_at]), lists.reshape(-1)])
    cut_at = jnp.stack([jnp.asarray(x, jnp.int32) for x in cut_at])

    spans, low = [], 0
    for size in split_heads(model // HD):
        spans.append((low, size))
        low += size
    count = len(spans)
    sent = pack(None, queries, keys, values, spans[:1], [], [], VMEM_WHOLE)
    laid = pack(cut_at, queries, after(keys, *sent), values, spans, spans, cuts, VMEM_LIMIT)
    blocks, heads_of, parts = laid[:count], laid[count : 2 * count], laid[2 * count :]
    sent = [[block] for block in (*sent, *blocks[1:])]
    if parts and count > 1:
        sent[-1] = parts

    onward = [(2 * g, 2 * g + 2) for g in range(groups - 1)]
    onward += [(2 * g + 3, 2 * g + 1) for g in range(groups - 1)]
    near = []
    for i, group_sent in enumerate(sent):
        if relay:
            swap = [(0, 1), (1, 0)]
            near.append([])
            for name, block in zip(("partner", "rest"), group_sent):
                with jax.named_scope(f"{name}_{i}"):
                    near[-1].append(lax.ppermute(block, "ulysses", swap))
        else:
            near.append(
                [
                    lax.ppermute(group_sent[0], both, [(j, j - o) for j in range(total) if 0 <= j - o < total])
                    for o in range(-hops, hops + 1)
                    if o
                ]
            )

    results, acc, mid = [], None, count - 3
    for i in range(count + 1):
        if i < count:
            pieces = [blocks[i], *near[i]]
            if relay:
                gate = near[i][0] if i < 2 else after(near[i][0], results[i - 2])
                with jax.named_scope(f"onward_{i}"):
                    pieces.append(lax.ppermute(gate, both, onward))
        if i >= 1:
            j = i - 1
            final = i == count
            early = None
            if final:
                early = results[max(mid + 1, 0) :]
            elif j == mid:
                early = results[:]
            split = relay and len(sent[j]) > 1
            layout = (len(whole_at) if split else 0, meta.shape[0] - lists.size, slots, len(whole_at) * rows)
            with jax.named_scope(f"attend_{j}"):
                result = attend(meta, layout, heads_of[j], held, spans[j], early, out_weight, acc if final else None, final)
            results.append(result)
            if j == mid:
                acc = result
        held = pieces
    return results[-1]


def solution(mesh):
    return jax.shard_map(
        on_device,
        mesh=mesh,
        in_specs=(
            P(("temporal", "ulysses"), None),
            P(("temporal", "ulysses"), None),
            P(("temporal", "ulysses"), None),
            P("temporal", None),
            P("temporal"),
            P(),
        ),
        out_specs=P(("temporal", "ulysses"), None),
        check_vma=False,
    )
```

```python
import functools
import math

import jax
import jax.numpy as jnp
from jax import lax
from jax.experimental import pallas as pl
from jax.experimental.pallas import tpu as pltpu
from jax.sharding import PartitionSpec as P

HD = 128
TILE = 128
REACH = 3
STRIP = 256
HBM = pl.BlockSpec(memory_space=pltpu.HBM)
VMEM = pl.BlockSpec(memory_space=pltpu.VMEM)
SMEM = pl.BlockSpec(memory_space=pltpu.SMEM)
VMEM_LIMIT = 14 * 1024 * 1024
VMEM_WHOLE = 63 * 1024 * 1024


def split_heads(heads):
    sizes = []
    for share in (4 / 12, 3 / 12, 2 / 12, 2 / 12):
        size = min(max(1, round(share * heads)), heads - sum(sizes) - 1)
        if size > 0:
            sizes.append(size)
    return sizes + [heads - sum(sizes)]


def pack_kernel(groups, q_groups, cuts, *refs):
    refs = list(refs)
    cut_ref = refs.pop(0) if cuts else None
    q_ref, k_ref, v_ref = [refs.pop(0) for _ in range(3)]
    outs = [refs.pop(0) for _ in groups]
    q_outs = [refs.pop(0) for _ in q_groups]
    cut_outs = [refs.pop(0) for _ in cuts]
    k_buf, out_buf, q_buf, sems, q_sems, cut_sems = refs
    rows = k_ref.shape[0]
    jobs, q_jobs = [], []
    for out, (low, size) in zip(outs, groups):
        for h in range(size):
            at = len(jobs)
            cols = pl.ds((low + h) * HD, HD)
            jobs.append(
                (
                    pltpu.make_async_copy(k_ref.at[:, cols], k_buf.at[at], sems.at[at, 0]),
                    pltpu.make_async_copy(v_ref.at[:, cols], out_buf.at[at, 1], sems.at[at, 1]),
                    pltpu.make_async_copy(out_buf.at[at], out.at[h], sems.at[at, 2]),
                )
            )
    for out, (low, size) in zip(q_outs, q_groups):
        for h in range(size):
            at = len(q_jobs)
            cols = pl.ds((low + h) * HD, HD)
            q_jobs.append(
                (
                    pltpu.make_async_copy(q_ref.at[:, cols], q_buf.at[at], q_sems.at[at, 0]),
                    pltpu.make_async_copy(q_buf.at[at], out.at[h], q_sems.at[at, 1]),
                )
            )
    for load_k, load_v, _ in jobs:
        load_k.start()
        load_v.start()
    for load, _ in q_jobs:
        load.start()
    for at, (load_k, load_v, store) in enumerate(jobs):
        load_k.wait()
        for tile in range(rows // TILE):
            span = slice(tile * TILE, (tile + 1) * TILE)
            out_buf[at, 0, span] = k_buf[at, span].T
        load_v.wait()
        store.start()
    cut_jobs = []
    for (start, size, which, extent), out in zip(cuts, cut_outs):
        part = pl.ds(pl.multiple_of(cut_ref[which] * TILE, TILE), extent * TILE)
        for h in range(size):
            source = out_buf.at[start - groups[0][0] + h, :, part]
            cut_jobs.append(pltpu.make_async_copy(source, out.at[h], cut_sems.at[len(cut_jobs)]))
            cut_jobs[-1].start()
    for load, store in q_jobs:
        load.wait()
        store.start()
    for _, _, store in jobs:
        store.wait()
    for _, store in q_jobs:
        store.wait()
    for store in cut_jobs:
        store.wait()


def pack(cut_at, queries, keys, values, groups, q_groups, cuts, limit):
    rows = keys.shape[0]
    heads = sum(size for _, size in groups)
    q_heads = sum(size for _, size in q_groups)
    shapes = [(size, 2, rows, HD) for _, size in groups] + [(size, rows, HD) for _, size in q_groups]
    shapes += [(size, 2, extent * TILE, HD) for _, size, _, extent in cuts]
    return pl.pallas_call(
        functools.partial(pack_kernel, groups, q_groups, cuts),
        out_shape=[jax.ShapeDtypeStruct(shape, keys.dtype) for shape in shapes],
        in_specs=[SMEM] * bool(cuts) + [HBM] * 3,
        out_specs=[HBM] * len(shapes),
        scratch_shapes=[
            pltpu.VMEM((heads, rows, HD), keys.dtype),
            pltpu.VMEM((heads, 2, rows, HD), keys.dtype),
            pltpu.VMEM((max(q_heads, 1), rows, HD), keys.dtype),
            pltpu.SemaphoreType.DMA((heads, 3)),
            pltpu.SemaphoreType.DMA((max(q_heads, 1), 2)),
            pltpu.SemaphoreType.DMA((max(sum(size for _, size, _, _ in cuts), 1),)),
        ],
        compiler_params=pltpu.CompilerParams(vmem_limit_bytes=limit),
        cost_estimate=pl.CostEstimate(flops=0, bytes_accessed=8 * rows * heads * HD, transcendentals=0),
    )(*([cut_at] if cuts else []), queries, keys, values)


def attend_kernel(cfg, meta, q_ref, *refs):
    low, size, shifts, place_at, list_at, slots, spans, early, has_acc, final = cfg
    refs = list(refs)
    piece_refs = [refs.pop(0) for _ in shifts]
    early_refs = [refs.pop(0) for _ in early or ()]
    w_ref = None if early is None else refs.pop(0)
    acc_ref = refs.pop(0) if has_acc else None
    out_ref, kv_buf = refs[:2]
    rows = q_ref.shape[1]
    tiles = rows // TILE
    att_buf, lead = out_ref, 0
    if early is not None:
        att_buf = refs[2]
        for extent, ref in zip(early, early_refs):
            att_buf[:, lead * HD : (lead + extent) * HD] = ref[...]
            lead += extent

    scale = math.log2(math.e) / math.sqrt(HD)
    zeros = jnp.zeros((TILE, HD), jnp.bfloat16)
    places, v_places, ones = [], [], []
    for tile in range(tiles):
        row = list_at + tile * (slots + 1)
        live = meta[row]
        at = [pl.multiple_of(meta[row + 1 + j] * TILE, TILE) for j in range(slots)]
        places.append(at)
        v_places.append([pl.multiple_of(jnp.where(j < live, at[j], spans), TILE) for j in range(slots)])
        ones.append([zeros + jnp.where(j < live, 1.0, 0.0).astype(jnp.bfloat16) for j in range(slots)])

    def scores(h, tile):
        k = jnp.concatenate([kv_buf[h % 2, 0, pl.ds(p, TILE)] for p in places[tile]], axis=1)
        q = q_ref[h, tile * TILE : (tile + 1) * TILE]
        return jnp.dot(q, k, preferred_element_type=jnp.float32)

    def finish(h, tile, s):
        top = jnp.max(s, axis=1, keepdims=True)
        p = jnp.exp2((s - top) * scale).astype(jnp.bfloat16)
        v = jnp.concatenate(
            [
                jnp.concatenate([kv_buf[h % 2, 1, pl.ds(at, TILE)], one], axis=1)
                for at, one in zip(v_places[tile], ones[tile])
            ],
            axis=0,
        )
        mixed = jnp.dot(p, v, preferred_element_type=jnp.float32)
        here = slice(tile * TILE, (tile + 1) * TILE)
        att_buf[here, (lead + h) * HD : (lead + h + 1) * HD] = (mixed[:, :HD] / mixed[:, HD:]).astype(jnp.bfloat16)

    def ready(h):
        for i, ref in enumerate(piece_refs):
            place = pl.ds(pl.multiple_of(meta[place_at + i] * TILE, TILE), ref.shape[2])
            for part in range(2):
                kv_buf[h % 2, part, place] = ref[h + shifts[i], part]
        kv_buf[h % 2, 1, spans : spans + TILE] = zeros

    jobs = [(h, tile) for h in range(size) for tile in range(tiles)]
    ready(0)
    ahead = scores(*jobs[0])
    for i, (h, tile) in enumerate(jobs):
        now = ahead
        if i + 1 < len(jobs):
            if jobs[i + 1][0] != h:
                ready(h + 1)
            ahead = scores(*jobs[i + 1])
        finish(h, tile, now)

    if early is None:
        return
    stores = []
    out_buf, out_sems = refs[3:] if final else (out_ref, None)
    for i, at in enumerate(range(0, out_buf.shape[1], STRIP)):
        here = slice(at, min(at + STRIP, out_buf.shape[1]))
        weights = w_ref[(low - lead) * HD : (low + size) * HD, here]
        part = jnp.dot(att_buf[...], weights, preferred_element_type=jnp.float32)
        if has_acc:
            part = part + acc_ref[:, here]
        out_buf[:, here] = part.astype(out_buf.dtype)
        if final:
            cols = pl.ds(at, here.stop - at)
            stores.append(pltpu.make_async_copy(out_buf.at[:, cols], out_ref.at[:, cols], out_sems.at[i]))
            stores[-1].start()
    for copy in stores:
        copy.wait()


def attend(meta, layout, queries, pieces, shifts, span, early, out_weight, acc, final):
    rows = queries.shape[1]
    low, size = span
    place_at, list_at, slots, reach = layout
    width = out_weight.shape[1]
    bf16 = jnp.bfloat16
    operands = [meta, queries, *pieces]
    scratch = [pltpu.VMEM((2, 2, reach + TILE, HD), bf16)]
    parts = None
    out_shape = jax.ShapeDtypeStruct((rows, size * HD), bf16)
    if early is not None:
        parts = tuple(part.shape[1] // HD for part in early)
        operands += [*early, out_weight]
        if acc is not None:
            operands.append(acc)
        scratch.append(pltpu.VMEM((rows, (size + sum(parts)) * HD), bf16))
        out_shape = jax.ShapeDtypeStruct((rows, width), bf16 if final else jnp.float32)
        if final:
            scratch += [pltpu.VMEM((rows, width), bf16), pltpu.SemaphoreType.DMA((-(-width // STRIP),))]
    return pl.pallas_call(
        functools.partial(
            attend_kernel, (low, size, shifts, place_at, list_at, slots, reach, parts, acc is not None, final)
        ),
        out_shape=out_shape,
        in_specs=[SMEM] + [VMEM] * (len(operands) - 1),
        out_specs=HBM if final else VMEM,
        scratch_shapes=scratch,
        compiler_params=pltpu.CompilerParams(vmem_limit_bytes=VMEM_LIMIT),
        cost_estimate=pl.CostEstimate(flops=0, bytes_accessed=0, transcendentals=0),
    )(*operands)


def after(array, *others):
    return lax.optimization_barrier((array, *others))[0]


def on_device(queries, keys, values, tile_list, counts, out_weight):
    rows, model = queries.shape
    tiles = rows // TILE
    groups, members = lax.axis_size("temporal"), lax.axis_size("ulysses")
    group, member = lax.axis_index("temporal"), lax.axis_index("ulysses")
    total = groups * members
    both = ("temporal", "ulysses")
    hops = -(-REACH // tiles)
    relay = members == 2 and hops == 1
    rim = min(REACH, tiles)
    whole_at = [tiles * hops] + [tiles * i for i in range(2 * hops + 1) if i != hops]
    cut_at = [member * (tiles - rim), (1 - member) * rim]
    part_at = []
    if relay:
        whole_at = [tiles, 2 * tiles * (1 - member), 2 * tiles * member]
        part_at = [
            tiles,
            (1 - member) * (3 * tiles - rim),
            (1 - member) * 2 * tiles + member * rim,
            (1 - member) * (tiles - rim) + member * 2 * tiles,
        ]
    first = ((group * members + member) - hops) * tiles
    slots = tile_list.shape[1]
    lists = jnp.concatenate([counts[:, None], tile_list - first], axis=1)
    lists = lax.dynamic_slice_in_dim(lists, member * tiles, tiles, axis=0)
    meta = jnp.concatenate([jnp.stack([jnp.asarray(x, jnp.int32) for x in whole_at + part_at]), lists.reshape(-1)])
    cut_at = jnp.stack([jnp.asarray(x, jnp.int32) for x in cut_at])

    spans, low = [], 0
    for size in split_heads(model // HD):
        spans.append((low, size))
        low += size
    count = len(spans)
    sent = pack(None, queries, keys, values, spans[:1], [], [], VMEM_WHOLE)
    split = max(1, count - 2) if relay and tiles > rim else count
    cuts = [(low, size, 0, rim) for low, size in spans[split:]]
    if cuts:
        rest_low = spans[split][0]
        cuts.append((rest_low, model // HD - rest_low, 1, tiles - rim))
    laid = pack(cut_at, queries, after(keys, *sent), values, spans, spans, cuts, VMEM_LIMIT)
    blocks, heads_of, parts = laid[:count], laid[count : 2 * count], laid[2 * count :]
    sent = [*sent, *blocks[1:split], *parts]

    onward = [(2 * g, 2 * g + 2) for g in range(groups - 1)]
    onward += [(2 * g + 3, 2 * g + 1) for g in range(groups - 1)]
    near = []
    for i, block in enumerate(sent):
        if relay:
            with jax.named_scope(f"partner_{i}" if i < count else f"rest_{i}"):
                near.append([lax.ppermute(block, "ulysses", [(0, 1), (1, 0)])])
        else:
            near.append(
                [
                    lax.ppermute(block, both, [(j, j - o) for j in range(total) if 0 <= j - o < total])
                    for o in range(-hops, hops + 1)
                    if o
                ]
            )

    results, acc, mid = [], None, count - 3
    for i in range(count + 1):
        if i < count:
            pieces = [blocks[i], *near[i]]
            shifts = [0] * len(pieces)
            if i >= split:
                pieces += near[count]
                shifts.append(spans[i][0] - rest_low)
            if relay:
                gate = near[i][0] if i < 2 else after(near[i][0], results[i - 2])
                with jax.named_scope(f"onward_{i}"):
                    pieces.append(lax.ppermute(gate, both, onward))
                shifts.append(0)
        if i >= 1:
            j = i - 1
            final = i == count
            early = None
            if final:
                early = results[max(mid + 1, 0) :]
            elif j == mid:
                early = results[:]
            layout = (len(whole_at) if j >= split else 0, meta.shape[0] - lists.size, slots, len(whole_at) * rows)
            with jax.named_scope(f"attend_{j}"):
                result = attend(meta, layout, heads_of[j], *held, spans[j], early, out_weight, acc if final else None, final)
            results.append(result)
            if j == mid:
                acc = result
        held = pieces, tuple(shifts)
    return results[-1]


def solution(mesh):
    return jax.shard_map(
        on_device,
        mesh=mesh,
        in_specs=(
            P(("temporal", "ulysses"), None),
            P(("temporal", "ulysses"), None),
            P(("temporal", "ulysses"), None),
            P("temporal", None),
            P("temporal"),
            P(),
        ),
        out_specs=P(("temporal", "ulysses"), None),
        check_vma=False,
    )
```

```python
import functools
import math

import jax
import jax.numpy as jnp
from jax import lax
from jax.experimental import pallas as pl
from jax.experimental.pallas import tpu as pltpu
from jax.sharding import PartitionSpec as P

HD = 128
TILE = 128
REACH = 3
STRIP = 256
HBM = pl.BlockSpec(memory_space=pltpu.HBM)
VMEM = pl.BlockSpec(memory_space=pltpu.VMEM)
SMEM = pl.BlockSpec(memory_space=pltpu.SMEM)
VMEM_LIMIT = 14 * 1024 * 1024
VMEM_WHOLE = 63 * 1024 * 1024


def split_heads(heads):
    sizes = []
    for share in (3 / 12, 3 / 12, 2 / 12, 2 / 12):
        size = min(max(1, round(share * heads)), heads - sum(sizes) - 1)
        if size > 0:
            sizes.append(size)
    return sizes + [heads - sum(sizes)]


def cut_spots(tiles, rim):
    member = lax.axis_index("ulysses")
    return [member * (tiles - rim), (1 - member) * rim]


def piece_spots(tiles, hops, rim, relay, parted):
    if not relay:
        return [tiles * hops] + [tiles * i for i in range(2 * hops + 1) if i != hops]
    member = lax.axis_index("ulysses")
    if not parted:
        return [tiles, 2 * tiles * (1 - member), 2 * tiles * member]
    return [
        tiles,
        (1 - member) * (3 * tiles - rim),
        (1 - member) * 2 * tiles + member * rim,
        (1 - member) * (tiles - rim) + member * 2 * tiles,
    ]


def pack_kernel(groups, q_groups, cuts, *refs):
    refs = list(refs)
    q_ref, k_ref, v_ref = [refs.pop(0) for _ in range(3)]
    outs = [refs.pop(0) for _ in groups]
    q_outs = [refs.pop(0) for _ in q_groups]
    cut_outs = [refs.pop(0) for _ in cuts]
    k_buf, out_buf, q_buf, sems, q_sems, cut_sems = refs
    rows = k_ref.shape[0]
    jobs, q_jobs = [], []
    for out, (low, size) in zip(outs, groups):
        for h in range(size):
            at = len(jobs)
            cols = pl.ds((low + h) * HD, HD)
            jobs.append(
                (
                    pltpu.make_async_copy(k_ref.at[:, cols], k_buf.at[at], sems.at[at, 0]),
                    pltpu.make_async_copy(v_ref.at[:, cols], out_buf.at[at, 1], sems.at[at, 1]),
                    pltpu.make_async_copy(out_buf.at[at], out.at[h], sems.at[at, 2]),
                )
            )
    for out, (low, size) in zip(q_outs, q_groups):
        for h in range(size):
            at = len(q_jobs)
            cols = pl.ds((low + h) * HD, HD)
            q_jobs.append(
                (
                    pltpu.make_async_copy(q_ref.at[:, cols], q_buf.at[at], q_sems.at[at, 0]),
                    pltpu.make_async_copy(q_buf.at[at], out.at[h], q_sems.at[at, 1]),
                )
            )
    for load_k, load_v, _ in jobs:
        load_k.start()
        load_v.start()
    for load, _ in q_jobs:
        load.start()
    for at, (load_k, load_v, store) in enumerate(jobs):
        load_k.wait()
        for tile in range(rows // TILE):
            span = slice(tile * TILE, (tile + 1) * TILE)
            out_buf[at, 0, span] = k_buf[at, span].T
        load_v.wait()
        store.start()
    cut_jobs = []
    if cuts:
        size = groups[-1][1]
        spots = cut_spots(rows // TILE, cuts[0])
        for h in range(size):
            for i, (extent, out) in enumerate(zip(cuts, cut_outs)):
                part = pl.ds(pl.multiple_of(spots[i] * TILE, TILE), extent * TILE)
                source = out_buf.at[len(jobs) - size + h, :, part]
                cut_jobs.append(pltpu.make_async_copy(source, out.at[h], cut_sems.at[h, i]))
                cut_jobs[-1].start()
    for load, store in q_jobs:
        load.wait()
        store.start()
    for _, _, store in jobs:
        store.wait()
    for _, store in q_jobs:
        store.wait()
    for store in cut_jobs:
        store.wait()


def pack(queries, keys, values, groups, q_groups, cuts, limit):
    rows = keys.shape[0]
    heads = sum(size for _, size in groups)
    q_heads = sum(size for _, size in q_groups)
    last = groups[-1][1]
    shapes = [(size, 2, rows, HD) for _, size in groups] + [(size, rows, HD) for _, size in q_groups]
    shapes += [(last, 2, extent * TILE, HD) for extent in cuts]
    return pl.pallas_call(
        functools.partial(pack_kernel, groups, q_groups, cuts),
        out_shape=[jax.ShapeDtypeStruct(shape, keys.dtype) for shape in shapes],
        in_specs=[HBM] * 3,
        out_specs=[HBM] * len(shapes),
        scratch_shapes=[
            pltpu.VMEM((heads, rows, HD), keys.dtype),
            pltpu.VMEM((heads, 2, rows, HD), keys.dtype),
            pltpu.VMEM((max(q_heads, 1), rows, HD), keys.dtype),
            pltpu.SemaphoreType.DMA((heads, 3)),
            pltpu.SemaphoreType.DMA((max(q_heads, 1), 2)),
            pltpu.SemaphoreType.DMA((last, max(len(cuts), 1))),
        ],
        compiler_params=pltpu.CompilerParams(vmem_limit_bytes=limit),
        cost_estimate=pl.CostEstimate(flops=0, bytes_accessed=8 * rows * heads * HD, transcendentals=0),
    )(queries, keys, values)


def attend_kernel(cfg, tiles_ref, counts_ref, q_ref, *refs):
    low, size, pieces, (hops, rim, relay, parted), early, has_acc, final = cfg
    refs = list(refs)
    piece_refs = [refs.pop(0) for _ in range(pieces)]
    early_refs = [refs.pop(0) for _ in early or ()]
    w_ref = None if early is None else refs.pop(0)
    acc_ref = refs.pop(0) if has_acc else None
    out_ref, kv_buf = refs[:2]
    rows = q_ref.shape[1]
    tiles = rows // TILE
    slots = tiles_ref.shape[1]
    spans = (2 * hops + 1) * rows
    spots = piece_spots(tiles, hops, rim, relay, parted)
    member, members = lax.axis_index("ulysses"), lax.axis_size("ulysses")
    first = (lax.axis_index("temporal") * members + member - hops) * tiles
    att_buf, lead = out_ref, 0
    if early is not None:
        att_buf = refs[2]
        for extent, ref in zip(early, early_refs):
            att_buf[:, lead * HD : (lead + extent) * HD] = ref[...]
            lead += extent

    scale = math.log2(math.e) / math.sqrt(HD)
    zeros = jnp.zeros((TILE, HD), jnp.bfloat16)
    places, v_places, ones = [], [], []
    for tile in range(tiles):
        row = member * tiles + tile
        live = counts_ref[row]
        at = [pl.multiple_of((tiles_ref[row, j] - first) * TILE, TILE) for j in range(slots)]
        places.append(at)
        v_places.append([pl.multiple_of(jnp.where(j < live, at[j], spans), TILE) for j in range(slots)])
        ones.append([zeros + jnp.where(j < live, 1.0, 0.0).astype(jnp.bfloat16) for j in range(slots)])

    def scores(h, tile):
        k = jnp.concatenate([kv_buf[h % 2, 0, pl.ds(p, TILE)] for p in places[tile]], axis=1)
        q = q_ref[h, tile * TILE : (tile + 1) * TILE]
        return jnp.dot(q, k, preferred_element_type=jnp.float32)

    def finish(h, tile, s):
        top = jnp.max(s, axis=1, keepdims=True)
        p = jnp.exp2((s - top) * scale).astype(jnp.bfloat16)
        v = jnp.concatenate(
            [
                jnp.concatenate([kv_buf[h % 2, 1, pl.ds(at, TILE)], one], axis=1)
                for at, one in zip(v_places[tile], ones[tile])
            ],
            axis=0,
        )
        mixed = jnp.dot(p, v, preferred_element_type=jnp.float32)
        here = slice(tile * TILE, (tile + 1) * TILE)
        att_buf[here, (lead + h) * HD : (lead + h + 1) * HD] = (mixed[:, :HD] / mixed[:, HD:]).astype(jnp.bfloat16)

    def ready(h):
        for i, ref in enumerate(piece_refs):
            place = pl.ds(pl.multiple_of(spots[i] * TILE, TILE), ref.shape[2])
            for part in range(2):
                kv_buf[h % 2, part, place] = ref[h, part]
        kv_buf[h % 2, 1, spans : spans + TILE] = zeros

    jobs = [(h, tile) for h in range(size) for tile in range(tiles)]
    ready(0)
    ahead = scores(*jobs[0])
    for i, (h, tile) in enumerate(jobs):
        now = ahead
        if i + 1 < len(jobs):
            if jobs[i + 1][0] != h:
                ready(h + 1)
            ahead = scores(*jobs[i + 1])
        finish(h, tile, now)

    if early is None:
        return
    stores = []
    out_buf, out_sems = refs[3:] if final else (out_ref, None)
    for i, at in enumerate(range(0, out_buf.shape[1], STRIP)):
        here = slice(at, min(at + STRIP, out_buf.shape[1]))
        weights = w_ref[(low - lead) * HD : (low + size) * HD, here]
        part = jnp.dot(att_buf[...], weights, preferred_element_type=jnp.float32)
        if has_acc:
            part = part + acc_ref[:, here]
        out_buf[:, here] = part.astype(out_buf.dtype)
        if final:
            cols = pl.ds(at, here.stop - at)
            stores.append(pltpu.make_async_copy(out_buf.at[:, cols], out_ref.at[:, cols], out_sems.at[i]))
            stores[-1].start()
    for copy in stores:
        copy.wait()


def attend(tile_list, counts, layout, queries, pieces, span, early, out_weight, acc, final):
    rows = queries.shape[1]
    low, size = span
    reach = (2 * layout[0] + 1) * rows
    width = out_weight.shape[1]
    bf16 = jnp.bfloat16
    operands = [tile_list, counts, queries, *pieces]
    scratch = [pltpu.VMEM((2, 2, reach + TILE, HD), bf16)]
    parts = None
    out_shape = jax.ShapeDtypeStruct((rows, size * HD), bf16)
    if early is not None:
        parts = tuple(part.shape[1] // HD for part in early)
        operands += [*early, out_weight]
        if acc is not None:
            operands.append(acc)
        scratch.append(pltpu.VMEM((rows, (size + sum(parts)) * HD), bf16))
        out_shape = jax.ShapeDtypeStruct((rows, width), bf16 if final else jnp.float32)
        if final:
            scratch += [pltpu.VMEM((rows, width), bf16), pltpu.SemaphoreType.DMA((-(-width // STRIP),))]
    return pl.pallas_call(
        functools.partial(
            attend_kernel, (low, size, len(pieces), layout, parts, acc is not None, final)
        ),
        out_shape=out_shape,
        in_specs=[SMEM] * 2 + [VMEM] * (len(operands) - 2),
        out_specs=HBM if final else VMEM,
        scratch_shapes=scratch,
        compiler_params=pltpu.CompilerParams(vmem_limit_bytes=VMEM_LIMIT),
        cost_estimate=pl.CostEstimate(flops=0, bytes_accessed=0, transcendentals=0),
    )(*operands)


def after(array, *others):
    return lax.optimization_barrier((array, *others))[0]


def on_device(queries, keys, values, tile_list, counts, out_weight):
    rows, model = queries.shape
    tiles = rows // TILE
    groups, members = lax.axis_size("temporal"), lax.axis_size("ulysses")
    total = groups * members
    both = ("temporal", "ulysses")
    hops = -(-REACH // tiles)
    relay = members == 2 and hops == 1
    rim = min(REACH, tiles)
    cuts = [rim, tiles - rim] if relay and tiles > rim else []

    spans, low = [], 0
    for size in split_heads(model // HD):
        spans.append((low, size))
        low += size
    count = len(spans)
    sent = pack(queries, keys, values, spans[:1], [], [], VMEM_WHOLE)
    laid = pack(queries, after(keys, *sent), values, spans, spans, cuts, VMEM_LIMIT)
    blocks, heads_of, parts = laid[:count], laid[count : 2 * count], laid[2 * count :]
    sent = [[block] for block in (*sent, *blocks[1:])]
    if parts and count > 1:
        sent[-1] = parts

    onward = [(2 * g, 2 * g + 2) for g in range(groups - 1)]
    onward += [(2 * g + 3, 2 * g + 1) for g in range(groups - 1)]
    near = []
    for i, group_sent in enumerate(sent):
        if relay:
            swap = [(0, 1), (1, 0)]
            near.append([])
            for name, block in zip(("partner", "rest"), group_sent):
                with jax.named_scope(f"{name}_{i}"):
                    near[-1].append(lax.ppermute(block, "ulysses", swap))
        else:
            near.append(
                [
                    lax.ppermute(group_sent[0], both, [(j, j - o) for j in range(total) if 0 <= j - o < total])
                    for o in range(-hops, hops + 1)
                    if o
                ]
            )

    results, acc, mid = [], None, count - 3
    for i in range(count + 1):
        if i < count:
            pieces = [blocks[i], *near[i]]
            if relay:
                gate = near[i][0] if i < 2 else after(near[i][0], results[i - 2])
                with jax.named_scope(f"onward_{i}"):
                    pieces.append(lax.ppermute(gate, both, onward))
        if i >= 1:
            j = i - 1
            final = i == count
            early = None
            if final:
                early = results[max(mid + 1, 0) :]
            elif j == mid:
                early = results[:]
            layout = (hops, rim, relay, len(sent[j]) > 1)
            with jax.named_scope(f"attend_{j}"):
                result = attend(tile_list, counts, layout, heads_of[j], held, spans[j], early, out_weight, acc if final else None, final)
            results.append(result)
            if j == mid:
                acc = result
        held = pieces
    return results[-1]


def solution(mesh):
    return jax.shard_map(
        on_device,
        mesh=mesh,
        in_specs=(
            P(("temporal", "ulysses"), None),
            P(("temporal", "ulysses"), None),
            P(("temporal", "ulysses"), None),
            P("temporal", None),
            P("temporal"),
            P(),
        ),
        out_specs=P(("temporal", "ulysses"), None),
        check_vma=False,
    )
```

```python
import functools
import math

import jax
import jax.numpy as jnp
from jax import lax
from jax.experimental import pallas as pl
from jax.experimental.pallas import tpu as pltpu
from jax.sharding import PartitionSpec as P

HD = 128
TILE = 128
REACH = 3
STRIP = 256
HBM = pl.BlockSpec(memory_space=pltpu.HBM)
VMEM = pl.BlockSpec(memory_space=pltpu.VMEM)
SMEM = pl.BlockSpec(memory_space=pltpu.SMEM)
VMEM_LIMIT = 14 * 1024 * 1024
VMEM_WHOLE = 63 * 1024 * 1024


def split_heads(heads):
    sizes = []
    for share in (4 / 12, 3 / 12, 2 / 12, 2 / 12):
        size = min(max(1, round(share * heads)), heads - sum(sizes) - 1)
        if size > 0:
            sizes.append(size)
    return sizes + [heads - sum(sizes)]


def cut_spots(tiles, rim):
    member = lax.axis_index("ulysses")
    return [member * (tiles - rim), (1 - member) * rim]


def piece_spots(tiles, hops, rim, relay, parted):
    if not relay:
        return [tiles * hops] + [tiles * i for i in range(2 * hops + 1) if i != hops]
    member = lax.axis_index("ulysses")
    if not parted:
        return [tiles, 2 * tiles * (1 - member), 2 * tiles * member]
    return [
        tiles,
        (1 - member) * (3 * tiles - rim),
        (1 - member) * 2 * tiles + member * rim,
        (1 - member) * (tiles - rim) + member * 2 * tiles,
    ]


def pack_kernel(groups, q_groups, cuts, *refs):
    refs = list(refs)
    q_ref, k_ref, v_ref = [refs.pop(0) for _ in range(3)]
    outs = [refs.pop(0) for _ in groups]
    q_outs = [refs.pop(0) for _ in q_groups]
    cut_outs = [refs.pop(0) for _ in cuts]
    k_buf, out_buf, q_buf, sems, q_sems, cut_sems = refs
    rows = k_ref.shape[0]
    jobs, q_jobs = [], []
    for out, (low, size) in zip(outs, groups):
        for h in range(size):
            at = len(jobs)
            cols = pl.ds((low + h) * HD, HD)
            jobs.append(
                (
                    pltpu.make_async_copy(k_ref.at[:, cols], k_buf.at[at], sems.at[at, 0]),
                    pltpu.make_async_copy(v_ref.at[:, cols], out_buf.at[at, 1], sems.at[at, 1]),
                    pltpu.make_async_copy(out_buf.at[at], out.at[h], sems.at[at, 2]),
                )
            )
    for out, (low, size) in zip(q_outs, q_groups):
        for h in range(size):
            at = len(q_jobs)
            cols = pl.ds((low + h) * HD, HD)
            q_jobs.append(
                (
                    pltpu.make_async_copy(q_ref.at[:, cols], q_buf.at[at], q_sems.at[at, 0]),
                    pltpu.make_async_copy(q_buf.at[at], out.at[h], q_sems.at[at, 1]),
                )
            )
    for load_k, load_v, _ in jobs:
        load_k.start()
        load_v.start()
    for load, _ in q_jobs:
        load.start()
    for at, (load_k, load_v, store) in enumerate(jobs):
        load_k.wait()
        for tile in range(rows // TILE):
            span = slice(tile * TILE, (tile + 1) * TILE)
            out_buf[at, 0, span] = k_buf[at, span].T
        load_v.wait()
        store.start()
    cut_jobs = []
    spots = cut_spots(rows // TILE, cuts[0][-1]) if cuts else []
    for (start, size, which, extent), out in zip(cuts, cut_outs):
        part = pl.ds(pl.multiple_of(spots[which] * TILE, TILE), extent * TILE)
        for h in range(size):
            source = out_buf.at[start - groups[0][0] + h, :, part]
            cut_jobs.append(pltpu.make_async_copy(source, out.at[h], cut_sems.at[len(cut_jobs)]))
            cut_jobs[-1].start()
    for load, store in q_jobs:
        load.wait()
        store.start()
    for _, _, store in jobs:
        store.wait()
    for _, store in q_jobs:
        store.wait()
    for store in cut_jobs:
        store.wait()


def pack(queries, keys, values, groups, q_groups, cuts, limit):
    rows = keys.shape[0]
    heads = sum(size for _, size in groups)
    q_heads = sum(size for _, size in q_groups)
    shapes = [(size, 2, rows, HD) for _, size in groups] + [(size, rows, HD) for _, size in q_groups]
    shapes += [(size, 2, extent * TILE, HD) for _, size, _, extent in cuts]
    return pl.pallas_call(
        functools.partial(pack_kernel, groups, q_groups, cuts),
        out_shape=[jax.ShapeDtypeStruct(shape, keys.dtype) for shape in shapes],
        in_specs=[HBM] * 3,
        out_specs=[HBM] * len(shapes),
        scratch_shapes=[
            pltpu.VMEM((heads, rows, HD), keys.dtype),
            pltpu.VMEM((heads, 2, rows, HD), keys.dtype),
            pltpu.VMEM((max(q_heads, 1), rows, HD), keys.dtype),
            pltpu.SemaphoreType.DMA((heads, 3)),
            pltpu.SemaphoreType.DMA((max(q_heads, 1), 2)),
            pltpu.SemaphoreType.DMA((max(sum(size for _, size, _, _ in cuts), 1),)),
        ],
        compiler_params=pltpu.CompilerParams(vmem_limit_bytes=limit),
        cost_estimate=pl.CostEstimate(flops=0, bytes_accessed=8 * rows * heads * HD, transcendentals=0),
    )(queries, keys, values)


def attend_kernel(cfg, tiles_ref, counts_ref, q_ref, *refs):
    low, size, shifts, (hops, rim, relay, parted), early, has_acc, final = cfg
    refs = list(refs)
    piece_refs = [refs.pop(0) for _ in shifts]
    early_refs = [refs.pop(0) for _ in early or ()]
    w_ref = None if early is None else refs.pop(0)
    acc_ref = refs.pop(0) if has_acc else None
    out_ref, kv_buf = refs[:2]
    rows = q_ref.shape[1]
    tiles = rows // TILE
    slots = tiles_ref.shape[1]
    spans = (2 * hops + 1) * rows
    spots = piece_spots(tiles, hops, rim, relay, parted)
    member, members = lax.axis_index("ulysses"), lax.axis_size("ulysses")
    first = (lax.axis_index("temporal") * members + member - hops) * tiles
    att_buf, lead = out_ref, 0
    if early is not None:
        att_buf = refs[2]
        for extent, ref in zip(early, early_refs):
            att_buf[:, lead * HD : (lead + extent) * HD] = ref[...]
            lead += extent

    scale = math.log2(math.e) / math.sqrt(HD)
    zeros = jnp.zeros((TILE, HD), jnp.bfloat16)
    places, v_places, ones = [], [], []
    for tile in range(tiles):
        row = member * tiles + tile
        live = counts_ref[row]
        at = [pl.multiple_of((tiles_ref[row, j] - first) * TILE, TILE) for j in range(slots)]
        places.append(at)
        v_places.append([pl.multiple_of(jnp.where(j < live, at[j], spans), TILE) for j in range(slots)])
        ones.append([zeros + jnp.where(j < live, 1.0, 0.0).astype(jnp.bfloat16) for j in range(slots)])

    def scores(h, tile):
        k = jnp.concatenate([kv_buf[h % 2, 0, pl.ds(p, TILE)] for p in places[tile]], axis=1)
        q = q_ref[h, tile * TILE : (tile + 1) * TILE]
        return jnp.dot(q, k, preferred_element_type=jnp.float32)

    def finish(h, tile, s):
        top = jnp.max(s, axis=1, keepdims=True)
        p = jnp.exp2((s - top) * scale).astype(jnp.bfloat16)
        v = jnp.concatenate(
            [
                jnp.concatenate([kv_buf[h % 2, 1, pl.ds(at, TILE)], one], axis=1)
                for at, one in zip(v_places[tile], ones[tile])
            ],
            axis=0,
        )
        mixed = jnp.dot(p, v, preferred_element_type=jnp.float32)
        here = slice(tile * TILE, (tile + 1) * TILE)
        att_buf[here, (lead + h) * HD : (lead + h + 1) * HD] = (mixed[:, :HD] / mixed[:, HD:]).astype(jnp.bfloat16)

    def ready(h):
        for i, ref in enumerate(piece_refs):
            place = pl.ds(pl.multiple_of(spots[i] * TILE, TILE), ref.shape[2])
            for part in range(2):
                kv_buf[h % 2, part, place] = ref[h + shifts[i], part]
        kv_buf[h % 2, 1, spans : spans + TILE] = zeros

    jobs = [(h, tile) for h in range(size) for tile in range(tiles)]
    ready(0)
    ahead = scores(*jobs[0])
    for i, (h, tile) in enumerate(jobs):
        now = ahead
        if i + 1 < len(jobs):
            if jobs[i + 1][0] != h:
                ready(h + 1)
            ahead = scores(*jobs[i + 1])
        finish(h, tile, now)

    if early is None:
        return
    stores = []
    out_buf, out_sems = refs[3:] if final else (out_ref, None)
    for i, at in enumerate(range(0, out_buf.shape[1], STRIP)):
        here = slice(at, min(at + STRIP, out_buf.shape[1]))
        weights = w_ref[(low - lead) * HD : (low + size) * HD, here]
        part = jnp.dot(att_buf[...], weights, preferred_element_type=jnp.float32)
        if has_acc:
            part = part + acc_ref[:, here]
        out_buf[:, here] = part.astype(out_buf.dtype)
        if final:
            cols = pl.ds(at, here.stop - at)
            stores.append(pltpu.make_async_copy(out_buf.at[:, cols], out_ref.at[:, cols], out_sems.at[i]))
            stores[-1].start()
    for copy in stores:
        copy.wait()


def attend(tile_list, counts, layout, queries, pieces, shifts, span, early, out_weight, acc, final):
    rows = queries.shape[1]
    low, size = span
    reach = (2 * layout[0] + 1) * rows
    width = out_weight.shape[1]
    bf16 = jnp.bfloat16
    operands = [tile_list, counts, queries, *pieces]
    scratch = [pltpu.VMEM((2, 2, reach + TILE, HD), bf16)]
    parts = None
    out_shape = jax.ShapeDtypeStruct((rows, size * HD), bf16)
    if early is not None:
        parts = tuple(part.shape[1] // HD for part in early)
        operands += [*early, out_weight]
        if acc is not None:
            operands.append(acc)
        scratch.append(pltpu.VMEM((rows, (size + sum(parts)) * HD), bf16))
        out_shape = jax.ShapeDtypeStruct((rows, width), bf16 if final else jnp.float32)
        if final:
            scratch += [pltpu.VMEM((rows, width), bf16), pltpu.SemaphoreType.DMA((-(-width // STRIP),))]
    return pl.pallas_call(
        functools.partial(
            attend_kernel, (low, size, shifts, layout, parts, acc is not None, final)
        ),
        out_shape=out_shape,
        in_specs=[SMEM] * 2 + [VMEM] * (len(operands) - 2),
        out_specs=HBM if final else VMEM,
        scratch_shapes=scratch,
        compiler_params=pltpu.CompilerParams(vmem_limit_bytes=VMEM_LIMIT),
        cost_estimate=pl.CostEstimate(flops=0, bytes_accessed=0, transcendentals=0),
    )(*operands)


def after(array, *others):
    return lax.optimization_barrier((array, *others))[0]


def on_device(queries, keys, values, tile_list, counts, out_weight):
    rows, model = queries.shape
    tiles = rows // TILE
    groups, members = lax.axis_size("temporal"), lax.axis_size("ulysses")
    total = groups * members
    both = ("temporal", "ulysses")
    hops = -(-REACH // tiles)
    relay = members == 2 and hops == 1
    rim = min(REACH, tiles)

    spans, low = [], 0
    for size in split_heads(model // HD):
        spans.append((low, size))
        low += size
    count = len(spans)
    sent = pack(queries, keys, values, spans[:1], [], [], VMEM_WHOLE)
    split = max(1, count - 2) if relay and tiles > rim else count
    cuts = [(low, size, 0, rim) for low, size in spans[split:]]
    if cuts:
        rest_low = spans[split][0]
        cuts.append((rest_low, model // HD - rest_low, 1, tiles - rim))
    laid = pack(queries, after(keys, *sent), values, spans, spans, cuts, VMEM_LIMIT)
    blocks, heads_of, parts = laid[:count], laid[count : 2 * count], laid[2 * count :]
    sent = [*sent, *blocks[1:split], *parts]

    onward = [(2 * g, 2 * g + 2) for g in range(groups - 1)]
    onward += [(2 * g + 3, 2 * g + 1) for g in range(groups - 1)]
    near = []
    for i, block in enumerate(sent):
        if relay:
            with jax.named_scope(f"partner_{i}" if i < count else f"rest_{i}"):
                near.append([lax.ppermute(block, "ulysses", [(0, 1), (1, 0)])])
        else:
            near.append(
                [
                    lax.ppermute(block, both, [(j, j - o) for j in range(total) if 0 <= j - o < total])
                    for o in range(-hops, hops + 1)
                    if o
                ]
            )

    results, acc, mid = [], None, count - 4
    for i in range(count + 1):
        if i < count:
            pieces = [blocks[i], *near[i]]
            shifts = [0] * len(pieces)
            if i >= split:
                pieces += near[count]
                shifts.append(spans[i][0] - rest_low)
            if relay:
                gate = near[i][0] if i < 2 else after(near[i][0], results[i - 2])
                with jax.named_scope(f"onward_{i}"):
                    pieces.append(lax.ppermute(gate, both, onward))
                shifts.append(0)
        if i >= 1:
            j = i - 1
            final = i == count
            early = None
            if final:
                early = results[max(mid + 1, 0) :]
            elif j == mid:
                early = results[:]
            layout = (hops, rim, relay, j >= split)
            with jax.named_scope(f"attend_{j}"):
                result = attend(tile_list, counts, layout, heads_of[j], *held, spans[j], early, out_weight, acc if final else None, final)
            results.append(result)
            if j == mid:
                acc = result
        held = pieces, tuple(shifts)
    return results[-1]


def solution(mesh):
    return jax.shard_map(
        on_device,
        mesh=mesh,
        in_specs=(
            P(("temporal", "ulysses"), None),
            P(("temporal", "ulysses"), None),
            P(("temporal", "ulysses"), None),
            P("temporal", None),
            P("temporal"),
            P(),
        ),
        out_specs=P(("temporal", "ulysses"), None),
        check_vma=False,
    )
```

```python
import functools
import math

import jax
import jax.numpy as jnp
from jax import lax
from jax.experimental import pallas as pl
from jax.experimental.pallas import tpu as pltpu
from jax.sharding import PartitionSpec as P

HD = 128
TILE = 128
REACH = 3
STRIP = 256
HBM = pl.BlockSpec(memory_space=pltpu.HBM)
VMEM = pl.BlockSpec(memory_space=pltpu.VMEM)
SMEM = pl.BlockSpec(memory_space=pltpu.SMEM)
VMEM_LIMIT = 14 * 1024 * 1024
VMEM_WHOLE = 63 * 1024 * 1024


def split_heads(heads):
    sizes = []
    for share in (4 / 12, 3 / 12, 2 / 12, 2 / 12):
        size = min(max(1, round(share * heads)), heads - sum(sizes) - 1)
        if size > 0:
            sizes.append(size)
    return sizes + [heads - sum(sizes)]


def cut_spots(tiles, rim):
    member = lax.axis_index("ulysses")
    return [member * (tiles - rim), (1 - member) * rim]


def piece_spots(tiles, hops, rim, relay, parted):
    if not relay:
        return [tiles * hops] + [tiles * i for i in range(2 * hops + 1) if i != hops]
    member = lax.axis_index("ulysses")
    if not parted:
        return [tiles, 2 * tiles * (1 - member), 2 * tiles * member]
    return [
        tiles,
        (1 - member) * (3 * tiles - rim),
        (1 - member) * 2 * tiles + member * rim,
        (1 - member) * (tiles - rim) + member * 2 * tiles,
    ]


def pack_kernel(groups, q_groups, cuts, *refs):
    refs = list(refs)
    q_ref, k_ref, v_ref = [refs.pop(0) for _ in range(3)]
    outs = [refs.pop(0) for _ in groups]
    q_outs = [refs.pop(0) for _ in q_groups]
    cut_outs = [refs.pop(0) for _ in cuts]
    k_buf, out_buf, q_buf, sems, q_sems, cut_sems = refs
    rows = k_ref.shape[0]
    jobs, q_jobs = [], []
    for out, (low, size) in zip(outs, groups):
        for h in range(size):
            at = len(jobs)
            cols = pl.ds((low + h) * HD, HD)
            jobs.append(
                (
                    pltpu.make_async_copy(k_ref.at[:, cols], k_buf.at[at], sems.at[at, 0]),
                    pltpu.make_async_copy(v_ref.at[:, cols], out_buf.at[at, 1], sems.at[at, 1]),
                    pltpu.make_async_copy(out_buf.at[at], out.at[h], sems.at[at, 2]),
                )
            )
    for out, (low, size) in zip(q_outs, q_groups):
        for h in range(size):
            at = len(q_jobs)
            cols = pl.ds((low + h) * HD, HD)
            q_jobs.append(
                (
                    pltpu.make_async_copy(q_ref.at[:, cols], q_buf.at[at], q_sems.at[at, 0]),
                    pltpu.make_async_copy(q_buf.at[at], out.at[h], q_sems.at[at, 1]),
                )
            )
    for load_k, load_v, _ in jobs:
        load_k.start()
        load_v.start()
    for load, _ in q_jobs:
        load.start()
    for at, (load_k, load_v, store) in enumerate(jobs):
        load_k.wait()
        for tile in range(rows // TILE):
            span = slice(tile * TILE, (tile + 1) * TILE)
            out_buf[at, 0, span] = k_buf[at, span].T
        load_v.wait()
        store.start()
    cut_jobs = []
    spots = cut_spots(rows // TILE, cuts[0][-1]) if cuts else []
    for (start, size, which, extent), out in zip(cuts, cut_outs):
        part = pl.ds(pl.multiple_of(spots[which] * TILE, TILE), extent * TILE)
        for h in range(size):
            source = out_buf.at[start - groups[0][0] + h, :, part]
            cut_jobs.append(pltpu.make_async_copy(source, out.at[h], cut_sems.at[len(cut_jobs)]))
            cut_jobs[-1].start()
    for load, store in q_jobs:
        load.wait()
        store.start()
    for _, _, store in jobs:
        store.wait()
    for _, store in q_jobs:
        store.wait()
    for store in cut_jobs:
        store.wait()


def pack(queries, keys, values, groups, q_groups, cuts, limit):
    rows = keys.shape[0]
    heads = sum(size for _, size in groups)
    q_heads = sum(size for _, size in q_groups)
    shapes = [(size, 2, rows, HD) for _, size in groups] + [(size, rows, HD) for _, size in q_groups]
    shapes += [(size, 2, extent * TILE, HD) for _, size, _, extent in cuts]
    return pl.pallas_call(
        functools.partial(pack_kernel, groups, q_groups, cuts),
        out_shape=[jax.ShapeDtypeStruct(shape, keys.dtype) for shape in shapes],
        in_specs=[HBM] * 3,
        out_specs=[HBM] * len(shapes),
        scratch_shapes=[
            pltpu.VMEM((heads, rows, HD), keys.dtype),
            pltpu.VMEM((heads, 2, rows, HD), keys.dtype),
            pltpu.VMEM((max(q_heads, 1), rows, HD), keys.dtype),
            pltpu.SemaphoreType.DMA((heads, 3)),
            pltpu.SemaphoreType.DMA((max(q_heads, 1), 2)),
            pltpu.SemaphoreType.DMA((max(sum(size for _, size, _, _ in cuts), 1),)),
        ],
        compiler_params=pltpu.CompilerParams(vmem_limit_bytes=limit),
        cost_estimate=pl.CostEstimate(flops=0, bytes_accessed=8 * rows * heads * HD, transcendentals=0),
    )(queries, keys, values)


def attend_kernel(cfg, tiles_ref, counts_ref, q_ref, *refs):
    low, size, shifts, (hops, rim, relay, parted), early, has_acc, final = cfg
    refs = list(refs)
    piece_refs = [refs.pop(0) for _ in shifts]
    early_refs = [refs.pop(0) for _ in early or ()]
    w_ref = None if early is None else refs.pop(0)
    acc_ref = refs.pop(0) if has_acc else None
    out_ref, kv_buf = refs[:2]
    rows = q_ref.shape[1]
    tiles = rows // TILE
    slots = tiles_ref.shape[1]
    spans = (2 * hops + 1) * rows
    spots = piece_spots(tiles, hops, rim, relay, parted)
    member, members = lax.axis_index("ulysses"), lax.axis_size("ulysses")
    first = (lax.axis_index("temporal") * members + member - hops) * tiles
    att_buf, lead = out_ref, 0
    if early is not None:
        att_buf = refs[2]
        for extent, ref in zip(early, early_refs):
            att_buf[:, lead * HD : (lead + extent) * HD] = ref[...]
            lead += extent

    scale = math.log2(math.e) / math.sqrt(HD)
    zeros = jnp.zeros((TILE, HD), jnp.bfloat16)
    places, v_places, ones = [], [], []
    for tile in range(tiles):
        row = member * tiles + tile
        live = counts_ref[row]
        at = [pl.multiple_of((tiles_ref[row, j] - first) * TILE, TILE) for j in range(slots)]
        places.append(at)
        v_places.append([pl.multiple_of(jnp.where(j < live, at[j], spans), TILE) for j in range(slots)])
        ones.append([zeros + jnp.where(j < live, 1.0, 0.0).astype(jnp.bfloat16) for j in range(slots)])

    def scores(h, tile):
        k = jnp.concatenate([kv_buf[h % 2, 0, pl.ds(p, TILE)] for p in places[tile]], axis=1)
        q = q_ref[h, tile * TILE : (tile + 1) * TILE]
        return jnp.dot(q, k, preferred_element_type=jnp.float32)

    def finish(h, tile, s):
        top = jnp.max(s, axis=1, keepdims=True)
        p = jnp.exp2((s - top) * scale).astype(jnp.bfloat16)
        v = jnp.concatenate(
            [
                jnp.concatenate([kv_buf[h % 2, 1, pl.ds(at, TILE)], one], axis=1)
                for at, one in zip(v_places[tile], ones[tile])
            ],
            axis=0,
        )
        mixed = jnp.dot(p, v, preferred_element_type=jnp.float32)
        here = slice(tile * TILE, (tile + 1) * TILE)
        att_buf[here, (lead + h) * HD : (lead + h + 1) * HD] = (mixed[:, :HD] / mixed[:, HD:]).astype(jnp.bfloat16)

    def ready(h):
        for i, ref in enumerate(piece_refs):
            place = pl.ds(pl.multiple_of(spots[i] * TILE, TILE), ref.shape[2])
            for part in range(2):
                kv_buf[h % 2, part, place] = ref[h + shifts[i], part]
        kv_buf[h % 2, 1, spans : spans + TILE] = zeros

    jobs = [(h, tile) for h in range(size) for tile in range(tiles)]
    ready(0)
    ahead = scores(*jobs[0])
    for i, (h, tile) in enumerate(jobs):
        now = ahead
        if i + 1 < len(jobs):
            if jobs[i + 1][0] != h:
                ready(h + 1)
            ahead = scores(*jobs[i + 1])
        finish(h, tile, now)

    if early is None:
        return
    stores = []
    out_buf, out_sems = refs[3:] if final else (out_ref, None)
    for i, at in enumerate(range(0, out_buf.shape[1], STRIP)):
        here = slice(at, min(at + STRIP, out_buf.shape[1]))
        weights = w_ref[(low - lead) * HD : (low + size) * HD, here]
        part = jnp.dot(att_buf[...], weights, preferred_element_type=jnp.float32)
        if has_acc:
            part = part + acc_ref[:, here]
        out_buf[:, here] = part.astype(out_buf.dtype)
        if final:
            cols = pl.ds(at, here.stop - at)
            stores.append(pltpu.make_async_copy(out_buf.at[:, cols], out_ref.at[:, cols], out_sems.at[i]))
            stores[-1].start()
    for copy in stores:
        copy.wait()


def attend(tile_list, counts, layout, queries, pieces, shifts, span, early, out_weight, acc, final):
    rows = queries.shape[1]
    low, size = span
    reach = (2 * layout[0] + 1) * rows
    width = out_weight.shape[1]
    bf16 = jnp.bfloat16
    operands = [tile_list, counts, queries, *pieces]
    scratch = [pltpu.VMEM((2, 2, reach + TILE, HD), bf16)]
    parts = None
    out_shape = jax.ShapeDtypeStruct((rows, size * HD), bf16)
    if early is not None:
        parts = tuple(part.shape[1] // HD for part in early)
        operands += [*early, out_weight]
        if acc is not None:
            operands.append(acc)
        scratch.append(pltpu.VMEM((rows, (size + sum(parts)) * HD), bf16))
        out_shape = jax.ShapeDtypeStruct((rows, width), bf16 if final else jnp.float32)
        if final:
            scratch += [pltpu.VMEM((rows, width), bf16), pltpu.SemaphoreType.DMA((-(-width // STRIP),))]
    return pl.pallas_call(
        functools.partial(
            attend_kernel, (low, size, shifts, layout, parts, acc is not None, final)
        ),
        out_shape=out_shape,
        in_specs=[SMEM] * 2 + [VMEM] * (len(operands) - 2),
        out_specs=HBM if final else VMEM,
        scratch_shapes=scratch,
        compiler_params=pltpu.CompilerParams(vmem_limit_bytes=VMEM_LIMIT),
        cost_estimate=pl.CostEstimate(flops=0, bytes_accessed=0, transcendentals=0),
    )(*operands)


def after(array, *others):
    return lax.optimization_barrier((array, *others))[0]


def on_device(queries, keys, values, tile_list, counts, out_weight):
    rows, model = queries.shape
    tiles = rows // TILE
    groups, members = lax.axis_size("temporal"), lax.axis_size("ulysses")
    total = groups * members
    both = ("temporal", "ulysses")
    hops = -(-REACH // tiles)
    relay = members == 2 and hops == 1
    rim = min(REACH, tiles)

    spans, low = [], 0
    for size in split_heads(model // HD):
        spans.append((low, size))
        low += size
    count = len(spans)
    sent = pack(queries, keys, values, spans[:1], [], [], VMEM_WHOLE)
    split = max(1, count - 2) if relay and tiles > rim else count
    cuts = [(low, size, 0, rim) for low, size in spans[split:]]
    if cuts:
        rest_low = spans[split][0]
        cuts.append((rest_low, model // HD - rest_low, 1, tiles - rim))
    laid = pack(queries, after(keys, *sent), values, spans, spans, cuts, VMEM_LIMIT)
    blocks, heads_of, parts = laid[:count], laid[count : 2 * count], laid[2 * count :]
    sent = [*sent, *blocks[1:split], *parts]

    onward = [(2 * g, 2 * g + 2) for g in range(groups - 1)]
    onward += [(2 * g + 3, 2 * g + 1) for g in range(groups - 1)]
    near = []
    for i, block in enumerate(sent):
        if relay:
            with jax.named_scope(f"partner_{i}" if i < count else f"rest_{i}"):
                near.append([lax.ppermute(block, "ulysses", [(0, 1), (1, 0)])])
        else:
            near.append(
                [
                    lax.ppermute(block, both, [(j, j - o) for j in range(total) if 0 <= j - o < total])
                    for o in range(-hops, hops + 1)
                    if o
                ]
            )

    ends = [j for j in (count - 4, count - 2) if j >= 0] + [count - 1]
    results, acc, begin = [], None, 0
    for i in range(count + 1):
        if i < count:
            pieces = [blocks[i], *near[i]]
            shifts = [0] * len(pieces)
            if i >= split:
                pieces += near[count]
                shifts.append(spans[i][0] - rest_low)
            if relay:
                gate = near[i][0] if i < 2 else after(near[i][0], results[i - 2])
                with jax.named_scope(f"onward_{i}"):
                    pieces.append(lax.ppermute(gate, both, onward))
                shifts.append(0)
        if i >= 1:
            j = i - 1
            final = i == count
            early = results[begin:] if j in ends else None
            layout = (hops, rim, relay, j >= split)
            with jax.named_scope(f"attend_{j}"):
                result = attend(
                    tile_list, counts, layout, heads_of[j], *held, spans[j], early, out_weight,
                    None if early is None else acc, final,
                )
            results.append(result)
            if early is not None:
                acc, begin = result, i
        held = pieces, tuple(shifts)
    return results[-1]


def solution(mesh):
    return jax.shard_map(
        on_device,
        mesh=mesh,
        in_specs=(
            P(("temporal", "ulysses"), None),
            P(("temporal", "ulysses"), None),
            P(("temporal", "ulysses"), None),
            P("temporal", None),
            P("temporal"),
            P(),
        ),
        out_specs=P(("temporal", "ulysses"), None),
        check_vma=False,
    )
```

```python
import functools
import math

import jax
import jax.numpy as jnp
from jax import lax
from jax.experimental import pallas as pl
from jax.experimental.pallas import tpu as pltpu
from jax.sharding import PartitionSpec as P

HD = 128
TILE = 128
REACH = 3
STRIP = 256
HBM = pl.BlockSpec(memory_space=pltpu.HBM)
VMEM = pl.BlockSpec(memory_space=pltpu.VMEM)
SMEM = pl.BlockSpec(memory_space=pltpu.SMEM)
VMEM_LIMIT = 14 * 1024 * 1024
VMEM_WHOLE = 63 * 1024 * 1024


def split_heads(heads):
    sizes = []
    for share in (3 / 12, 3 / 12, 3 / 12, 2 / 12):
        size = min(max(1, round(share * heads)), heads - sum(sizes) - 1)
        if size > 0:
            sizes.append(size)
    return sizes + [heads - sum(sizes)]


def cut_spots(tiles, rim):
    member = lax.axis_index("ulysses")
    return [member * (tiles - rim), (1 - member) * rim]


def piece_spots(tiles, hops, rim, relay, parted):
    if not relay:
        return [tiles * hops] + [tiles * i for i in range(2 * hops + 1) if i != hops]
    member = lax.axis_index("ulysses")
    if not parted:
        return [tiles, 2 * tiles * (1 - member), 2 * tiles * member]
    return [
        tiles,
        (1 - member) * (3 * tiles - rim),
        (1 - member) * 2 * tiles + member * rim,
        (1 - member) * (tiles - rim) + member * 2 * tiles,
    ]


def pack_kernel(groups, q_groups, cuts, *refs):
    refs = list(refs)
    q_ref, k_ref, v_ref = [refs.pop(0) for _ in range(3)]
    outs = [refs.pop(0) for _ in groups]
    q_outs = [refs.pop(0) for _ in q_groups]
    cut_outs = [refs.pop(0) for _ in cuts]
    k_buf, out_buf, q_buf, sems, q_sems, cut_sems = refs
    rows = k_ref.shape[0]
    jobs, q_jobs = [], []
    for out, (low, size) in zip(outs, groups):
        for h in range(size):
            at = len(jobs)
            cols = pl.ds((low + h) * HD, HD)
            jobs.append(
                (
                    pltpu.make_async_copy(k_ref.at[:, cols], k_buf.at[at], sems.at[at, 0]),
                    pltpu.make_async_copy(v_ref.at[:, cols], out_buf.at[at, 1], sems.at[at, 1]),
                    pltpu.make_async_copy(out_buf.at[at], out.at[h], sems.at[at, 2]),
                )
            )
    for out, (low, size) in zip(q_outs, q_groups):
        for h in range(size):
            at = len(q_jobs)
            cols = pl.ds((low + h) * HD, HD)
            q_jobs.append(
                (
                    pltpu.make_async_copy(q_ref.at[:, cols], q_buf.at[at], q_sems.at[at, 0]),
                    pltpu.make_async_copy(q_buf.at[at], out.at[h], q_sems.at[at, 1]),
                )
            )
    for load_k, load_v, _ in jobs:
        load_k.start()
        load_v.start()
    for load, _ in q_jobs:
        load.start()
    for at, (load_k, load_v, store) in enumerate(jobs):
        load_k.wait()
        for tile in range(rows // TILE):
            span = slice(tile * TILE, (tile + 1) * TILE)
            out_buf[at, 0, span] = k_buf[at, span].T
        load_v.wait()
        store.start()
    cut_jobs = []
    spots = cut_spots(rows // TILE, cuts[0][-1]) if cuts else []
    for (start, size, which, extent), out in zip(cuts, cut_outs):
        part = pl.ds(pl.multiple_of(spots[which] * TILE, TILE), extent * TILE)
        for h in range(size):
            source = out_buf.at[start - groups[0][0] + h, :, part]
            cut_jobs.append(pltpu.make_async_copy(source, out.at[h], cut_sems.at[len(cut_jobs)]))
            cut_jobs[-1].start()
    for load, store in q_jobs:
        load.wait()
        store.start()
    for _, _, store in jobs:
        store.wait()
    for _, store in q_jobs:
        store.wait()
    for store in cut_jobs:
        store.wait()


def pack(queries, keys, values, groups, q_groups, cuts, limit):
    rows = keys.shape[0]
    heads = sum(size for _, size in groups)
    q_heads = sum(size for _, size in q_groups)
    shapes = [(size, 2, rows, HD) for _, size in groups] + [(size, rows, HD) for _, size in q_groups]
    shapes += [(size, 2, extent * TILE, HD) for _, size, _, extent in cuts]
    return pl.pallas_call(
        functools.partial(pack_kernel, groups, q_groups, cuts),
        out_shape=[jax.ShapeDtypeStruct(shape, keys.dtype) for shape in shapes],
        in_specs=[HBM] * 3,
        out_specs=[HBM] * len(shapes),
        scratch_shapes=[
            pltpu.VMEM((heads, rows, HD), keys.dtype),
            pltpu.VMEM((heads, 2, rows, HD), keys.dtype),
            pltpu.VMEM((max(q_heads, 1), rows, HD), keys.dtype),
            pltpu.SemaphoreType.DMA((heads, 3)),
            pltpu.SemaphoreType.DMA((max(q_heads, 1), 2)),
            pltpu.SemaphoreType.DMA((max(sum(size for _, size, _, _ in cuts), 1),)),
        ],
        compiler_params=pltpu.CompilerParams(vmem_limit_bytes=limit),
        cost_estimate=pl.CostEstimate(flops=0, bytes_accessed=8 * rows * heads * HD, transcendentals=0),
    )(queries, keys, values)


def attend_kernel(cfg, tiles_ref, counts_ref, q_ref, *refs):
    low, size, shifts, (hops, rim, relay, parted), early, has_acc, final = cfg
    refs = list(refs)
    piece_refs = [refs.pop(0) for _ in shifts]
    early_refs = [refs.pop(0) for _ in early or ()]
    w_ref = None if early is None else refs.pop(0)
    acc_ref = refs.pop(0) if has_acc else None
    out_ref, kv_buf = refs[:2]
    rows = q_ref.shape[1]
    tiles = rows // TILE
    slots = tiles_ref.shape[1]
    spans = (2 * hops + 1) * rows
    spots = piece_spots(tiles, hops, rim, relay, parted)
    member, members = lax.axis_index("ulysses"), lax.axis_size("ulysses")
    first = (lax.axis_index("temporal") * members + member - hops) * tiles
    att_buf, lead = out_ref, 0
    if early is not None:
        att_buf = refs[2]
        for extent, ref in zip(early, early_refs):
            att_buf[:, lead * HD : (lead + extent) * HD] = ref[...]
            lead += extent

    scale = math.log2(math.e) / math.sqrt(HD)
    zeros = jnp.zeros((TILE, HD), jnp.bfloat16)
    places, v_places, ones = [], [], []
    for tile in range(tiles):
        row = member * tiles + tile
        live = counts_ref[row]
        at = [pl.multiple_of((tiles_ref[row, j] - first) * TILE, TILE) for j in range(slots)]
        places.append(at)
        v_places.append([pl.multiple_of(jnp.where(j < live, at[j], spans), TILE) for j in range(slots)])
        ones.append([zeros + jnp.where(j < live, 1.0, 0.0).astype(jnp.bfloat16) for j in range(slots)])

    def scores(h, tile):
        k = jnp.concatenate([kv_buf[h % 2, 0, pl.ds(p, TILE)] for p in places[tile]], axis=1)
        q = q_ref[h, tile * TILE : (tile + 1) * TILE]
        return jnp.dot(q, k, preferred_element_type=jnp.float32)

    def finish(h, tile, s):
        top = jnp.max(s, axis=1, keepdims=True)
        p = jnp.exp2((s - top) * scale).astype(jnp.bfloat16)
        v = jnp.concatenate(
            [
                jnp.concatenate([kv_buf[h % 2, 1, pl.ds(at, TILE)], one], axis=1)
                for at, one in zip(v_places[tile], ones[tile])
            ],
            axis=0,
        )
        mixed = jnp.dot(p, v, preferred_element_type=jnp.float32)
        here = slice(tile * TILE, (tile + 1) * TILE)
        att_buf[here, (lead + h) * HD : (lead + h + 1) * HD] = (mixed[:, :HD] / mixed[:, HD:]).astype(jnp.bfloat16)

    def ready(h):
        for i, ref in enumerate(piece_refs):
            place = pl.ds(pl.multiple_of(spots[i] * TILE, TILE), ref.shape[2])
            for part in range(2):
                kv_buf[h % 2, part, place] = ref[h + shifts[i], part]
        kv_buf[h % 2, 1, spans : spans + TILE] = zeros

    jobs = [(h, tile) for h in range(size) for tile in range(tiles)]
    ready(0)
    ahead = scores(*jobs[0])
    for i, (h, tile) in enumerate(jobs):
        now = ahead
        if i + 1 < len(jobs):
            if jobs[i + 1][0] != h:
                ready(h + 1)
            ahead = scores(*jobs[i + 1])
        finish(h, tile, now)

    if early is None:
        return
    stores = []
    out_buf, out_sems = refs[3:] if final else (out_ref, None)
    for i, at in enumerate(range(0, out_buf.shape[1], STRIP)):
        here = slice(at, min(at + STRIP, out_buf.shape[1]))
        weights = w_ref[(low - lead) * HD : (low + size) * HD, here]
        part = jnp.dot(att_buf[...], weights, preferred_element_type=jnp.float32)
        if has_acc:
            part = part + acc_ref[:, here]
        out_buf[:, here] = part.astype(out_buf.dtype)
        if final:
            cols = pl.ds(at, here.stop - at)
            stores.append(pltpu.make_async_copy(out_buf.at[:, cols], out_ref.at[:, cols], out_sems.at[i]))
            stores[-1].start()
    for copy in stores:
        copy.wait()


def attend(tile_list, counts, layout, queries, pieces, shifts, span, early, out_weight, acc, final):
    rows = queries.shape[1]
    low, size = span
    reach = (2 * layout[0] + 1) * rows
    width = out_weight.shape[1]
    bf16 = jnp.bfloat16
    operands = [tile_list, counts, queries, *pieces]
    scratch = [pltpu.VMEM((2, 2, reach + TILE, HD), bf16)]
    parts = None
    out_shape = jax.ShapeDtypeStruct((rows, size * HD), bf16)
    if early is not None:
        parts = tuple(part.shape[1] // HD for part in early)
        operands += [*early, out_weight]
        if acc is not None:
            operands.append(acc)
        scratch.append(pltpu.VMEM((rows, (size + sum(parts)) * HD), bf16))
        out_shape = jax.ShapeDtypeStruct((rows, width), bf16 if final else jnp.float32)
        if final:
            scratch += [pltpu.VMEM((rows, width), bf16), pltpu.SemaphoreType.DMA((-(-width // STRIP),))]
    return pl.pallas_call(
        functools.partial(
            attend_kernel, (low, size, shifts, layout, parts, acc is not None, final)
        ),
        out_shape=out_shape,
        in_specs=[SMEM] * 2 + [VMEM] * (len(operands) - 2),
        out_specs=HBM if final else VMEM,
        scratch_shapes=scratch,
        compiler_params=pltpu.CompilerParams(vmem_limit_bytes=VMEM_LIMIT),
        cost_estimate=pl.CostEstimate(flops=0, bytes_accessed=0, transcendentals=0),
    )(*operands)


def after(array, *others):
    return lax.optimization_barrier((array, *others))[0]


def on_device(queries, keys, values, tile_list, counts, out_weight):
    rows, model = queries.shape
    tiles = rows // TILE
    groups, members = lax.axis_size("temporal"), lax.axis_size("ulysses")
    total = groups * members
    both = ("temporal", "ulysses")
    hops = -(-REACH // tiles)
    relay = members == 2 and hops == 1
    rim = min(REACH, tiles)

    spans, low = [], 0
    for size in split_heads(model // HD):
        spans.append((low, size))
        low += size
    count = len(spans)
    sent = pack(queries, keys, values, spans[:1], [], [], VMEM_WHOLE)
    split = max(1, count - 2) if relay and tiles > rim else count
    cuts = [(low, size, 0, rim) for low, size in spans[split:]]
    if cuts:
        rest_low = spans[split][0]
        cuts.append((rest_low, model // HD - rest_low, 1, tiles - rim))
    laid = pack(queries, after(keys, *sent), values, spans, spans, cuts, VMEM_LIMIT)
    blocks, heads_of, parts = laid[:count], laid[count : 2 * count], laid[2 * count :]
    sent = [*sent, *blocks[1:split], *parts]

    onward = [(2 * g, 2 * g + 2) for g in range(groups - 1)]
    onward += [(2 * g + 3, 2 * g + 1) for g in range(groups - 1)]
    near = []
    for i, block in enumerate(sent):
        if relay:
            with jax.named_scope(f"partner_{i}" if i < count else f"rest_{i}"):
                near.append([lax.ppermute(block, "ulysses", [(0, 1), (1, 0)])])
        else:
            near.append(
                [
                    lax.ppermute(block, both, [(j, j - o) for j in range(total) if 0 <= j - o < total])
                    for o in range(-hops, hops + 1)
                    if o
                ]
            )

    ends = [j for j in (count - 4, count - 2) if j >= 0] + [count - 1]
    results, acc, begin = [], None, 0
    for i in range(count + 1):
        if i < count:
            pieces = [blocks[i], *near[i]]
            shifts = [0] * len(pieces)
            if i >= split:
                pieces += near[count]
                shifts.append(spans[i][0] - rest_low)
            if relay:
                back = 3 if i == count - 1 else 2
                gate = near[i][0] if i < back else after(near[i][0], results[i - back])
                with jax.named_scope(f"onward_{i}"):
                    pieces.append(lax.ppermute(gate, both, onward))
                shifts.append(0)
        if i >= 1:
            j = i - 1
            final = i == count
            early = results[begin:] if j in ends else None
            layout = (hops, rim, relay, j >= split)
            with jax.named_scope(f"attend_{j}"):
                result = attend(
                    tile_list, counts, layout, heads_of[j], *held, spans[j], early, out_weight,
                    None if early is None else acc, final,
                )
            results.append(result)
            if early is not None:
                acc, begin = result, i
        held = pieces, tuple(shifts)
    return results[-1]


def solution(mesh):
    return jax.shard_map(
        on_device,
        mesh=mesh,
        in_specs=(
            P(("temporal", "ulysses"), None),
            P(("temporal", "ulysses"), None),
            P(("temporal", "ulysses"), None),
            P("temporal", None),
            P("temporal"),
            P(),
        ),
        out_specs=P(("temporal", "ulysses"), None),
        check_vma=False,
    )
```

```python
import functools
import math

import jax
import jax.numpy as jnp
from jax import lax
from jax.experimental import pallas as pl
from jax.experimental.pallas import tpu as pltpu
from jax.sharding import PartitionSpec as P

HD = 128
TILE = 128
REACH = 3
STRIP = 256
HBM = pl.BlockSpec(memory_space=pltpu.HBM)
VMEM = pl.BlockSpec(memory_space=pltpu.VMEM)
SMEM = pl.BlockSpec(memory_space=pltpu.SMEM)
VMEM_LIMIT = 14 * 1024 * 1024
VMEM_WHOLE = 63 * 1024 * 1024


def split_heads(heads):
    sizes = []
    for share in (3 / 12, 3 / 12, 3 / 12, 2 / 12):
        size = min(max(1, round(share * heads)), heads - sum(sizes) - 1)
        if size > 0:
            sizes.append(size)
    return sizes + [heads - sum(sizes)]


def cut_spots(tiles, rim):
    member = lax.axis_index("ulysses")
    return [member * (tiles - rim), (1 - member) * rim]


def piece_spots(tiles, hops, rim, relay, parted):
    if not relay:
        return [tiles * hops] + [tiles * i for i in range(2 * hops + 1) if i != hops]
    member = lax.axis_index("ulysses")
    if not parted:
        return [tiles, 2 * tiles * (1 - member), 2 * tiles * member]
    return [
        tiles,
        (1 - member) * (3 * tiles - rim),
        (1 - member) * 2 * tiles + member * rim,
        (1 - member) * (tiles - rim) + member * 2 * tiles,
    ]


def pack_kernel(groups, q_groups, cuts, *refs):
    refs = list(refs)
    q_ref, k_ref, v_ref = [refs.pop(0) for _ in range(3)]
    outs = [refs.pop(0) for _ in groups]
    q_outs = [refs.pop(0) for _ in q_groups]
    cut_outs = [refs.pop(0) for _ in cuts]
    k_buf, out_buf, q_buf, sems, q_sems, cut_sems = refs
    rows = k_ref.shape[0]
    jobs, q_jobs = [], []
    for out, (low, size) in zip(outs, groups):
        for h in range(size):
            at = len(jobs)
            cols = pl.ds((low + h) * HD, HD)
            jobs.append(
                (
                    pltpu.make_async_copy(k_ref.at[:, cols], k_buf.at[at], sems.at[at, 0]),
                    pltpu.make_async_copy(v_ref.at[:, cols], out_buf.at[at, 1], sems.at[at, 1]),
                    pltpu.make_async_copy(out_buf.at[at], out.at[h], sems.at[at, 2]),
                )
            )
    for out, (low, size) in zip(q_outs, q_groups):
        for h in range(size):
            at = len(q_jobs)
            cols = pl.ds((low + h) * HD, HD)
            q_jobs.append(
                (
                    pltpu.make_async_copy(q_ref.at[:, cols], q_buf.at[at], q_sems.at[at, 0]),
                    pltpu.make_async_copy(q_buf.at[at], out.at[h], q_sems.at[at, 1]),
                )
            )
    for load_k, load_v, _ in jobs:
        load_k.start()
        load_v.start()
    for load, _ in q_jobs:
        load.start()
    for at, (load_k, load_v, store) in enumerate(jobs):
        load_k.wait()
        for tile in range(rows // TILE):
            span = slice(tile * TILE, (tile + 1) * TILE)
            out_buf[at, 0, span] = k_buf[at, span].T
        load_v.wait()
        store.start()
    cut_jobs = []
    spots = cut_spots(rows // TILE, cuts[0][-1]) if cuts else []
    for (start, size, which, extent), out in zip(cuts, cut_outs):
        part = pl.ds(pl.multiple_of(spots[which] * TILE, TILE), extent * TILE)
        for h in range(size):
            source = out_buf.at[start - groups[0][0] + h, :, part]
            cut_jobs.append(pltpu.make_async_copy(source, out.at[h], cut_sems.at[len(cut_jobs)]))
            cut_jobs[-1].start()
    for load, store in q_jobs:
        load.wait()
        store.start()
    for _, _, store in jobs:
        store.wait()
    for _, store in q_jobs:
        store.wait()
    for store in cut_jobs:
        store.wait()


def pack(queries, keys, values, groups, q_groups, cuts, limit):
    rows = keys.shape[0]
    heads = sum(size for _, size in groups)
    q_heads = sum(size for _, size in q_groups)
    shapes = [(size, 2, rows, HD) for _, size in groups] + [(size, rows, HD) for _, size in q_groups]
    shapes += [(size, 2, extent * TILE, HD) for _, size, _, extent in cuts]
    return pl.pallas_call(
        functools.partial(pack_kernel, groups, q_groups, cuts),
        out_shape=[jax.ShapeDtypeStruct(shape, keys.dtype) for shape in shapes],
        in_specs=[HBM] * 3,
        out_specs=[HBM] * len(shapes),
        scratch_shapes=[
            pltpu.VMEM((heads, rows, HD), keys.dtype),
            pltpu.VMEM((heads, 2, rows, HD), keys.dtype),
            pltpu.VMEM((max(q_heads, 1), rows, HD), keys.dtype),
            pltpu.SemaphoreType.DMA((heads, 3)),
            pltpu.SemaphoreType.DMA((max(q_heads, 1), 2)),
            pltpu.SemaphoreType.DMA((max(sum(size for _, size, _, _ in cuts), 1),)),
        ],
        compiler_params=pltpu.CompilerParams(vmem_limit_bytes=limit),
        cost_estimate=pl.CostEstimate(flops=0, bytes_accessed=8 * rows * heads * HD, transcendentals=0),
    )(queries, keys, values)


def attend_kernel(cfg, tiles_ref, counts_ref, q_ref, *refs):
    low, size, shifts, (hops, rim, relay, parted), early, projects, has_acc, final = cfg
    refs = list(refs)
    piece_refs = [refs.pop(0) for _ in shifts]
    early_refs = [refs.pop(0) for _ in early or ()]
    w_ref = refs.pop(0) if projects else None
    acc_ref = refs.pop(0) if has_acc else None
    out_ref, kv_buf = refs[:2]
    rows = q_ref.shape[1]
    tiles = rows // TILE
    slots = tiles_ref.shape[1]
    spans = (2 * hops + 1) * rows
    spots = piece_spots(tiles, hops, rim, relay, parted)
    member, members = lax.axis_index("ulysses"), lax.axis_size("ulysses")
    first = (lax.axis_index("temporal") * members + member - hops) * tiles
    att_buf, lead = out_ref, 0
    if early is not None:
        att_buf = refs[2] if projects else out_ref
        for extent, ref in zip(early, early_refs):
            att_buf[:, lead * HD : (lead + extent) * HD] = ref[...]
            lead += extent

    scale = math.log2(math.e) / math.sqrt(HD)
    zeros = jnp.zeros((TILE, HD), jnp.bfloat16)
    places, v_places, ones = [], [], []
    for tile in range(tiles):
        row = member * tiles + tile
        live = counts_ref[row]
        at = [pl.multiple_of((tiles_ref[row, j] - first) * TILE, TILE) for j in range(slots)]
        places.append(at)
        v_places.append([pl.multiple_of(jnp.where(j < live, at[j], spans), TILE) for j in range(slots)])
        ones.append([zeros + jnp.where(j < live, 1.0, 0.0).astype(jnp.bfloat16) for j in range(slots)])

    def scores(h, tile):
        k = jnp.concatenate([kv_buf[h % 2, 0, pl.ds(p, TILE)] for p in places[tile]], axis=1)
        q = q_ref[h, tile * TILE : (tile + 1) * TILE]
        return jnp.dot(q, k, preferred_element_type=jnp.float32)

    def finish(h, tile, s):
        top = jnp.max(s, axis=1, keepdims=True)
        p = jnp.exp2((s - top) * scale).astype(jnp.bfloat16)
        v = jnp.concatenate(
            [
                jnp.concatenate([kv_buf[h % 2, 1, pl.ds(at, TILE)], one], axis=1)
                for at, one in zip(v_places[tile], ones[tile])
            ],
            axis=0,
        )
        mixed = jnp.dot(p, v, preferred_element_type=jnp.float32)
        here = slice(tile * TILE, (tile + 1) * TILE)
        att_buf[here, (lead + h) * HD : (lead + h + 1) * HD] = (mixed[:, :HD] / mixed[:, HD:]).astype(jnp.bfloat16)

    def ready(h):
        for i, ref in enumerate(piece_refs):
            place = pl.ds(pl.multiple_of(spots[i] * TILE, TILE), ref.shape[2])
            for part in range(2):
                kv_buf[h % 2, part, place] = ref[h + shifts[i], part]
        kv_buf[h % 2, 1, spans : spans + TILE] = zeros

    jobs = [(h, tile) for h in range(size) for tile in range(tiles)]
    ready(0)
    ahead = scores(*jobs[0])
    for i, (h, tile) in enumerate(jobs):
        now = ahead
        if i + 1 < len(jobs):
            if jobs[i + 1][0] != h:
                ready(h + 1)
            ahead = scores(*jobs[i + 1])
        finish(h, tile, now)

    if not projects:
        return
    stores = []
    out_buf, out_sems = refs[3:] if final else (out_ref, None)
    for i, at in enumerate(range(0, out_buf.shape[1], STRIP)):
        here = slice(at, min(at + STRIP, out_buf.shape[1]))
        weights = w_ref[(low - lead) * HD : (low + size) * HD, here]
        part = jnp.dot(att_buf[...], weights, preferred_element_type=jnp.float32)
        if has_acc:
            part = part + acc_ref[:, here]
        out_buf[:, here] = part.astype(out_buf.dtype)
        if final:
            cols = pl.ds(at, here.stop - at)
            stores.append(pltpu.make_async_copy(out_buf.at[:, cols], out_ref.at[:, cols], out_sems.at[i]))
            stores[-1].start()
    for copy in stores:
        copy.wait()


def attend(tile_list, counts, layout, queries, pieces, shifts, span, early, out_weight, acc, final):
    rows = queries.shape[1]
    low, size = span
    reach = (2 * layout[0] + 1) * rows
    projects = out_weight is not None
    bf16 = jnp.bfloat16
    operands = [tile_list, counts, queries, *pieces]
    scratch = [pltpu.VMEM((2, 2, reach + TILE, HD), bf16)]
    parts = None
    out_shape = jax.ShapeDtypeStruct((rows, size * HD), bf16)
    if early is not None:
        parts = tuple(part.shape[1] // HD for part in early)
        operands += early
        out_shape = jax.ShapeDtypeStruct((rows, (size + sum(parts)) * HD), bf16)
    if projects:
        width = out_weight.shape[1]
        operands.append(out_weight)
        if acc is not None:
            operands.append(acc)
        scratch.append(pltpu.VMEM(out_shape.shape, bf16))
        out_shape = jax.ShapeDtypeStruct((rows, width), bf16 if final else jnp.float32)
        if final:
            scratch += [pltpu.VMEM((rows, width), bf16), pltpu.SemaphoreType.DMA((-(-width // STRIP),))]
    return pl.pallas_call(
        functools.partial(
            attend_kernel, (low, size, shifts, layout, parts, projects, acc is not None, final)
        ),
        out_shape=out_shape,
        in_specs=[SMEM] * 2 + [VMEM] * (len(operands) - 2),
        out_specs=HBM if final else VMEM,
        scratch_shapes=scratch,
        compiler_params=pltpu.CompilerParams(vmem_limit_bytes=VMEM_LIMIT),
        cost_estimate=pl.CostEstimate(flops=0, bytes_accessed=0, transcendentals=0),
    )(*operands)


def after(array, *others):
    return lax.optimization_barrier((array, *others))[0]


def on_device(queries, keys, values, tile_list, counts, out_weight):
    rows, model = queries.shape
    tiles = rows // TILE
    groups, members = lax.axis_size("temporal"), lax.axis_size("ulysses")
    total = groups * members
    both = ("temporal", "ulysses")
    hops = -(-REACH // tiles)
    relay = members == 2 and hops == 1
    rim = min(REACH, tiles)

    spans, low = [], 0
    for size in split_heads(model // HD):
        spans.append((low, size))
        low += size
    count = len(spans)
    sent = pack(queries, keys, values, spans[:1], [], [], VMEM_WHOLE)
    split = max(1, count - 2) if relay and tiles > rim else count
    cuts = [(low, size, 0, rim) for low, size in spans[split:]]
    if cuts:
        rest_low = spans[split][0]
        cuts.append((rest_low, model // HD - rest_low, 1, tiles - rim))
    laid = pack(queries, after(keys, *sent), values, spans, spans, cuts, VMEM_LIMIT)
    blocks, heads_of, parts = laid[:count], laid[count : 2 * count], laid[2 * count :]
    sent = [*sent, *blocks[1:split], *parts]

    onward = [(2 * g, 2 * g + 2) for g in range(groups - 1)]
    onward += [(2 * g + 3, 2 * g + 1) for g in range(groups - 1)]
    near = []
    for i, block in enumerate(sent):
        if relay:
            with jax.named_scope(f"partner_{i}" if i < count else f"rest_{i}"):
                near.append([lax.ppermute(block, "ulysses", [(0, 1), (1, 0)])])
        else:
            near.append(
                [
                    lax.ppermute(block, both, [(j, j - o) for j in range(total) if 0 <= j - o < total])
                    for o in range(-hops, hops + 1)
                    if o
                ]
            )

    ends = [j for j in (count - 4,) if j >= 0] + [count - 1]
    results, acc, begin = [], None, 0
    for i in range(count + 1):
        if i < count:
            pieces = [blocks[i], *near[i]]
            shifts = [0] * len(pieces)
            if i >= split:
                pieces += near[count]
                shifts.append(spans[i][0] - rest_low)
            if relay:
                back = 3 if i == count - 1 else 2
                gate = near[i][0] if i < back else after(near[i][0], results[i - back])
                with jax.named_scope(f"onward_{i}"):
                    pieces.append(lax.ppermute(gate, both, onward))
                shifts.append(0)
        if i >= 1:
            j = i - 1
            final = i == count
            projects = j in ends
            early = results[begin:] if projects or j == count - 2 else None
            layout = (hops, rim, relay, j >= split)
            with jax.named_scope(f"attend_{j}"):
                result = attend(
                    tile_list, counts, layout, heads_of[j], *held, spans[j], early,
                    out_weight if projects else None, acc if projects else None, final,
                )
            results.append(result)
            if projects:
                acc, begin = result, i
            elif early is not None:
                begin = j
        held = pieces, tuple(shifts)
    return results[-1]


def solution(mesh):
    return jax.shard_map(
        on_device,
        mesh=mesh,
        in_specs=(
            P(("temporal", "ulysses"), None),
            P(("temporal", "ulysses"), None),
            P(("temporal", "ulysses"), None),
            P("temporal", None),
            P("temporal"),
            P(),
        ),
        out_specs=P(("temporal", "ulysses"), None),
        check_vma=False,
    )
```

```python
import functools
import math

import jax
import jax.numpy as jnp
from jax import lax
from jax.experimental import pallas as pl
from jax.experimental.pallas import tpu as pltpu
from jax.sharding import PartitionSpec as P

HD = 128
TILE = 128
REACH = 3
STRIP = 256
HBM = pl.BlockSpec(memory_space=pltpu.HBM)
VMEM = pl.BlockSpec(memory_space=pltpu.VMEM)
SMEM = pl.BlockSpec(memory_space=pltpu.SMEM)
VMEM_LIMIT = 14 * 1024 * 1024
VMEM_WHOLE = 63 * 1024 * 1024


def split_heads(heads):
    sizes = []
    for share in (3 / 12, 3 / 12, 3 / 12, 2 / 12):
        size = min(max(1, round(share * heads)), heads - sum(sizes) - 1)
        if size > 0:
            sizes.append(size)
    return sizes + [heads - sum(sizes)]


def cut_spots(tiles, rim):
    member = lax.axis_index("ulysses")
    return [member * (tiles - rim), (1 - member) * rim]


def piece_spots(tiles, hops, rim, relay, parted):
    if not relay:
        return [tiles * hops] + [tiles * i for i in range(2 * hops + 1) if i != hops]
    member = lax.axis_index("ulysses")
    if not parted:
        return [tiles, 2 * tiles * (1 - member), 2 * tiles * member]
    return [
        tiles,
        (1 - member) * (3 * tiles - rim),
        (1 - member) * 2 * tiles + member * rim,
        (1 - member) * (tiles - rim) + member * 2 * tiles,
    ]


def pack_kernel(groups, q_groups, cuts, *refs):
    refs = list(refs)
    q_ref, k_ref, v_ref = [refs.pop(0) for _ in range(3)]
    outs = [refs.pop(0) for _ in groups]
    q_outs = [refs.pop(0) for _ in q_groups]
    cut_outs = [refs.pop(0) for _ in cuts]
    k_buf, out_buf, q_buf, sems, q_sems, cut_sems = refs
    rows = k_ref.shape[0]
    jobs, q_jobs = [], []
    for out, (low, size) in zip(outs, groups):
        for h in range(size):
            at = len(jobs)
            cols = pl.ds((low + h) * HD, HD)
            jobs.append(
                (
                    pltpu.make_async_copy(k_ref.at[:, cols], k_buf.at[at], sems.at[at, 0]),
                    pltpu.make_async_copy(v_ref.at[:, cols], out_buf.at[at, 1], sems.at[at, 1]),
                    pltpu.make_async_copy(out_buf.at[at], out.at[h], sems.at[at, 2]),
                )
            )
    for out, (low, size) in zip(q_outs, q_groups):
        for h in range(size):
            at = len(q_jobs)
            cols = pl.ds((low + h) * HD, HD)
            q_jobs.append(
                (
                    pltpu.make_async_copy(q_ref.at[:, cols], q_buf.at[at], q_sems.at[at, 0]),
                    pltpu.make_async_copy(q_buf.at[at], out.at[h], q_sems.at[at, 1]),
                )
            )
    for load_k, load_v, _ in jobs:
        load_k.start()
        load_v.start()
    for load, _ in q_jobs:
        load.start()
    for at, (load_k, load_v, store) in enumerate(jobs):
        load_k.wait()
        for tile in range(rows // TILE):
            span = slice(tile * TILE, (tile + 1) * TILE)
            out_buf[at, 0, span] = k_buf[at, span].T
        load_v.wait()
        store.start()
    cut_jobs = []
    spots = cut_spots(rows // TILE, cuts[0][-1]) if cuts else []
    for (start, size, which, extent), out in zip(cuts, cut_outs):
        part = pl.ds(pl.multiple_of(spots[which] * TILE, TILE), extent * TILE)
        for h in range(size):
            source = out_buf.at[start - groups[0][0] + h, :, part]
            cut_jobs.append(pltpu.make_async_copy(source, out.at[h], cut_sems.at[len(cut_jobs)]))
            cut_jobs[-1].start()
    for load, store in q_jobs:
        load.wait()
        store.start()
    for _, _, store in jobs:
        store.wait()
    for _, store in q_jobs:
        store.wait()
    for store in cut_jobs:
        store.wait()


def pack(queries, keys, values, groups, q_groups, cuts, limit):
    rows = keys.shape[0]
    heads = sum(size for _, size in groups)
    q_heads = sum(size for _, size in q_groups)
    shapes = [(size, 2, rows, HD) for _, size in groups] + [(size, rows, HD) for _, size in q_groups]
    shapes += [(size, 2, extent * TILE, HD) for _, size, _, extent in cuts]
    return pl.pallas_call(
        functools.partial(pack_kernel, groups, q_groups, cuts),
        out_shape=[jax.ShapeDtypeStruct(shape, keys.dtype) for shape in shapes],
        in_specs=[HBM] * 3,
        out_specs=[HBM] * len(shapes),
        scratch_shapes=[
            pltpu.VMEM((heads, rows, HD), keys.dtype),
            pltpu.VMEM((heads, 2, rows, HD), keys.dtype),
            pltpu.VMEM((max(q_heads, 1), rows, HD), keys.dtype),
            pltpu.SemaphoreType.DMA((heads, 3)),
            pltpu.SemaphoreType.DMA((max(q_heads, 1), 2)),
            pltpu.SemaphoreType.DMA((max(sum(size for _, size, _, _ in cuts), 1),)),
        ],
        compiler_params=pltpu.CompilerParams(vmem_limit_bytes=limit),
        cost_estimate=pl.CostEstimate(flops=0, bytes_accessed=8 * rows * heads * HD, transcendentals=0),
    )(queries, keys, values)


def attend_kernel(cfg, tiles_ref, counts_ref, q_ref, *refs):
    low, size, shifts, (hops, rim, relay, parted), early, projects, has_acc, final = cfg
    refs = list(refs)
    piece_refs = [refs.pop(0) for _ in shifts]
    early_refs = [refs.pop(0) for _ in early or ()]
    w_ref = refs.pop(0) if projects else None
    acc_ref = refs.pop(0) if has_acc else None
    out_ref, kv_buf = refs[:2]
    rows = q_ref.shape[1]
    tiles = rows // TILE
    slots = tiles_ref.shape[1]
    spans = (2 * hops + 1) * rows
    spots = piece_spots(tiles, hops, rim, relay, parted)
    member, members = lax.axis_index("ulysses"), lax.axis_size("ulysses")
    first = (lax.axis_index("temporal") * members + member - hops) * tiles
    att_buf, lead = out_ref, 0
    if early is not None:
        att_buf = refs[2] if projects else out_ref
        for extent, ref in zip(early, early_refs):
            att_buf[:, lead * HD : (lead + extent) * HD] = ref[...]
            lead += extent

    scale = math.log2(math.e) / math.sqrt(HD)
    zeros = jnp.zeros((TILE, HD), jnp.bfloat16)
    places, v_places, ones = [], [], []
    for tile in range(tiles):
        row = member * tiles + tile
        live = counts_ref[row]
        at = [pl.multiple_of((tiles_ref[row, j] - first) * TILE, TILE) for j in range(slots)]
        places.append(at)
        v_places.append([pl.multiple_of(jnp.where(j < live, at[j], spans), TILE) for j in range(slots)])
        ones.append([zeros + jnp.where(j < live, 1.0, 0.0).astype(jnp.bfloat16) for j in range(slots)])

    def scores(h, tile):
        k = jnp.concatenate([kv_buf[h % 2, 0, pl.ds(p, TILE)] for p in places[tile]], axis=1)
        q = q_ref[h, tile * TILE : (tile + 1) * TILE]
        return jnp.dot(q, k, preferred_element_type=jnp.float32)

    def finish(h, tile, s):
        top = jnp.max(s, axis=1, keepdims=True)
        p = jnp.exp2((s - top) * scale).astype(jnp.bfloat16)
        v = jnp.concatenate(
            [
                jnp.concatenate([kv_buf[h % 2, 1, pl.ds(at, TILE)], one], axis=1)
                for at, one in zip(v_places[tile], ones[tile])
            ],
            axis=0,
        )
        mixed = jnp.dot(p, v, preferred_element_type=jnp.float32)
        here = slice(tile * TILE, (tile + 1) * TILE)
        att_buf[here, (lead + h) * HD : (lead + h + 1) * HD] = (mixed[:, :HD] / mixed[:, HD:]).astype(jnp.bfloat16)

    def ready(h):
        for i, ref in enumerate(piece_refs):
            place = pl.ds(pl.multiple_of(spots[i] * TILE, TILE), ref.shape[2])
            for part in range(2):
                kv_buf[h % 2, part, place] = ref[h + shifts[i], part]
        kv_buf[h % 2, 1, spans : spans + TILE] = zeros

    strips = []
    if final and lead:
        strips = list(range(0, w_ref.shape[1], STRIP))

    def lay_strip(at):
        here = slice(at, min(at + STRIP, w_ref.shape[1]))
        weights = w_ref[(low - lead) * HD : low * HD, here]
        part = jnp.dot(att_buf[:, : lead * HD], weights, preferred_element_type=jnp.float32)
        if has_acc:
            part = part + acc_ref[:, here]
        sum_buf[:, here] = part

    if final:
        sum_buf = refs[5]
    jobs = [(h, tile) for h in range(size) for tile in range(tiles)]
    share = -(-len(strips) // len(jobs))
    ready(0)
    ahead = scores(*jobs[0])
    for i, (h, tile) in enumerate(jobs):
        now = ahead
        if i + 1 < len(jobs):
            if jobs[i + 1][0] != h:
                ready(h + 1)
            ahead = scores(*jobs[i + 1])
        for at in strips[i * share : (i + 1) * share]:
            lay_strip(at)
        finish(h, tile, now)

    if not projects:
        return
    stores = []
    out_buf, out_sems = refs[3:5] if final else (out_ref, None)
    skip = lead if strips else 0
    for i, at in enumerate(range(0, out_buf.shape[1], STRIP)):
        here = slice(at, min(at + STRIP, out_buf.shape[1]))
        weights = w_ref[(low - lead + skip) * HD : (low + size) * HD, here]
        part = jnp.dot(att_buf[:, skip * HD :], weights, preferred_element_type=jnp.float32)
        if strips:
            part = part + sum_buf[:, here]
        elif has_acc:
            part = part + acc_ref[:, here]
        out_buf[:, here] = part.astype(out_buf.dtype)
        if final:
            cols = pl.ds(at, here.stop - at)
            stores.append(pltpu.make_async_copy(out_buf.at[:, cols], out_ref.at[:, cols], out_sems.at[i]))
            stores[-1].start()
    for copy in stores:
        copy.wait()


def attend(tile_list, counts, layout, queries, pieces, shifts, span, early, out_weight, acc, final):
    rows = queries.shape[1]
    low, size = span
    reach = (2 * layout[0] + 1) * rows
    projects = out_weight is not None
    bf16 = jnp.bfloat16
    operands = [tile_list, counts, queries, *pieces]
    scratch = [pltpu.VMEM((2, 2, reach + TILE, HD), bf16)]
    parts = None
    out_shape = jax.ShapeDtypeStruct((rows, size * HD), bf16)
    if early is not None:
        parts = tuple(part.shape[1] // HD for part in early)
        operands += early
        out_shape = jax.ShapeDtypeStruct((rows, (size + sum(parts)) * HD), bf16)
    if projects:
        width = out_weight.shape[1]
        operands.append(out_weight)
        if acc is not None:
            operands.append(acc)
        scratch.append(pltpu.VMEM(out_shape.shape, bf16))
        out_shape = jax.ShapeDtypeStruct((rows, width), bf16 if final else jnp.float32)
        if final:
            scratch += [pltpu.VMEM((rows, width), bf16), pltpu.SemaphoreType.DMA((-(-width // STRIP),))]
            scratch.append(pltpu.VMEM((rows, width), jnp.float32))
    return pl.pallas_call(
        functools.partial(
            attend_kernel, (low, size, shifts, layout, parts, projects, acc is not None, final)
        ),
        out_shape=out_shape,
        in_specs=[SMEM] * 2 + [VMEM] * (len(operands) - 2),
        out_specs=HBM if final else VMEM,
        scratch_shapes=scratch,
        compiler_params=pltpu.CompilerParams(vmem_limit_bytes=VMEM_LIMIT * (2 if final else 1)),
        cost_estimate=pl.CostEstimate(flops=0, bytes_accessed=0, transcendentals=0),
    )(*operands)


def after(array, *others):
    return lax.optimization_barrier((array, *others))[0]


def on_device(queries, keys, values, tile_list, counts, out_weight):
    rows, model = queries.shape
    tiles = rows // TILE
    groups, members = lax.axis_size("temporal"), lax.axis_size("ulysses")
    total = groups * members
    both = ("temporal", "ulysses")
    hops = -(-REACH // tiles)
    relay = members == 2 and hops == 1
    rim = min(REACH, tiles)

    spans, low = [], 0
    for size in split_heads(model // HD):
        spans.append((low, size))
        low += size
    count = len(spans)
    sent = pack(queries, keys, values, spans[:1], [], [], VMEM_WHOLE)
    split = max(1, count - 2) if relay and tiles > rim else count
    cuts = [(low, size, 0, rim) for low, size in spans[split:]]
    if cuts:
        rest_low = spans[split][0]
        cuts.append((rest_low, model // HD - rest_low, 1, tiles - rim))
    laid = pack(queries, after(keys, *sent), values, spans, spans, cuts, VMEM_LIMIT)
    blocks, heads_of, parts = laid[:count], laid[count : 2 * count], laid[2 * count :]
    sent = [*sent, *blocks[1:split], *parts]

    onward = [(2 * g, 2 * g + 2) for g in range(groups - 1)]
    onward += [(2 * g + 3, 2 * g + 1) for g in range(groups - 1)]
    near = []
    for i, block in enumerate(sent):
        if relay:
            with jax.named_scope(f"partner_{i}" if i < count else f"rest_{i}"):
                near.append([lax.ppermute(block, "ulysses", [(0, 1), (1, 0)])])
        else:
            near.append(
                [
                    lax.ppermute(block, both, [(j, j - o) for j in range(total) if 0 <= j - o < total])
                    for o in range(-hops, hops + 1)
                    if o
                ]
            )

    ends = [j for j in (count - 4,) if j >= 0] + [count - 1]
    results, acc, begin = [], None, 0
    for i in range(count + 1):
        if i < count:
            pieces = [blocks[i], *near[i]]
            shifts = [0] * len(pieces)
            if i >= split:
                pieces += near[count]
                shifts.append(spans[i][0] - rest_low)
            if relay:
                back = 3 if i == count - 1 else 2
                gate = near[i][0] if i < back else after(near[i][0], results[i - back])
                with jax.named_scope(f"onward_{i}"):
                    pieces.append(lax.ppermute(gate, both, onward))
                shifts.append(0)
        if i >= 1:
            j = i - 1
            final = i == count
            projects = j in ends
            early = results[begin:] if projects or j == count - 2 else None
            layout = (hops, rim, relay, j >= split)
            with jax.named_scope(f"attend_{j}"):
                result = attend(
                    tile_list, counts, layout, heads_of[j], *held, spans[j], early,
                    out_weight if projects else None, acc if projects else None, final,
                )
            results.append(result)
            if projects:
                acc, begin = result, i
            elif early is not None:
                begin = j
        held = pieces, tuple(shifts)
    return results[-1]


def solution(mesh):
    return jax.shard_map(
        on_device,
        mesh=mesh,
        in_specs=(
            P(("temporal", "ulysses"), None),
            P(("temporal", "ulysses"), None),
            P(("temporal", "ulysses"), None),
            P("temporal", None),
            P("temporal"),
            P(),
        ),
        out_specs=P(("temporal", "ulysses"), None),
        check_vma=False,
    )
```
